32 devices in a mesh: img: 8 (over y, x, core), txt: 4 (over z).
Axes of the slice: x: 2, y: 2, z: 4, core: 2. Of those that a mesh axis runs over, the one named last changes fastest.
Arguments:
- image_emb: float32 [1024, 768], P(('img', 'txt')), may hold values from -0.6 to 0.6
- text_emb: float32 [1024, 768], P(('txt', 'img')), may hold values from -0.6 to 0.6
- pairs: int32 [1024], P('img'), may hold values from 0 to 1023, each once
- log_scale: float32 [1], replicated, may hold values from 2 to 2.6
- bias: float32 [1], replicated, may hold values from -12 to -8
Outputs:
- image_loss: float32 [1024], P('img')
- image_grad: float32 [1024, 768], P(('img', 'txt'))
- text_grad: float32 [1024, 768], P(('txt', 'img'))
The draws below stay inside these ranges and needn't reach their ends.
Inputs may be any that keep to these rules, and one draw needn't show every extreme that they name: `pairs`: each text is matched to exactly one image.
All inputs are finite; a program needn't handle non-finite values.
Results may differ from the reference program's by a relative error of at most 0.0003.
Values sent between devices are 32-bit elements; how exact they have to be, the bound alone decides.
No kernel may reach another device: no remote copies, remote signals or barrier semaphores. Data moves between devices by JAX's collectives and lax.ppermute only.
A program may use at most 64 MiB of HBM per device.

```python
import jax
import jax.numpy as jnp
from jax import lax

E = 768
NI = 1024
NT = 1024
N_IMG = 8


def block_levels(key, shape, shards, low, high):
    level, own = 1.0, jax.random.fold_in(key, 6)
    for axis_at, blocks in shards:
        steps = jnp.exp(jax.random.uniform(jax.random.fold_in(own, axis_at), (blocks,), jnp.float32, low / len(shards), high / len(shards)))
        level = level * jnp.repeat(steps, shape[axis_at] // blocks).reshape([-1 if axis == axis_at else 1 for axis in range(len(shape))])
    return level


def noise(own_key, shape, scale, reach, cuts=(), kind=jnp.bfloat16):
    array = scale * jax.random.normal(own_key, shape, jnp.float32)
    if cuts:
        array = array * block_levels(own_key, shape, cuts, -0.22, 0.18)
    return jnp.clip(array, -reach, reach).astype(kind)


def setup_inputs(seed: int = 0) -> dict:
    key_of = jax.random.split(jax.random.key(seed), 6)
    image_emb = noise(key_of[0], (NI, E), 0.104, 0.6, ((0, 32),), jnp.float32)
    text_emb = noise(key_of[1], (NT, E), 0.104, 0.6, ((0, 32),), jnp.float32)
    pairs = jax.random.permutation(key_of[2], NT).astype(jnp.int32)
    log_scale = jnp.clip(jax.random.uniform(key_of[3], (1,), jnp.float32, 2.0, 2.6), 2.0, 2.6)
    bias = jnp.clip(jax.random.uniform(key_of[4], (1,), jnp.float32, -12.0, -8.0), -12.0, -8.0)
    return {"image_emb": image_emb, "text_emb": text_emb, "pairs": pairs, "log_scale": log_scale, "bias": bias}


def reference(image_emb, text_emb, pairs, log_scale, bias):
    scale = jnp.exp(log_scale[0])
    shift = bias[0]
    rows = image_emb.shape[0]
    nblk = max(N_IMG // 8, 1)
    block = rows // nblk
    width = image_emb.shape[1]
    img_blocks = image_emb.reshape(nblk, block, width)
    pair_blocks = pairs.reshape(nblk, block)
    columns = jnp.arange(text_emb.shape[0], dtype=jnp.int32)

    def step(total, item):
        images, matched = item
        dots = lax.dot_general(images, text_emb, (((1,), (1,)), ((), ())), precision=lax.Precision.HIGHEST, preferred_element_type=jnp.float32)
        logits = scale * dots + shift
        sign = jnp.where(matched[:, None] == columns[None, :], 1.0, -1.0).astype(logits.dtype)
        loss = jnp.sum(jax.nn.softplus(-sign * logits), axis=1)
        dlogits = -sign * jax.nn.sigmoid(-sign * logits)
        grad_img = scale * jnp.dot(dlogits, text_emb, precision=lax.Precision.HIGHEST, preferred_element_type=jnp.float32)
        grad_txt = lax.dot_general(dlogits, images, (((0,), (0,)), ((), ())), precision=lax.Precision.HIGHEST, preferred_element_type=jnp.float32)
        return total + scale * grad_txt, (loss, grad_img)

    text_grad, (losses, grads) = lax.scan(step, jnp.zeros_like(text_emb), (img_blocks, pair_blocks))
    return losses.reshape(rows), grads.reshape(rows, width), text_grad
```

```python
import jax
import jax.numpy as jnp
from jax import lax
from jax.sharding import PartitionSpec as P


def partner(n, me, k):
    if n & (n - 1) == 0:
        return me ^ k
    return (k - me) % n


def rounds(n):
    if n & (n - 1) == 0:
        return range(1, n)
    return range(n)


def swap(x, axis, n, k):
    return lax.ppermute(x, axis, [(i, partner(n, i, k)) for i in range(n)])


def per_device(sizes, image_emb, text_emb, pairs, log_scale, bias):
    n_img, n_txt = sizes
    me_img, me_txt = lax.axis_index("img"), lax.axis_index("txt")
    rows, cols = image_emb.shape[0], text_emb.shape[0]

    images = jnp.concatenate(
        [image_emb] + [swap(image_emb, "txt", n_txt, k) for k in range(1, n_txt)]
    )
    texts = jnp.concatenate(
        [text_emb] + [swap(text_emb, "img", n_img, k) for k in range(1, n_img)]
    )
    image_order = jnp.stack([partner(n_txt, me_txt, k) for k in range(n_txt)])
    text_order = jnp.stack([partner(n_img, me_img, k) for k in range(n_img)])
    scale = jnp.exp(log_scale[0])
    shift = bias[0]
    dots = lax.dot_general(
        images,
        texts,
        (((1,), (1,)), ((), ())),
        precision=lax.Precision.HIGHEST,
        preferred_element_type=jnp.float32,
    )
    logits = scale * dots + shift
    matched = pairs.reshape(n_txt, rows)[image_order].reshape(-1)
    columns = (
        (me_txt * n_img + text_order)[:, None] * cols + jnp.arange(cols, dtype=jnp.int32)
    ).reshape(-1)
    sign = jnp.where(matched[:, None] == columns[None, :], 1.0, -1.0).astype(jnp.float32)
    loss_part = jnp.sum(jax.nn.softplus(-sign * logits), axis=1)
    loss_part = loss_part.reshape(n_txt, rows)[image_order].reshape(-1)
    dlogits = -sign * jax.nn.sigmoid(-sign * logits)
    image_term = scale * jnp.dot(
        dlogits, texts, precision=lax.Precision.HIGHEST, preferred_element_type=jnp.float32
    )
    text_term = scale * lax.dot_general(
        dlogits,
        images,
        (((0,), (0,)), ((), ())),
        precision=lax.Precision.HIGHEST,
        preferred_element_type=jnp.float32,
    )
    loss_row = jnp.pad(loss_part, (0, image_emb.shape[1] - loss_part.shape[0]))[None]
    image_msgs = [
        jnp.concatenate([image_term[k * rows:(k + 1) * rows], loss_row]) for k in range(n_txt)
    ]
    image_sum = image_msgs[0] + sum(swap(image_msgs[k], "txt", n_txt, k) for k in range(1, n_txt))
    text_grad = text_term[:cols] + sum(
        swap(text_term[k * cols:(k + 1) * cols], "img", n_img, k) for k in range(1, n_img)
    )
    return (image_sum[rows, :loss_part.shape[0]], image_sum[:rows], text_grad)


def per_device_large(image_emb, text_emb, pairs, log_scale, bias):
    images = lax.all_gather(image_emb, "txt", axis=0, tiled=True)
    texts = lax.all_gather(text_emb, "img", axis=0, tiled=True)
    scale = jnp.exp(log_scale[0])
    shift = bias[0]
    text_count = texts.shape[0]
    dots = lax.dot_general(
        images,
        texts,
        (((1,), (1,)), ((), ())),
        precision=lax.Precision.HIGHEST,
        preferred_element_type=jnp.float32,
    )
    logits = scale * dots + shift
    columns = lax.axis_index("txt") * text_count + jnp.arange(text_count, dtype=jnp.int32)
    sign = jnp.where(pairs[:, None] == columns[None, :], 1.0, -1.0).astype(jnp.float32)
    loss_part = jnp.sum(jax.nn.softplus(-sign * logits), axis=1)
    image_loss = lax.psum(loss_part, "txt")
    dlogits = -sign * jax.nn.sigmoid(-sign * logits)
    image_term = scale * jnp.dot(
        dlogits, texts, precision=lax.Precision.HIGHEST, preferred_element_type=jnp.float32
    )
    image_grad = lax.psum_scatter(image_term, "txt", scatter_dimension=0, tiled=True)
    text_term = scale * lax.dot_general(
        dlogits,
        images,
        (((0,), (0,)), ((), ())),
        precision=lax.Precision.HIGHEST,
        preferred_element_type=jnp.float32,
    )
    text_grad = lax.psum_scatter(text_term, "img", scatter_dimension=0, tiled=True)
    return (image_loss, image_grad, text_grad)


def solution(mesh):
    sizes = (mesh.shape["img"], mesh.shape["txt"])
    if max(sizes) <= 8:
        body = lambda *arrays: per_device(sizes, *arrays)
    else:
        body = per_device_large
    return jax.shard_map(
        body,
        mesh=mesh,
        in_specs=(P(("img", "txt"), None), P(("txt", "img"), None), P("img"), P(), P()),
        out_specs=(P("img"), P(("img", "txt"), None), P(("txt", "img"), None)),
        check_vma=False,
    )
```

```python
import jax
import jax.numpy as jnp
from jax import lax
from jax.sharding import PartitionSpec as P


def spread(x, axis, n):
    return lax.all_to_all(jnp.broadcast_to(x[None], (n,) + x.shape), axis, 0, 0)


def per_device(sizes, image_emb, text_emb, pairs, log_scale, bias):
    n_img, n_txt = sizes
    me_txt = lax.axis_index("txt")
    rows, cols = image_emb.shape[0], text_emb.shape[0]

    width = image_emb.shape[1]
    images = spread(image_emb, "txt", n_txt).reshape(-1, width)
    texts = spread(text_emb, "img", n_img).reshape(-1, width)
    scale = jnp.exp(log_scale[0])
    shift = bias[0]
    dots = lax.dot_general(
        images,
        texts,
        (((1,), (1,)), ((), ())),
        precision=lax.Precision.HIGHEST,
        preferred_element_type=jnp.float32,
    )
    logits = scale * dots + shift
    columns = me_txt * texts.shape[0] + jnp.arange(texts.shape[0], dtype=jnp.int32)
    sign = jnp.where(pairs[:, None] == columns[None, :], 1.0, -1.0).astype(jnp.float32)
    loss_part = jnp.sum(jax.nn.softplus(-sign * logits), axis=1)
    dlogits = -sign * jax.nn.sigmoid(-sign * logits)
    image_term = scale * jnp.dot(
        dlogits, texts, precision=lax.Precision.HIGHEST, preferred_element_type=jnp.float32
    )
    text_term = scale * lax.dot_general(
        dlogits,
        images,
        (((0,), (0,)), ((), ())),
        precision=lax.Precision.HIGHEST,
        preferred_element_type=jnp.float32,
    )
    text_grad = jnp.sum(
        lax.all_to_all(text_term.reshape(n_img, cols, width), "img", 0, 0), axis=0
    )
    loss_row = jnp.pad(loss_part, (0, width - loss_part.shape[0]))
    image_msgs = jnp.concatenate(
        [image_term.reshape(n_txt, rows, width), jnp.broadcast_to(loss_row, (n_txt, 1, width))],
        axis=1,
    )
    image_sum = jnp.sum(lax.all_to_all(image_msgs, "txt", 0, 0), axis=0)
    return (image_sum[rows, :loss_part.shape[0]], image_sum[:rows], text_grad)


def per_device_large(image_emb, text_emb, pairs, log_scale, bias):
    images = lax.all_gather(image_emb, "txt", axis=0, tiled=True)
    texts = lax.all_gather(text_emb, "img", axis=0, tiled=True)
    scale = jnp.exp(log_scale[0])
    shift = bias[0]
    text_count = texts.shape[0]
    dots = lax.dot_general(
        images,
        texts,
        (((1,), (1,)), ((), ())),
        precision=lax.Precision.HIGHEST,
        preferred_element_type=jnp.float32,
    )
    logits = scale * dots + shift
    columns = lax.axis_index("txt") * text_count + jnp.arange(text_count, dtype=jnp.int32)
    sign = jnp.where(pairs[:, None] == columns[None, :], 1.0, -1.0).astype(jnp.float32)
    loss_part = jnp.sum(jax.nn.softplus(-sign * logits), axis=1)
    image_loss = lax.psum(loss_part, "txt")
    dlogits = -sign * jax.nn.sigmoid(-sign * logits)
    image_term = scale * jnp.dot(
        dlogits, texts, precision=lax.Precision.HIGHEST, preferred_element_type=jnp.float32
    )
    image_grad = lax.psum_scatter(image_term, "txt", scatter_dimension=0, tiled=True)
    text_term = scale * lax.dot_general(
        dlogits,
        images,
        (((0,), (0,)), ((), ())),
        precision=lax.Precision.HIGHEST,
        preferred_element_type=jnp.float32,
    )
    text_grad = lax.psum_scatter(text_term, "img", scatter_dimension=0, tiled=True)
    return (image_loss, image_grad, text_grad)


def solution(mesh):
    sizes = (mesh.shape["img"], mesh.shape["txt"])
    if max(sizes) <= 8:
        body = lambda *arrays: per_device(sizes, *arrays)
    else:
        body = per_device_large
    return jax.shard_map(
        body,
        mesh=mesh,
        in_specs=(P(("img", "txt"), None), P(("txt", "img"), None), P("img"), P(), P()),
        out_specs=(P("img"), P(("img", "txt"), None), P(("txt", "img"), None)),
        check_vma=False,
    )
```

```python
import jax
import jax.numpy as jnp
from jax import lax
from jax.sharding import PartitionSpec as P


def exchange(x, axis, n, k):
    return lax.ppermute(x, axis, [(i, i ^ k) for i in range(n)])


def untwist(blocks, me):
    n = blocks.shape[0]
    bit = 1
    while bit < n:
        paired = blocks.reshape((n // (2 * bit), 2, bit) + blocks.shape[1:])
        flipped = paired[:, ::-1]
        blocks = jnp.where(me & bit, flipped, paired).reshape(blocks.shape)
        bit *= 2
    return blocks


def dot(a, b, contract):
    return lax.dot_general(
        a,
        b,
        ((contract[:1], contract[1:]), ((), ())),
        precision=lax.Precision.HIGH,
        preferred_element_type=jnp.float32,
    )


def losses(images, texts, matched, columns, scale, shift):
    logits = scale * dot(images, texts, (1, 1)) + shift
    match = matched[:, None] == columns[None, :]
    v = jnp.where(match, -logits, logits)
    e = jnp.exp(-jnp.abs(v))
    loss = jnp.maximum(v, 0.0) + jnp.log1p(e)
    s = scale * jnp.where(v >= 0, 1.0, e) / (1.0 + e)
    return jnp.sum(loss, axis=1), jnp.where(match, -s, s)


def per_device(sizes, image_emb, text_emb, pairs, log_scale, bias):
    n_img, n_txt = sizes
    chips = n_img // 2
    me_img, me_txt = lax.axis_index("img"), lax.axis_index("txt")
    rows, cols, width = image_emb.shape[0], text_emb.shape[0], image_emb.shape[1]
    scale = jnp.exp(log_scale[0])
    shift = bias[0]

    image_blocks, text_blocks = [image_emb], [text_emb]
    for k in range(1, max(n_txt, chips)):
        if k < n_txt:
            image_blocks.append(exchange(image_emb, "txt", n_txt, k))
        if k < chips:
            text_blocks.append(exchange(text_emb, "img", n_img, 2 * k))
    near = jnp.concatenate(text_blocks)
    far = exchange(near, "img", n_img, 1)
    images = jnp.concatenate(image_blocks)

    matched = untwist(pairs.reshape(n_txt, rows), me_txt).reshape(-1)
    place = jnp.arange(chips * cols, dtype=jnp.int32)
    chip = (me_img // 2) ^ (place // cols)
    column = (me_txt * n_img + 2 * chip) * cols + place % cols
    core = me_img % 2
    loss_near, d_near = losses(images, near, matched, column + core * cols, scale, shift)
    loss_far, d_far = losses(images, far, matched, column + (1 - core) * cols, scale, shift)

    text_far = dot(d_far, images, (0, 0))
    text_back = exchange(text_far, "img", n_img, 1)
    image_term = dot(d_near, near, (1, 0)) + dot(d_far, far, (1, 0))
    loss_part = (loss_near + loss_far).reshape(n_txt, rows)
    image_back, loss_sum = [image_term[:rows]], loss_part
    for k in range(1, n_txt):
        loss_row = jnp.stack([loss_part[k ^ m] for m in range(n_txt)]).reshape(1, -1)
        loss_row = jnp.pad(loss_row, ((0, 7), (0, width - loss_row.shape[1])))
        sent = jnp.concatenate([image_term[k * rows:(k + 1) * rows], loss_row])
        got = exchange(sent, "txt", n_txt, k)
        image_back.append(got[:rows])
        loss_sum = loss_sum + got[rows, :n_txt * rows].reshape(n_txt, rows)
    text_term = dot(d_near, images, (0, 0)) + text_back
    text_grad = text_term[:cols]
    for k in range(1, chips):
        text_grad = text_grad + exchange(text_term[k * cols:(k + 1) * cols], "img", n_img, 2 * k)
    image_grad = sum(image_back)
    image_loss = untwist(loss_sum, me_txt).reshape(-1)
    return (image_loss, image_grad, text_grad)


def per_device_large(image_emb, text_emb, pairs, log_scale, bias):
    images = lax.all_gather(image_emb, "txt", axis=0, tiled=True)
    texts = lax.all_gather(text_emb, "img", axis=0, tiled=True)
    scale = jnp.exp(log_scale[0])
    shift = bias[0]
    text_count = texts.shape[0]
    dots = lax.dot_general(
        images,
        texts,
        (((1,), (1,)), ((), ())),
        precision=lax.Precision.HIGHEST,
        preferred_element_type=jnp.float32,
    )
    logits = scale * dots + shift
    columns = lax.axis_index("txt") * text_count + jnp.arange(text_count, dtype=jnp.int32)
    sign = jnp.where(pairs[:, None] == columns[None, :], 1.0, -1.0).astype(jnp.float32)
    loss_part = jnp.sum(jax.nn.softplus(-sign * logits), axis=1)
    image_loss = lax.psum(loss_part, "txt")
    dlogits = -sign * jax.nn.sigmoid(-sign * logits)
    image_term = scale * jnp.dot(
        dlogits, texts, precision=lax.Precision.HIGHEST, preferred_element_type=jnp.float32
    )
    image_grad = lax.psum_scatter(image_term, "txt", scatter_dimension=0, tiled=True)
    text_term = scale * lax.dot_general(
        dlogits,
        images,
        (((0,), (0,)), ((), ())),
        precision=lax.Precision.HIGHEST,
        preferred_element_type=jnp.float32,
    )
    text_grad = lax.psum_scatter(text_term, "img", scatter_dimension=0, tiled=True)
    return (image_loss, image_grad, text_grad)


def solution(mesh):
    sizes = (mesh.shape["img"], mesh.shape["txt"])
    if all(n in (2, 4, 8) for n in sizes):
        body = lambda *arrays: per_device(sizes, *arrays)
    else:
        body = per_device_large
    return jax.shard_map(
        body,
        mesh=mesh,
        in_specs=(P(("img", "txt"), None), P(("txt", "img"), None), P("img"), P(), P()),
        out_specs=(P("img"), P(("img", "txt"), None), P(("txt", "img"), None)),
        check_vma=False,
    )
```

```python
import jax
import jax.numpy as jnp
from jax import lax
from jax.sharding import PartitionSpec as P


def exchange(x, axis, n, k):
    return lax.ppermute(x, axis, [(i, i ^ k) for i in range(n)])


def untwist(blocks, me):
    n = blocks.shape[0]
    bit = 1
    while bit < n:
        paired = blocks.reshape((n // (2 * bit), 2, bit) + blocks.shape[1:])
        flipped = paired[:, ::-1]
        blocks = jnp.where(me & bit, flipped, paired).reshape(blocks.shape)
        bit *= 2
    return blocks


def dot(a, b, contract):
    return lax.dot_general(
        a,
        b,
        ((contract[:1], contract[1:]), ((), ())),
        precision=lax.Precision.HIGH,
        preferred_element_type=jnp.float32,
    )


def after(x, *others):
    return lax.optimization_barrier((x,) + others)[0]


def quadrant(images, texts, matched, columns, scale, shift):
    logits = scale * dot(images, texts, (1, 1)) + shift
    match = matched[:, None] == columns[None, :]
    v = jnp.where(match, -logits, logits)
    e = jnp.exp(-jnp.abs(v))
    loss = jnp.maximum(v, 0.0) + jnp.log1p(e)
    s = scale * jnp.where(v >= 0, 1.0, e) / (1.0 + e)
    return jnp.sum(loss, axis=1), jnp.where(match, -s, s)


def per_device(sizes, image_emb, text_emb, pairs, log_scale, bias):
    n_img, n_txt = sizes
    chips = n_img // 2
    me_img, me_txt = lax.axis_index("img"), lax.axis_index("txt")
    rows, cols, width = image_emb.shape[0], text_emb.shape[0], image_emb.shape[1]
    scale = jnp.exp(log_scale[0])
    shift = bias[0]

    matched = untwist(pairs.reshape(n_txt, rows), me_txt).reshape(-1)
    text_blocks = {0: text_emb}
    image_blocks = {0: image_emb}
    for k in range(1, max(n_txt, chips)):
        if k < chips:
            text_blocks[k] = exchange(text_emb, "img", n_img, 2 * k)
        if 1 < k < n_txt:
            image_blocks[k] = exchange(image_emb, "txt", n_txt, k)
    image_blocks[1] = exchange(after(image_emb, text_blocks[1]), "txt", n_txt, 1)
    near = jnp.concatenate([text_blocks[k] for k in range(chips)])
    far = exchange(near, "img", n_img, 1)
    images = jnp.concatenate([image_blocks[k] for k in range(n_txt)])
    count = n_txt * rows
    pair_row = jnp.pad(matched.astype(jnp.float32)[None], ((0, 7), (0, width - count)))
    pair = exchange(jnp.concatenate([images, pair_row]), "img", n_img, 1)
    pair_images, matched_pair = pair[:count], pair[count, :count].astype(jnp.int32)

    place = jnp.arange(chips * cols, dtype=jnp.int32)
    chip = (me_img // 2) ^ (place // cols)
    core = me_img % 2
    column = (me_txt * n_img + 2 * chip + core) * cols + place % cols
    far_column = column + (1 - 2 * core) * cols
    loss_near, d_near = quadrant(images, near, matched, column, scale, shift)
    loss_far, d_far = quadrant(images, far, matched, far_column, scale, shift)

    image_term = dot(d_near, near, (1, 0)) + dot(d_far, far, (1, 0))
    loss_part = (loss_near + loss_far).reshape(n_txt, rows)
    image_back, loss_sum = [image_term[:rows]], loss_part
    for k in range(1, n_txt):
        loss_row = jnp.stack([loss_part[k ^ m] for m in range(n_txt)]).reshape(1, -1)
        loss_row = jnp.pad(loss_row, ((0, 7), (0, width - loss_row.shape[1])))
        sent = jnp.concatenate([image_term[k * rows:(k + 1) * rows], loss_row])
        got = exchange(sent, "txt", n_txt, k)
        image_back.append(got[:rows])
        loss_sum = loss_sum + got[rows, :count].reshape(n_txt, rows)

    _, d_pair = quadrant(pair_images, near, matched_pair, column, scale, shift)
    text_term = dot(d_near, images, (0, 0)) + dot(d_pair, pair_images, (0, 0))
    text_grad = text_term[:cols]
    for k in range(1, chips):
        text_grad = text_grad + exchange(text_term[k * cols:(k + 1) * cols], "img", n_img, 2 * k)
    image_grad = sum(image_back)
    image_loss = untwist(loss_sum, me_txt).reshape(-1)
    return (image_loss, image_grad, text_grad)


def per_device_large(image_emb, text_emb, pairs, log_scale, bias):
    images = lax.all_gather(image_emb, "txt", axis=0, tiled=True)
    texts = lax.all_gather(text_emb, "img", axis=0, tiled=True)
    scale = jnp.exp(log_scale[0])
    shift = bias[0]
    text_count = texts.shape[0]
    dots = lax.dot_general(
        images,
        texts,
        (((1,), (1,)), ((), ())),
        precision=lax.Precision.HIGHEST,
        preferred_element_type=jnp.float32,
    )
    logits = scale * dots + shift
    columns = lax.axis_index("txt") * text_count + jnp.arange(text_count, dtype=jnp.int32)
    sign = jnp.where(pairs[:, None] == columns[None, :], 1.0, -1.0).astype(jnp.float32)
    loss_part = jnp.sum(jax.nn.softplus(-sign * logits), axis=1)
    image_loss = lax.psum(loss_part, "txt")
    dlogits = -sign * jax.nn.sigmoid(-sign * logits)
    image_term = scale * jnp.dot(
        dlogits, texts, precision=lax.Precision.HIGHEST, preferred_element_type=jnp.float32
    )
    image_grad = lax.psum_scatter(image_term, "txt", scatter_dimension=0, tiled=True)
    text_term = scale * lax.dot_general(
        dlogits,
        images,
        (((0,), (0,)), ((), ())),
        precision=lax.Precision.HIGHEST,
        preferred_element_type=jnp.float32,
    )
    text_grad = lax.psum_scatter(text_term, "img", scatter_dimension=0, tiled=True)
    return (image_loss, image_grad, text_grad)


def solution(mesh):
    sizes = (mesh.shape["img"], mesh.shape["txt"])
    if all(n in (2, 4, 8) for n in sizes):
        body = lambda *arrays: per_device(sizes, *arrays)
    else:
        body = per_device_large
    return jax.shard_map(
        body,
        mesh=mesh,
        in_specs=(P(("img", "txt"), None), P(("txt", "img"), None), P("img"), P(), P()),
        out_specs=(P("img"), P(("img", "txt"), None), P(("txt", "img"), None)),
        check_vma=False,
    )
```

```python
import jax
import jax.numpy as jnp
from jax import lax
from jax.sharding import PartitionSpec as P


def exchange(x, axis, n, k):
    return lax.ppermute(x, axis, [(i, i ^ k) for i in range(n)])


def untwist(blocks, me):
    n = blocks.shape[0]
    bit = 1
    while bit < n:
        paired = blocks.reshape((n // (2 * bit), 2, bit) + blocks.shape[1:])
        flipped = paired[:, ::-1]
        blocks = jnp.where(me & bit, flipped, paired).reshape(blocks.shape)
        bit *= 2
    return blocks


def dot(a, b, contract):
    return lax.dot_general(
        a,
        b,
        ((contract[:1], contract[1:]), ((), ())),
        precision=lax.Precision.HIGH,
        preferred_element_type=jnp.float32,
    )


def quadrant(images, texts, matched, columns, scale, shift):
    logits = scale * dot(images, texts, (1, 1)) + shift
    match = matched[:, None] == columns[None, :]
    v = jnp.where(match, -logits, logits)
    e = jnp.exp(-jnp.abs(v))
    loss = jnp.maximum(v, 0.0) + jnp.log1p(e)
    s = scale * jnp.where(v >= 0, 1.0, e) / (1.0 + e)
    return jnp.sum(loss, axis=1), jnp.where(match, -s, s)


def per_device(sizes, image_emb, text_emb, pairs, log_scale, bias):
    n_img, n_txt = sizes
    chips = n_img // 2
    me_img, me_txt = lax.axis_index("img"), lax.axis_index("txt")
    rows, cols, width = image_emb.shape[0], text_emb.shape[0], image_emb.shape[1]
    scale = jnp.exp(log_scale[0])
    shift = bias[0]

    matched = untwist(pairs.reshape(n_txt, rows), me_txt).reshape(-1)
    near = text_emb
    image_blocks = {0: image_emb}
    order = [k for k in range(2, n_txt)] + [1]
    step = 1
    while step < chips:
        near = jnp.concatenate([near, exchange(near, "img", n_img, 2 * step)])
        for k in order[:2]:
            image_blocks[k] = exchange(image_emb, "txt", n_txt, k)
        order = order[2:]
        step *= 2
    for k in order:
        image_blocks[k] = exchange(image_emb, "txt", n_txt, k)
    far = exchange(near, "img", n_img, 1)
    images = jnp.concatenate([image_blocks[k] for k in range(n_txt)])
    count = n_txt * rows
    pair_row = jnp.pad(matched.astype(jnp.float32)[None], ((0, 7), (0, width - count)))
    pair = exchange(jnp.concatenate([images, pair_row]), "img", n_img, 1)
    pair_images, matched_pair = pair[:count], pair[count, :count].astype(jnp.int32)

    place = jnp.arange(chips * cols, dtype=jnp.int32)
    chip = (me_img // 2) ^ (place // cols)
    core = me_img % 2
    column = (me_txt * n_img + 2 * chip + core) * cols + place % cols
    far_column = column + (1 - 2 * core) * cols
    loss_near, d_near = quadrant(images, near, matched, column, scale, shift)
    loss_far, d_far = quadrant(images, far, matched, far_column, scale, shift)

    image_term = dot(d_near, near, (1, 0)) + dot(d_far, far, (1, 0))
    loss_part = (loss_near + loss_far).reshape(n_txt, rows)
    image_grad, loss_sum = image_term[:rows], loss_part
    for k in range(1, n_txt):
        loss_tile = jnp.stack([loss_part[k ^ m] for m in range(n_txt)]).reshape(-1, 128)
        loss_tile = jnp.pad(loss_tile, ((0, -loss_tile.shape[0] % 8), (0, 0))).reshape(-1, 8, 128)
        term_tiles = image_term[k * rows:(k + 1) * rows].reshape(rows // 8, 8, width // 128, 128)
        term_tiles = jnp.swapaxes(term_tiles, 1, 2).reshape(-1, 8, 128)
        got = exchange(jnp.concatenate([term_tiles, loss_tile]), "txt", n_txt, k)
        got_tiles = got[:term_tiles.shape[0]].reshape(rows // 8, width // 128, 8, 128)
        image_grad = image_grad + jnp.swapaxes(got_tiles, 1, 2).reshape(rows, width)
        loss_sum = loss_sum + got[term_tiles.shape[0]:].reshape(-1)[:count].reshape(n_txt, rows)

    _, d_pair = quadrant(pair_images, near, matched_pair, column, scale, shift)
    text_term = dot(d_near, images, (0, 0)) + dot(d_pair, pair_images, (0, 0))
    text_grad = text_term[:cols]
    for k in range(1, chips):
        text_grad = text_grad + exchange(text_term[k * cols:(k + 1) * cols], "img", n_img, 2 * k)
    image_loss = untwist(loss_sum, me_txt).reshape(-1)
    return (image_loss, image_grad, text_grad)


def per_device_large(image_emb, text_emb, pairs, log_scale, bias):
    images = lax.all_gather(image_emb, "txt", axis=0, tiled=True)
    texts = lax.all_gather(text_emb, "img", axis=0, tiled=True)
    scale = jnp.exp(log_scale[0])
    shift = bias[0]
    text_count = texts.shape[0]
    dots = lax.dot_general(
        images,
        texts,
        (((1,), (1,)), ((), ())),
        precision=lax.Precision.HIGHEST,
        preferred_element_type=jnp.float32,
    )
    logits = scale * dots + shift
    columns = lax.axis_index("txt") * text_count + jnp.arange(text_count, dtype=jnp.int32)
    sign = jnp.where(pairs[:, None] == columns[None, :], 1.0, -1.0).astype(jnp.float32)
    loss_part = jnp.sum(jax.nn.softplus(-sign * logits), axis=1)
    image_loss = lax.psum(loss_part, "txt")
    dlogits = -sign * jax.nn.sigmoid(-sign * logits)
    image_term = scale * jnp.dot(
        dlogits, texts, precision=lax.Precision.HIGHEST, preferred_element_type=jnp.float32
    )
    image_grad = lax.psum_scatter(image_term, "txt", scatter_dimension=0, tiled=True)
    text_term = scale * lax.dot_general(
        dlogits,
        images,
        (((0,), (0,)), ((), ())),
        precision=lax.Precision.HIGHEST,
        preferred_element_type=jnp.float32,
    )
    text_grad = lax.psum_scatter(text_term, "img", scatter_dimension=0, tiled=True)
    return (image_loss, image_grad, text_grad)


def solution(mesh):
    sizes = (mesh.shape["img"], mesh.shape["txt"])
    if all(n in (2, 4, 8) for n in sizes):
        body = lambda *arrays: per_device(sizes, *arrays)
    else:
        body = per_device_large
    return jax.shard_map(
        body,
        mesh=mesh,
        in_specs=(P(("img", "txt"), None), P(("txt", "img"), None), P("img"), P(), P()),
        out_specs=(P("img"), P(("img", "txt"), None), P(("txt", "img"), None)),
        check_vma=False,
    )
```

```python
import jax
import jax.numpy as jnp
from jax import lax
from jax.sharding import PartitionSpec as P


def exchange(x, axis, n, k):
    return lax.ppermute(x, axis, [(i, i ^ k) for i in range(n)])


def untwist(blocks, me):
    n = blocks.shape[0]
    bit = 1
    while bit < n:
        paired = blocks.reshape((n // (2 * bit), 2, bit) + blocks.shape[1:])
        flipped = paired[:, ::-1]
        blocks = jnp.where(me & bit, flipped, paired).reshape(blocks.shape)
        bit *= 2
    return blocks


def dot(a, b, contract):
    return lax.dot_general(
        a,
        b,
        ((contract[:1], contract[1:]), ((), ())),
        precision=lax.Precision.HIGH,
        preferred_element_type=jnp.float32,
    )


def quadrant(images, texts, matched, columns, scale, shift):
    logits = scale * dot(images, texts, (1, 1)) + shift
    match = matched[:, None] == columns[None, :]
    v = jnp.where(match, -logits, logits)
    e = jnp.exp(-jnp.abs(v))
    loss = jnp.maximum(v, 0.0) + jnp.log1p(e)
    s = scale * jnp.where(v >= 0, 1.0, e) / (1.0 + e)
    return jnp.sum(loss, axis=1), jnp.where(match, -s, s)


def per_device(sizes, image_emb, text_emb, pairs, log_scale, bias):
    n_img, n_txt = sizes
    chips = n_img // 2
    me_img, me_txt = lax.axis_index("img"), lax.axis_index("txt")
    rows, cols, width = image_emb.shape[0], text_emb.shape[0], image_emb.shape[1]
    scale = jnp.exp(log_scale[0])
    shift = bias[0]

    matched = untwist(pairs.reshape(n_txt, rows), me_txt).reshape(-1)
    near = text_emb
    image_blocks = {0: image_emb}
    order = [k for k in range(2, n_txt)] + [1]
    step = 1
    while step < chips:
        near = jnp.concatenate([near, exchange(near, "img", n_img, 2 * step)])
        for k in order[:2]:
            image_blocks[k] = exchange(image_emb, "txt", n_txt, k)
        order = order[2:]
        step *= 2
    for k in order:
        image_blocks[k] = exchange(image_emb, "txt", n_txt, k)
    far = exchange(near, "img", n_img, 1)
    images = jnp.concatenate([image_blocks[k] for k in range(n_txt)])
    count = n_txt * rows
    pair_row = jnp.pad(matched.astype(jnp.float32)[None], ((0, 7), (0, width - count)))
    pair = exchange(jnp.concatenate([images, pair_row]), "img", n_img, 1)
    pair_images, matched_pair = pair[:count], pair[count, :count].astype(jnp.int32)

    place = jnp.arange(chips * cols, dtype=jnp.int32)
    chip = (me_img // 2) ^ (place // cols)
    core = me_img % 2
    column = (me_txt * n_img + 2 * chip + core) * cols + place % cols
    far_column = column + (1 - 2 * core) * cols
    loss_near, d_near = quadrant(images, near, matched, column, scale, shift)
    loss_far, d_far = quadrant(images, far, matched, far_column, scale, shift)

    image_term = dot(d_near, near, (1, 0)) + dot(d_far, far, (1, 0))
    loss_part = (loss_near + loss_far).reshape(n_txt, rows)
    messages = {}
    for k in range(1, n_txt):
        loss_tile = jnp.stack([loss_part[k ^ m] for m in range(n_txt)]).reshape(-1, 128)
        loss_tile = jnp.pad(loss_tile, ((0, -loss_tile.shape[0] % 8), (0, 0))).reshape(-1, 8, 128)
        term_tiles = image_term[k * rows:(k + 1) * rows].reshape(rows // 8, 8, width // 128, 128)
        term_tiles = jnp.swapaxes(term_tiles, 1, 2).reshape(-1, 8, 128)
        messages[k] = jnp.concatenate([term_tiles, loss_tile])
    pair_images, messages = lax.optimization_barrier((pair_images, messages))
    image_grad, loss_sum = image_term[:rows], loss_part
    for k in range(1, n_txt):
        got = exchange(messages[k], "txt", n_txt, k)
        got_tiles = got[:term_tiles.shape[0]].reshape(rows // 8, width // 128, 8, 128)
        image_grad = image_grad + jnp.swapaxes(got_tiles, 1, 2).reshape(rows, width)
        loss_sum = loss_sum + got[term_tiles.shape[0]:].reshape(-1)[:count].reshape(n_txt, rows)

    _, d_pair = quadrant(pair_images, near, matched_pair, column, scale, shift)
    text_term = dot(d_near, images, (0, 0)) + dot(d_pair, pair_images, (0, 0))
    text_grad = text_term[:cols]
    for k in range(1, chips):
        text_grad = text_grad + exchange(text_term[k * cols:(k + 1) * cols], "img", n_img, 2 * k)
    image_loss = untwist(loss_sum, me_txt).reshape(-1)
    return (image_loss, image_grad, text_grad)


def per_device_large(image_emb, text_emb, pairs, log_scale, bias):
    images = lax.all_gather(image_emb, "txt", axis=0, tiled=True)
    texts = lax.all_gather(text_emb, "img", axis=0, tiled=True)
    scale = jnp.exp(log_scale[0])
    shift = bias[0]
    text_count = texts.shape[0]
    dots = lax.dot_general(
        images,
        texts,
        (((1,), (1,)), ((), ())),
        precision=lax.Precision.HIGHEST,
        preferred_element_type=jnp.float32,
    )
    logits = scale * dots + shift
    columns = lax.axis_index("txt") * text_count + jnp.arange(text_count, dtype=jnp.int32)
    sign = jnp.where(pairs[:, None] == columns[None, :], 1.0, -1.0).astype(jnp.float32)
    loss_part = jnp.sum(jax.nn.softplus(-sign * logits), axis=1)
    image_loss = lax.psum(loss_part, "txt")
    dlogits = -sign * jax.nn.sigmoid(-sign * logits)
    image_term = scale * jnp.dot(
        dlogits, texts, precision=lax.Precision.HIGHEST, preferred_element_type=jnp.float32
    )
    image_grad = lax.psum_scatter(image_term, "txt", scatter_dimension=0, tiled=True)
    text_term = scale * lax.dot_general(
        dlogits,
        images,
        (((0,), (0,)), ((), ())),
        precision=lax.Precision.HIGHEST,
        preferred_element_type=jnp.float32,
    )
    text_grad = lax.psum_scatter(text_term, "img", scatter_dimension=0, tiled=True)
    return (image_loss, image_grad, text_grad)


def solution(mesh):
    sizes = (mesh.shape["img"], mesh.shape["txt"])
    if all(n in (2, 4, 8) for n in sizes):
        body = lambda *arrays: per_device(sizes, *arrays)
    else:
        body = per_device_large
    return jax.shard_map(
        body,
        mesh=mesh,
        in_specs=(P(("img", "txt"), None), P(("txt", "img"), None), P("img"), P(), P()),
        out_specs=(P("img"), P(("img", "txt"), None), P(("txt", "img"), None)),
        check_vma=False,
    )
```

```python
import functools

import jax
import jax.numpy as jnp
from jax import lax
from jax.experimental import pallas as pl
from jax.experimental.pallas import tpu as pltpu
from jax.sharding import PartitionSpec as P

LANES = 128


def exchange(x, axis, n, k):
    return lax.ppermute(x, axis, [(i, i ^ k) for i in range(n)])


def halves(x):
    high = x.astype(jnp.bfloat16)
    return high, (x - high.astype(jnp.float32)).astype(jnp.bfloat16)


def dot(a, b, contract):
    def part(x, y):
        dims = ((contract[:1], contract[1:]), ((), ()))
        return lax.dot_general(x, y, dims, preferred_element_type=jnp.float32)

    return part(a[0], b[0]) + (part(a[0], b[1]) + part(a[1], b[0]))


def untwist(row, block, me):
    lane = lax.broadcasted_iota(jnp.int32, row.shape, 1)
    step = block
    while step < LANES:
        up, down = pltpu.roll(row, LANES - step, 1), pltpu.roll(row, step, 1)
        flipped = jnp.where((lane // step) % 2 == 0, up, down)
        row = jnp.where((me // (step // block)) % 2 == 1, flipped, row)
        step *= 2
    return row


def text_ids(shape, n_img, cols, far):
    me_img, me_txt = lax.axis_index("img"), lax.axis_index("txt")
    place = lax.broadcasted_iota(jnp.int32, shape, 0)
    half = n_img // 2 * cols
    core = me_img % 2
    if far:
        core = core ^ (place // half)
        place = place % half
    chip = (me_img // 2) ^ (place // cols)
    return (me_txt * n_img + 2 * chip + core) * cols + place % cols


def derivative(texts, images, ids, matched, scale, shift):
    logits = scale * dot(texts, images, (1, 1)) + shift
    match = ids == matched
    v = jnp.where(match, -logits, logits)
    e = jnp.exp(-jnp.abs(v))
    loss = jnp.maximum(v, 0.0) + jnp.log1p(e)
    s = scale * jnp.where(v >= 0, 1.0, e) / (1.0 + e)
    return loss, jnp.where(match, -s, s)


def image_kernel(n_img, n_txt, rows, cols, *refs):
    log_scale, bias, bundle, near, far, own_ref, loss_ref, d_ref = refs[:8]
    message_refs = refs[8:]
    count = n_txt * rows
    me_txt = lax.axis_index("txt")
    scale = jnp.exp(jnp.full((1, LANES), log_scale[0], jnp.float32))
    images = halves(bundle[:count])
    texts = halves(jnp.concatenate([near[...], far[...]]))
    matched = untwist(bundle[count:count + 1, :LANES], rows, me_txt).astype(jnp.int32)
    ids = text_ids((texts[0].shape[0], count), n_img, cols, True)
    loss, d = derivative(texts, images, ids, matched, scale, bias[0])
    d_ref[...] = d[:near.shape[0]]
    term = dot(halves(d), texts, (0, 0))
    own_ref[...] = term[:rows]
    loss_row = untwist(jnp.sum(loss, axis=0, keepdims=True), rows, me_txt)
    loss_tile = jnp.broadcast_to(loss_row, (8, LANES))
    loss_ref[...] = loss_tile
    across = term.shape[1] // LANES
    for k, ref in enumerate(message_refs, 1):
        for r in range(rows // 8):
            for c in range(across):
                ref[r * across + c] = term[
                    k * rows + r * 8:k * rows + r * 8 + 8, c * LANES:(c + 1) * LANES
                ]
        ref[rows // 8 * across] = loss_tile


def text_kernel(n_img, n_txt, rows, cols, *refs):
    log_scale, bias, bundle, pair, near, d_ref = refs[:6]
    block_refs = refs[6:]
    count = n_txt * rows
    scale = jnp.exp(jnp.full((1, LANES), log_scale[0], jnp.float32))
    others = halves(pair[:count])
    texts = halves(near[...])
    matched = untwist(pair[count:count + 1, :LANES], rows, lax.axis_index("txt")).astype(jnp.int32)
    ids = text_ids((texts[0].shape[0], count), n_img, cols, False)
    _, d = derivative(texts, others, ids, matched, scale, bias[0])
    term = dot(halves(d_ref[...]), halves(bundle[:count]), (1, 0)) + dot(halves(d), others, (1, 0))
    for k, ref in enumerate(block_refs):
        ref[...] = term[k * cols:(k + 1) * cols]


def image_sum_kernel(n_txt, own_ref, loss_ref, *refs):
    messages, (image_loss, image_grad) = refs[:n_txt - 1], refs[n_txt - 1:]
    rows, width = own_ref.shape
    across = width // LANES
    for r in range(rows // 8):
        for c in range(across):
            at = (slice(r * 8, r * 8 + 8), slice(c * LANES, (c + 1) * LANES))
            image_grad[at] = own_ref[at] + sum(m[r * across + c] for m in messages)
    image_loss[...] = (loss_ref[...] + sum(m[rows // 8 * across] for m in messages))[:1]


def text_sum_kernel(_, *refs):
    blocks, text_grad = refs[:-1], refs[-1]
    text_grad[...] = sum(b[...] for b in blocks)


def in_vmem(*arrays):
    return [pltpu.with_memory_space_constraint(x, pltpu.VMEM) for x in arrays]


def vmem(shape):
    return pltpu.VMEM(shape, jnp.float32)


def per_device(sizes, image_emb, text_emb, pairs, log_scale, bias):
    n_img, n_txt = sizes
    chips = n_img // 2
    rows, cols, width = image_emb.shape[0], text_emb.shape[0], image_emb.shape[1]
    count = n_txt * rows
    tiles = rows * width // (8 * LANES)
    smem, whole = pl.BlockSpec(memory_space=pltpu.SMEM), pl.BlockSpec(memory_space=pltpu.VMEM)

    near = text_emb
    image_blocks = {0: image_emb}
    order = [k for k in range(2, n_txt)] + [1]
    step = 1
    while step < chips:
        near = jnp.concatenate([near, exchange(near, "img", n_img, 2 * step)])
        for k in order[:2]:
            image_blocks[k] = exchange(image_emb, "txt", n_txt, k)
        order = order[2:]
        step *= 2
    for k in order:
        image_blocks[k] = exchange(image_emb, "txt", n_txt, k)
    far = exchange(near, "img", n_img, 1)
    pair_row = jnp.pad(pairs.astype(jnp.float32)[None], ((0, 7), (0, width - count)))
    bundle = jnp.concatenate([image_blocks[k] for k in range(n_txt)] + [pair_row])
    pair = exchange(bundle, "img", n_img, 1)

    own, loss_tile, d_near, *messages = pl.pallas_call(
        functools.partial(image_kernel, n_img, n_txt, rows, cols),
        out_shape=[vmem((rows, width)), vmem((8, LANES)), vmem((chips * cols, count))]
        + [vmem((tiles + 1, 8, LANES))] * (n_txt - 1),
        in_specs=[smem] * 2 + [whole] * 3,
        out_specs=[whole] * (2 + n_txt),
        name="image_terms",
    )(log_scale, bias, *in_vmem(bundle, near, far))
    messages = [exchange(m, "txt", n_txt, k) for k, m in enumerate(messages, 1)]

    blocks = pl.pallas_call(
        functools.partial(text_kernel, n_img, n_txt, rows, cols),
        out_shape=[vmem((cols, width))] * chips,
        in_specs=[smem] * 2 + [whole] * 4,
        out_specs=[whole] * chips,
        name="text_terms",
    )(log_scale, bias, *in_vmem(bundle, pair, near, d_near))
    blocks = [blocks[0]] + [exchange(blocks[k], "img", n_img, 2 * k) for k in range(1, chips)]

    image_loss, image_grad = pl.pallas_call(
        functools.partial(image_sum_kernel, n_txt),
        out_shape=[
            jax.ShapeDtypeStruct((1, LANES), jnp.float32),
            jax.ShapeDtypeStruct(image_emb.shape, jnp.float32),
        ],
        in_specs=[whole] * (1 + n_txt),
        out_specs=[whole] * 2,
        name="image_sums",
    )(*in_vmem(own, loss_tile, *messages))
    text_grad = pl.pallas_call(
        text_sum_kernel,
        out_shape=jax.ShapeDtypeStruct(text_emb.shape, jnp.float32),
        in_specs=[pl.BlockSpec(memory_space=pl.ANY)] + [whole] * chips,
        out_specs=whole,
        name="text_sums",
    )(image_loss, *in_vmem(*blocks))
    return (image_loss.reshape(count), image_grad, text_grad)


def per_device_large(image_emb, text_emb, pairs, log_scale, bias):
    images = lax.all_gather(image_emb, "txt", axis=0, tiled=True)
    texts = lax.all_gather(text_emb, "img", axis=0, tiled=True)
    scale = jnp.exp(log_scale[0])
    shift = bias[0]
    text_count = texts.shape[0]
    dots = lax.dot_general(
        images,
        texts,
        (((1,), (1,)), ((), ())),
        precision=lax.Precision.HIGHEST,
        preferred_element_type=jnp.float32,
    )
    logits = scale * dots + shift
    columns = lax.axis_index("txt") * text_count + jnp.arange(text_count, dtype=jnp.int32)
    sign = jnp.where(pairs[:, None] == columns[None, :], 1.0, -1.0).astype(jnp.float32)
    loss_part = jnp.sum(jax.nn.softplus(-sign * logits), axis=1)
    image_loss = lax.psum(loss_part, "txt")
    dlogits = -sign * jax.nn.sigmoid(-sign * logits)
    image_term = scale * jnp.dot(
        dlogits, texts, precision=lax.Precision.HIGHEST, preferred_element_type=jnp.float32
    )
    image_grad = lax.psum_scatter(image_term, "txt", scatter_dimension=0, tiled=True)
    text_term = scale * lax.dot_general(
        dlogits,
        images,
        (((0,), (0,)), ((), ())),
        precision=lax.Precision.HIGHEST,
        preferred_element_type=jnp.float32,
    )
    text_grad = lax.psum_scatter(text_term, "img", scatter_dimension=0, tiled=True)
    return (image_loss, image_grad, text_grad)


def solution(mesh):
    sizes = (mesh.shape["img"], mesh.shape["txt"])

    def body(image_emb, *others):
        small = all(n in (2, 4, 8) for n in sizes)
        if small and sizes[1] * image_emb.shape[0] == LANES and image_emb.shape[0] % 8 == 0:
            return per_device(sizes, image_emb, *others)
        return per_device_large(image_emb, *others)

    return jax.shard_map(
        body,
        mesh=mesh,
        in_specs=(P(("img", "txt"), None), P(("txt", "img"), None), P("img"), P(), P()),
        out_specs=(P("img"), P(("img", "txt"), None), P(("txt", "img"), None)),
        check_vma=False,
    )
```

```python
import functools

import jax
import jax.numpy as jnp
from jax import lax
from jax.experimental import pallas as pl
from jax.experimental.pallas import tpu as pltpu
from jax.sharding import PartitionSpec as P

LANES = 128


def exchange(x, axis, n, k):
    return lax.ppermute(x, axis, [(i, i ^ k) for i in range(n)])


def halves(x):
    high = x.astype(jnp.bfloat16)
    return high, (x - high.astype(jnp.float32)).astype(jnp.bfloat16)


def dot(a, b, contract):
    def part(x, y):
        dims = ((contract[:1], contract[1:]), ((), ()))
        return lax.dot_general(x, y, dims, preferred_element_type=jnp.float32)

    return part(a[0], b[0]) + (part(a[0], b[1]) + part(a[1], b[0]))


def untwist(row, block, me):
    lane = lax.broadcasted_iota(jnp.int32, row.shape, 1)
    step = block
    while step < LANES:
        up, down = pltpu.roll(row, LANES - step, 1), pltpu.roll(row, step, 1)
        flipped = jnp.where((lane // step) % 2 == 0, up, down)
        row = jnp.where((me // (step // block)) % 2 == 1, flipped, row)
        step *= 2
    return row


def text_ids(shape, n_img, cols, far):
    me_img, me_txt = lax.axis_index("img"), lax.axis_index("txt")
    place = lax.broadcasted_iota(jnp.int32, shape, 0)
    half = n_img // 2 * cols
    core = me_img % 2
    if far:
        core = core ^ (place // half)
        place = place % half
    chip = (me_img // 2) ^ (place // cols)
    return (me_txt * n_img + 2 * chip + core) * cols + place % cols


def derivative(texts, images, ids, matched, scale, shift):
    logits = scale * dot(texts, images, (1, 1)) + shift
    match = ids == matched
    v = jnp.where(match, -logits, logits)
    e = jnp.exp(-jnp.abs(v))
    loss = jnp.maximum(v, 0.0) + jnp.log1p(e)
    s = scale * jnp.where(v >= 0, 1.0, e) / (1.0 + e)
    return loss, jnp.where(match, -s, s)


def image_kernel(n_img, n_txt, rows, cols, *refs):
    log_scale, bias, bundle, near, far, own_ref, loss_ref, d_ref = refs[:8]
    message_refs = refs[8:]
    count = n_txt * rows
    me_txt = lax.axis_index("txt")
    scale = jnp.exp(jnp.full((1, LANES), log_scale[0], jnp.float32))
    images = halves(bundle[:count])
    texts = halves(jnp.concatenate([near[...], far[...]]))
    matched = untwist(bundle[count:count + 1, :LANES], rows, me_txt).astype(jnp.int32)
    ids = text_ids((texts[0].shape[0], count), n_img, cols, True)
    loss, d = derivative(texts, images, ids, matched, scale, bias[0])
    d_ref[...] = d[:near.shape[0]]
    term = dot(halves(d), texts, (0, 0))
    own_ref[...] = term[:rows]
    loss_row = untwist(jnp.sum(loss, axis=0, keepdims=True), rows, me_txt)
    loss_tile = jnp.broadcast_to(loss_row, (8, LANES))
    loss_ref[...] = loss_tile
    across = term.shape[1] // LANES
    for k, ref in enumerate(message_refs, 1):
        for r in range(rows // 8):
            for c in range(across):
                ref[r * across + c] = term[
                    k * rows + r * 8:k * rows + r * 8 + 8, c * LANES:(c + 1) * LANES
                ]
        ref[rows // 8 * across] = loss_tile


def text_kernel(n_img, n_txt, rows, cols, *refs):
    log_scale, bias, bundle, pair, near, d_ref = refs[:6]
    block_refs = refs[6:]
    count = n_txt * rows
    scale = jnp.exp(jnp.full((1, LANES), log_scale[0], jnp.float32))
    others = halves(pair[:count])
    texts = halves(near[...])
    matched = untwist(pair[count:count + 1, :LANES], rows, lax.axis_index("txt")).astype(jnp.int32)
    ids = text_ids((texts[0].shape[0], count), n_img, cols, False)
    _, d = derivative(texts, others, ids, matched, scale, bias[0])
    term = dot(halves(d_ref[...]), halves(bundle[:count]), (1, 0)) + dot(halves(d), others, (1, 0))
    for k, ref in enumerate(block_refs):
        ref[...] = term[k * cols:(k + 1) * cols]


def image_sum_kernel(n_txt, own_ref, loss_ref, *refs):
    messages, (image_loss, image_grad) = refs[:n_txt - 1], refs[n_txt - 1:]
    rows, width = own_ref.shape
    across = width // LANES
    for r in range(rows // 8):
        for c in range(across):
            at = (slice(r * 8, r * 8 + 8), slice(c * LANES, (c + 1) * LANES))
            image_grad[at] = own_ref[at] + sum(m[r * across + c] for m in messages)
    image_loss[...] = (loss_ref[...] + sum(m[rows // 8 * across] for m in messages))[:1]


def text_sum_kernel(_, *refs):
    blocks, text_grad = refs[:-1], refs[-1]
    text_grad[...] = sum(b[...] for b in blocks)


def in_vmem(*arrays):
    return [pltpu.with_memory_space_constraint(x, pltpu.VMEM) for x in arrays]


def vmem(shape):
    return pltpu.VMEM(shape, jnp.float32)


def per_device(sizes, image_emb, text_emb, pairs, log_scale, bias):
    n_img, n_txt = sizes
    chips = n_img // 2
    rows, cols, width = image_emb.shape[0], text_emb.shape[0], image_emb.shape[1]
    count = n_txt * rows
    tiles = rows * width // (8 * LANES)
    smem, whole = pl.BlockSpec(memory_space=pltpu.SMEM), pl.BlockSpec(memory_space=pltpu.VMEM)

    text_blocks, image_blocks = {0: text_emb}, {0: image_emb}
    for k in range(1, max(n_txt, chips)):
        if k < chips:
            text_blocks[k] = exchange(text_emb, "img", n_img, 2 * k)
        if 1 < k < n_txt:
            image_blocks[k] = exchange(image_emb, "txt", n_txt, k)
    late_image, _ = lax.optimization_barrier((image_emb, text_blocks[1]))
    image_blocks[1] = exchange(late_image, "txt", n_txt, 1)
    near = jnp.concatenate([text_blocks[k] for k in range(chips)])
    far = exchange(near, "img", n_img, 1)
    pair_row = jnp.pad(pairs.astype(jnp.float32)[None], ((0, 7), (0, width - count)))
    bundle = jnp.concatenate([image_blocks[k] for k in range(n_txt)] + [pair_row])
    pair = exchange(bundle, "img", n_img, 1)

    own, loss_tile, d_near, *messages = pl.pallas_call(
        functools.partial(image_kernel, n_img, n_txt, rows, cols),
        out_shape=[vmem((rows, width)), vmem((8, LANES)), vmem((chips * cols, count))]
        + [vmem((tiles + 1, 8, LANES))] * (n_txt - 1),
        in_specs=[smem] * 2 + [whole] * 3,
        out_specs=[whole] * (2 + n_txt),
        name="image_terms",
    )(log_scale, bias, *in_vmem(bundle, near, far))
    messages = [exchange(m, "txt", n_txt, k) for k, m in enumerate(messages, 1)]

    blocks = pl.pallas_call(
        functools.partial(text_kernel, n_img, n_txt, rows, cols),
        out_shape=[vmem((cols, width))] * chips,
        in_specs=[smem] * 2 + [whole] * 4,
        out_specs=[whole] * chips,
        name="text_terms",
    )(log_scale, bias, *in_vmem(bundle, pair, near, d_near))
    blocks = [blocks[0]] + [exchange(blocks[k], "img", n_img, 2 * k) for k in range(1, chips)]

    image_loss, image_grad = pl.pallas_call(
        functools.partial(image_sum_kernel, n_txt),
        out_shape=[
            jax.ShapeDtypeStruct((1, LANES), jnp.float32),
            jax.ShapeDtypeStruct(image_emb.shape, jnp.float32),
        ],
        in_specs=[whole] * (1 + n_txt),
        out_specs=[whole] * 2,
        name="image_sums",
    )(*in_vmem(own, loss_tile, *messages))
    text_grad = pl.pallas_call(
        text_sum_kernel,
        out_shape=jax.ShapeDtypeStruct(text_emb.shape, jnp.float32),
        in_specs=[pl.BlockSpec(memory_space=pl.ANY)] + [whole] * chips,
        out_specs=whole,
        name="text_sums",
    )(image_loss, *in_vmem(*blocks))
    return (image_loss.reshape(count), image_grad, text_grad)


def per_device_large(image_emb, text_emb, pairs, log_scale, bias):
    images = lax.all_gather(image_emb, "txt", axis=0, tiled=True)
    texts = lax.all_gather(text_emb, "img", axis=0, tiled=True)
    scale = jnp.exp(log_scale[0])
    shift = bias[0]
    text_count = texts.shape[0]
    dots = lax.dot_general(
        images,
        texts,
        (((1,), (1,)), ((), ())),
        precision=lax.Precision.HIGHEST,
        preferred_element_type=jnp.float32,
    )
    logits = scale * dots + shift
    columns = lax.axis_index("txt") * text_count + jnp.arange(text_count, dtype=jnp.int32)
    sign = jnp.where(pairs[:, None] == columns[None, :], 1.0, -1.0).astype(jnp.float32)
    loss_part = jnp.sum(jax.nn.softplus(-sign * logits), axis=1)
    image_loss = lax.psum(loss_part, "txt")
    dlogits = -sign * jax.nn.sigmoid(-sign * logits)
    image_term = scale * jnp.dot(
        dlogits, texts, precision=lax.Precision.HIGHEST, preferred_element_type=jnp.float32
    )
    image_grad = lax.psum_scatter(image_term, "txt", scatter_dimension=0, tiled=True)
    text_term = scale * lax.dot_general(
        dlogits,
        images,
        (((0,), (0,)), ((), ())),
        precision=lax.Precision.HIGHEST,
        preferred_element_type=jnp.float32,
    )
    text_grad = lax.psum_scatter(text_term, "img", scatter_dimension=0, tiled=True)
    return (image_loss, image_grad, text_grad)


def solution(mesh):
    sizes = (mesh.shape["img"], mesh.shape["txt"])

    def body(image_emb, *others):
        small = all(n in (2, 4, 8) for n in sizes)
        if small and sizes[1] * image_emb.shape[0] == LANES and image_emb.shape[0] % 8 == 0:
            return per_device(sizes, image_emb, *others)
        return per_device_large(image_emb, *others)

    return jax.shard_map(
        body,
        mesh=mesh,
        in_specs=(P(("img", "txt"), None), P(("txt", "img"), None), P("img"), P(), P()),
        out_specs=(P("img"), P(("img", "txt"), None), P(("txt", "img"), None)),
        check_vma=False,
    )
```

```python
import functools

import jax
import jax.numpy as jnp
from jax import lax
from jax.experimental import pallas as pl
from jax.experimental.pallas import tpu as pltpu
from jax.sharding import PartitionSpec as P

LANES = 128


def exchange(x, axis, n, k):
    return lax.ppermute(x, axis, [(i, i ^ k) for i in range(n)])


def halves(x):
    high = x.astype(jnp.bfloat16)
    return high, (x - high.astype(jnp.float32)).astype(jnp.bfloat16)


def dot(a, b, contract):
    def part(x, y):
        dims = ((contract[:1], contract[1:]), ((), ()))
        return lax.dot_general(x, y, dims, preferred_element_type=jnp.float32)

    return part(a[0], b[0]) + (part(a[0], b[1]) + part(a[1], b[0]))


def untwist(row, block, me):
    lane = lax.broadcasted_iota(jnp.int32, row.shape, 1)
    step = block
    while step < LANES:
        up, down = pltpu.roll(row, LANES - step, 1), pltpu.roll(row, step, 1)
        flipped = jnp.where((lane // step) % 2 == 0, up, down)
        row = jnp.where((me // (step // block)) % 2 == 1, flipped, row)
        step *= 2
    return row


def text_ids(shape, n_img, cols, far):
    me_img, me_txt = lax.axis_index("img"), lax.axis_index("txt")
    place = lax.broadcasted_iota(jnp.int32, shape, 0)
    half = n_img // 2 * cols
    core = me_img % 2
    if far:
        core = core ^ (place // half)
        place = place % half
    chip = (me_img // 2) ^ (place // cols)
    return (me_txt * n_img + 2 * chip + core) * cols + place % cols


def derivative(texts, images, ids, matched, scale, shift):
    logits = scale * dot(texts, images, (1, 1)) + shift
    match = ids == matched
    v = jnp.where(match, -logits, logits)
    e = jnp.exp(-jnp.abs(v))
    loss = jnp.maximum(v, 0.0) + jnp.log1p(e)
    s = scale * jnp.where(v >= 0, 1.0, e) / (1.0 + e)
    return loss, jnp.where(match, -s, s)


def row_of_numbers(bundle, rows, count):
    matched = untwist(bundle[count:count + 1, :LANES], rows, lax.axis_index("txt"))
    scale = jnp.exp(bundle[count:count + 1, LANES:2 * LANES])
    return matched.astype(jnp.int32), scale, bundle[count:count + 1, 2 * LANES:3 * LANES]


def image_kernel(
    n_img, n_txt, rows, cols, bundle, near, far, own, first, second, third, d_near
):
    count = n_txt * rows
    me_txt = lax.axis_index("txt")
    matched, scale, shift = row_of_numbers(bundle, rows, count)
    images = halves(bundle[:count])
    texts = halves(jnp.concatenate([near[...], far[...]]))
    ids = text_ids((texts[0].shape[0], count), n_img, cols, True)
    loss, d = derivative(texts, images, ids, matched, scale, shift)
    d_near[...] = d[:near.shape[0]]
    term = dot(halves(d), texts, (0, 0))
    own[...] = term[:rows]
    first[...] = term[rows:2 * rows]
    loss_row = untwist(jnp.sum(loss, axis=0, keepdims=True), rows, me_txt)
    loss_tile = jnp.broadcast_to(loss_row, (8, LANES))
    across = term.shape[1] // LANES
    for k, ref in ((2, second), (3, third)):
        for r in range(rows // 8):
            for c in range(across):
                ref[r * across + c] = term[
                    k * rows + r * 8:k * rows + r * 8 + 8, c * LANES:(c + 1) * LANES
                ]
        ref[rows // 8 * across] = loss_tile


def text_kernel(n_img, n_txt, rows, cols, *refs):
    bundle, pair, near, d_ref = refs[:4]
    block_refs = refs[4:]
    count = n_txt * rows
    matched, scale, shift = row_of_numbers(pair, rows, count)
    others = halves(pair[:count])
    texts = halves(near[...])
    ids = text_ids((texts[0].shape[0], count), n_img, cols, False)
    _, d = derivative(texts, others, ids, matched, scale, shift)
    term = dot(halves(d_ref[...]), halves(bundle[:count]), (1, 0)) + dot(halves(d), others, (1, 0))
    for k, ref in enumerate(block_refs):
        ref[...] = term[k * cols:(k + 1) * cols]


def image_sum_kernel(own, first, second, got, image_loss, image_grad):
    rows, width = own.shape
    across = width // LANES
    for r in range(rows // 8):
        for c in range(across):
            at = (slice(r * 8, r * 8 + 8), slice(c * LANES, (c + 1) * LANES))
            image_grad[at] = own[at] + first[at] + got[r * across + c]
    image_loss[...] = (second[rows // 8 * across] + got[rows // 8 * across])[:1]


def text_sum_kernel(_, *refs):
    blocks, text_grad = refs[:-1], refs[-1]
    text_grad[...] = sum(b[...] for b in blocks)


def in_vmem(*arrays):
    return [pltpu.with_memory_space_constraint(x, pltpu.VMEM) for x in arrays]


def vmem(shape):
    return pltpu.VMEM(shape, jnp.float32)


def per_device(sizes, image_emb, text_emb, pairs, log_scale, bias):
    n_img, n_txt = sizes
    chips = n_img // 2
    rows, cols, width = image_emb.shape[0], text_emb.shape[0], image_emb.shape[1]
    count = n_txt * rows
    tiles = rows * width // (8 * LANES)
    whole = pl.BlockSpec(memory_space=pltpu.VMEM)

    second_image = exchange(image_emb, "txt", n_txt, 2)
    text_blocks = [text_emb]
    for k in range(1, chips):
        text_blocks.append(exchange(text_emb, "img", n_img, 2 * k))
    first_image = exchange(image_emb, "txt", n_txt, 1)
    third_image = exchange(second_image, "txt", n_txt, 1)
    near = jnp.concatenate(text_blocks)
    far = exchange(near, "img", n_img, 1)
    numbers = jnp.concatenate(
        [pairs.astype(jnp.float32), jnp.broadcast_to(log_scale, LANES), jnp.broadcast_to(bias, LANES)]
    )
    numbers = jnp.pad(numbers[None], ((0, 7), (0, width - numbers.shape[0])))
    bundle = jnp.concatenate([image_emb, first_image, second_image, third_image, numbers])
    pair = exchange(bundle, "img", n_img, 1)

    own, first, second, third, d_near = pl.pallas_call(
        functools.partial(image_kernel, n_img, n_txt, rows, cols),
        out_shape=[vmem((rows, width))] * 2
        + [vmem((tiles + 1, 8, LANES))] * 2
        + [vmem((chips * cols, count))],
        in_specs=[whole] * 3,
        out_specs=[whole] * 5,
        name="image_terms",
    )(*in_vmem(bundle, near, far))
    blocks = list(pl.pallas_call(
        functools.partial(text_kernel, n_img, n_txt, rows, cols),
        out_shape=[vmem((cols, width))] * chips,
        in_specs=[whole] * 4,
        out_specs=[whole] * chips,
        name="text_terms",
    )(*in_vmem(bundle, pair, near, d_near)))
    third, _ = lax.optimization_barrier((exchange(third, "txt", n_txt, 1), blocks[0]))
    second = second + third
    got = exchange(second, "txt", n_txt, 2)
    first = exchange(first, "txt", n_txt, 1)
    for k in range(chips - 1, 0, -1):
        blocks[k] = exchange(blocks[k], "img", n_img, 2 * k)

    image_loss, image_grad = pl.pallas_call(
        image_sum_kernel,
        out_shape=[
            jax.ShapeDtypeStruct((1, LANES), jnp.float32),
            jax.ShapeDtypeStruct(image_emb.shape, jnp.float32),
        ],
        in_specs=[whole] * 4,
        out_specs=[whole] * 2,
        name="image_sums",
    )(*in_vmem(own, first, second, got))
    text_grad = pl.pallas_call(
        text_sum_kernel,
        out_shape=jax.ShapeDtypeStruct(text_emb.shape, jnp.float32),
        in_specs=[pl.BlockSpec(memory_space=pl.ANY)] + [whole] * chips,
        out_specs=whole,
        name="text_sums",
    )(image_loss, *in_vmem(*blocks))
    return (image_loss.reshape(count), image_grad, text_grad)


def per_device_large(image_emb, text_emb, pairs, log_scale, bias):
    images = lax.all_gather(image_emb, "txt", axis=0, tiled=True)
    texts = lax.all_gather(text_emb, "img", axis=0, tiled=True)
    scale = jnp.exp(log_scale[0])
    shift = bias[0]
    text_count = texts.shape[0]
    dots = lax.dot_general(
        images,
        texts,
        (((1,), (1,)), ((), ())),
        precision=lax.Precision.HIGHEST,
        preferred_element_type=jnp.float32,
    )
    logits = scale * dots + shift
    columns = lax.axis_index("txt") * text_count + jnp.arange(text_count, dtype=jnp.int32)
    sign = jnp.where(pairs[:, None] == columns[None, :], 1.0, -1.0).astype(jnp.float32)
    loss_part = jnp.sum(jax.nn.softplus(-sign * logits), axis=1)
    image_loss = lax.psum(loss_part, "txt")
    dlogits = -sign * jax.nn.sigmoid(-sign * logits)
    image_term = scale * jnp.dot(
        dlogits, texts, precision=lax.Precision.HIGHEST, preferred_element_type=jnp.float32
    )
    image_grad = lax.psum_scatter(image_term, "txt", scatter_dimension=0, tiled=True)
    text_term = scale * lax.dot_general(
        dlogits,
        images,
        (((0,), (0,)), ((), ())),
        precision=lax.Precision.HIGHEST,
        preferred_element_type=jnp.float32,
    )
    text_grad = lax.psum_scatter(text_term, "img", scatter_dimension=0, tiled=True)
    return (image_loss, image_grad, text_grad)


def solution(mesh):
    sizes = (mesh.shape["img"], mesh.shape["txt"])

    def body(image_emb, *others):
        rows = image_emb.shape[0]
        if sizes[0] in (4, 8) and sizes[1] == 4 and rows * 4 == LANES:
            return per_device(sizes, image_emb, *others)
        return per_device_large(image_emb, *others)

    return jax.shard_map(
        body,
        mesh=mesh,
        in_specs=(P(("img", "txt"), None), P(("txt", "img"), None), P("img"), P(), P()),
        out_specs=(P("img"), P(("img", "txt"), None), P(("txt", "img"), None)),
        check_vma=False,
    )
```

```python
import functools

import jax
import jax.numpy as jnp
from jax import lax
from jax.experimental import pallas as pl
from jax.experimental.pallas import tpu as pltpu
from jax.sharding import PartitionSpec as P

LANES = 128


def exchange(x, axis, n, k):
    return lax.ppermute(x, axis, [(i, i ^ k) for i in range(n)])


def after(x, other):
    return lax.optimization_barrier((x, other))[0]


def halves(x):
    high = x.astype(jnp.bfloat16)
    return high, (x - high.astype(jnp.float32)).astype(jnp.bfloat16)


def dot(a, b, contract):
    def part(x, y):
        dims = ((contract[:1], contract[1:]), ((), ()))
        return lax.dot_general(x, y, dims, preferred_element_type=jnp.float32)

    return part(a[0], b[0]) + (part(a[0], b[1]) + part(a[1], b[0]))


def untwist(row, block, me):
    lane = lax.broadcasted_iota(jnp.int32, row.shape, 1)
    step = block
    while step < LANES:
        up, down = pltpu.roll(row, LANES - step, 1), pltpu.roll(row, step, 1)
        flipped = jnp.where((lane // step) % 2 == 0, up, down)
        row = jnp.where((me // (step // block)) % 2 == 1, flipped, row)
        step *= 2
    return row


def text_ids(shape, n_img, cols, far):
    me_img, me_txt = lax.axis_index("img"), lax.axis_index("txt")
    place = lax.broadcasted_iota(jnp.int32, shape, 0)
    half = n_img // 2 * cols
    core = me_img % 2
    if far:
        core = core ^ (place // half)
        place = place % half
    chip = (me_img // 2) ^ (place // cols)
    return (me_txt * n_img + 2 * chip + core) * cols + place % cols


def derivative(texts, images, ids, matched, scale, shift):
    logits = scale * dot(texts, images, (1, 1)) + shift
    match = ids == matched
    v = jnp.where(match, -logits, logits)
    e = jnp.exp(-jnp.abs(v))
    loss = jnp.maximum(v, 0.0) + jnp.log1p(e)
    s = scale * jnp.where(v >= 0, 1.0, e) / (1.0 + e)
    return loss, jnp.where(match, -s, s)


def row_of_numbers(bundle, rows, count):
    matched = untwist(bundle[count:count + 1, :LANES], rows, lax.axis_index("txt"))
    scale = jnp.exp(bundle[count:count + 1, LANES:2 * LANES])
    return matched.astype(jnp.int32), scale, bundle[count:count + 1, 2 * LANES:3 * LANES]


def image_kernel(n_img, n_txt, rows, cols, bundle, near, far, own, loss_ref, d_near, *messages):
    count = n_txt * rows
    matched, scale, shift = row_of_numbers(bundle, rows, count)
    images = halves(bundle[:count])
    texts = halves(jnp.concatenate([near[...], far[...]]))
    ids = text_ids((texts[0].shape[0], count), n_img, cols, True)
    loss, d = derivative(texts, images, ids, matched, scale, shift)
    d_near[...] = d[:near.shape[0]]
    term = dot(halves(d), texts, (0, 0))
    own[...] = term[:rows]
    loss_row = untwist(jnp.sum(loss, axis=0, keepdims=True), rows, lax.axis_index("txt"))
    loss_tile = jnp.broadcast_to(loss_row, (8, LANES))
    loss_ref[...] = loss_tile
    across = term.shape[1] // LANES
    for k, ref in enumerate(messages, 1):
        for r in range(rows // 8):
            for c in range(across):
                ref[r * across + c] = term[
                    k * rows + r * 8:k * rows + r * 8 + 8, c * LANES:(c + 1) * LANES
                ]
        ref[rows // 8 * across] = loss_tile


def text_kernel(n_img, n_txt, rows, cols, *refs):
    bundle, pair, near, d_ref = refs[:4]
    block_refs = refs[4:]
    count = n_txt * rows
    matched, scale, shift = row_of_numbers(pair, rows, count)
    others = halves(pair[:count])
    texts = halves(near[...])
    ids = text_ids((texts[0].shape[0], count), n_img, cols, False)
    _, d = derivative(texts, others, ids, matched, scale, shift)
    term = dot(halves(d_ref[...]), halves(bundle[:count]), (1, 0)) + dot(halves(d), others, (1, 0))
    for k, ref in enumerate(block_refs):
        ref[...] = term[k * cols:(k + 1) * cols]


def image_sum_kernel(n_txt, own_ref, loss_ref, *refs):
    messages, (image_loss, image_grad) = refs[:n_txt - 1], refs[n_txt - 1:]
    rows, width = own_ref.shape
    across = width // LANES
    for r in range(rows // 8):
        for c in range(across):
            at = (slice(r * 8, r * 8 + 8), slice(c * LANES, (c + 1) * LANES))
            image_grad[at] = own_ref[at] + sum(m[r * across + c] for m in messages)
    image_loss[...] = (loss_ref[...] + sum(m[rows // 8 * across] for m in messages))[:1]


def text_sum_kernel(_, *refs):
    blocks, text_grad = refs[:-1], refs[-1]
    text_grad[...] = sum(b[...] for b in blocks)


def in_vmem(*arrays):
    return [pltpu.with_memory_space_constraint(x, pltpu.VMEM) for x in arrays]


def vmem(shape):
    return pltpu.VMEM(shape, jnp.float32)


def per_device(sizes, image_emb, text_emb, pairs, log_scale, bias):
    n_img, n_txt = sizes
    chips = n_img // 2
    rows, cols, width = image_emb.shape[0], text_emb.shape[0], image_emb.shape[1]
    count = n_txt * rows
    tiles = rows * width // (8 * LANES)
    whole = pl.BlockSpec(memory_space=pltpu.VMEM)

    text_blocks, image_blocks = [text_emb], {0: image_emb}
    for k in range(1, max(n_txt, chips)):
        if k < chips:
            text_blocks.append(exchange(text_emb, "img", n_img, 2 * k))
        if 1 < k < n_txt:
            image_blocks[k] = exchange(image_emb, "txt", n_txt, k)
    image_blocks[1] = exchange(after(image_emb, text_blocks[1]), "txt", n_txt, 1)
    near = jnp.concatenate(text_blocks)
    far = exchange(near, "img", n_img, 1)
    numbers = jnp.concatenate(
        [pairs.astype(jnp.float32), jnp.broadcast_to(log_scale, LANES), jnp.broadcast_to(bias, LANES)]
    )
    numbers = jnp.pad(numbers[None], ((0, 7), (0, width - numbers.shape[0])))
    bundle = jnp.concatenate([image_blocks[k] for k in range(n_txt)] + [numbers])

    own, loss_tile, d_near, *messages = pl.pallas_call(
        functools.partial(image_kernel, n_img, n_txt, rows, cols),
        out_shape=[vmem((rows, width)), vmem((8, LANES)), vmem((chips * cols, count))]
        + [vmem((tiles + 1, 8, LANES))] * (n_txt - 1),
        in_specs=[whole] * 3,
        out_specs=[whole] * (2 + n_txt),
        name="image_terms",
    )(*in_vmem(bundle, near, far))
    messages = [exchange(messages[k - 1], "txt", n_txt, k) for k in range(n_txt - 1, 0, -1)]

    pair = exchange(after(bundle, own), "img", n_img, 1)
    blocks = pl.pallas_call(
        functools.partial(text_kernel, n_img, n_txt, rows, cols),
        out_shape=[vmem((cols, width))] * chips,
        in_specs=[whole] * 4,
        out_specs=[whole] * chips,
        name="text_terms",
    )(*in_vmem(bundle, pair, near, d_near))
    blocks = list(blocks)
    blocks[1] = after(blocks[1], messages[-1])
    blocks = [exchange(blocks[k], "img", n_img, 2 * k) for k in range(chips - 1, 0, -1)] + [blocks[0]]

    image_loss, image_grad = pl.pallas_call(
        functools.partial(image_sum_kernel, n_txt),
        out_shape=[
            jax.ShapeDtypeStruct((1, LANES), jnp.float32),
            jax.ShapeDtypeStruct(image_emb.shape, jnp.float32),
        ],
        in_specs=[whole] * (1 + n_txt),
        out_specs=[whole] * 2,
        name="image_sums",
    )(*in_vmem(own, loss_tile, *messages))
    text_grad = pl.pallas_call(
        text_sum_kernel,
        out_shape=jax.ShapeDtypeStruct(text_emb.shape, jnp.float32),
        in_specs=[pl.BlockSpec(memory_space=pl.ANY)] + [whole] * chips,
        out_specs=whole,
        name="text_sums",
    )(image_loss, *in_vmem(*blocks))
    return (image_loss.reshape(count), image_grad, text_grad)


def per_device_large(image_emb, text_emb, pairs, log_scale, bias):
    images = lax.all_gather(image_emb, "txt", axis=0, tiled=True)
    texts = lax.all_gather(text_emb, "img", axis=0, tiled=True)
    scale = jnp.exp(log_scale[0])
    shift = bias[0]
    text_count = texts.shape[0]
    dots = lax.dot_general(
        images,
        texts,
        (((1,), (1,)), ((), ())),
        precision=lax.Precision.HIGHEST,
        preferred_element_type=jnp.float32,
    )
    logits = scale * dots + shift
    columns = lax.axis_index("txt") * text_count + jnp.arange(text_count, dtype=jnp.int32)
    sign = jnp.where(pairs[:, None] == columns[None, :], 1.0, -1.0).astype(jnp.float32)
    loss_part = jnp.sum(jax.nn.softplus(-sign * logits), axis=1)
    image_loss = lax.psum(loss_part, "txt")
    dlogits = -sign * jax.nn.sigmoid(-sign * logits)
    image_term = scale * jnp.dot(
        dlogits, texts, precision=lax.Precision.HIGHEST, preferred_element_type=jnp.float32
    )
    image_grad = lax.psum_scatter(image_term, "txt", scatter_dimension=0, tiled=True)
    text_term = scale * lax.dot_general(
        dlogits,
        images,
        (((0,), (0,)), ((), ())),
        precision=lax.Precision.HIGHEST,
        preferred_element_type=jnp.float32,
    )
    text_grad = lax.psum_scatter(text_term, "img", scatter_dimension=0, tiled=True)
    return (image_loss, image_grad, text_grad)


def solution(mesh):
    sizes = (mesh.shape["img"], mesh.shape["txt"])

    def body(image_emb, *others):
        rows = image_emb.shape[0]
        if sizes[0] in (4, 8) and sizes[1] == 4 and rows * 4 == LANES:
            return per_device(sizes, image_emb, *others)
        return per_device_large(image_emb, *others)

    return jax.shard_map(
        body,
        mesh=mesh,
        in_specs=(P(("img", "txt"), None), P(("txt", "img"), None), P("img"), P(), P()),
        out_specs=(P("img"), P(("img", "txt"), None), P(("txt", "img"), None)),
        check_vma=False,
    )
```

```python
import functools

import jax
import jax.numpy as jnp
from jax import lax
from jax.experimental import pallas as pl
from jax.experimental.pallas import tpu as pltpu
from jax.sharding import PartitionSpec as P

LANES = 128


def exchange(x, axis, n, k):
    return lax.ppermute(x, axis, [(i, i ^ k) for i in range(n)])


def after(x, other):
    return lax.optimization_barrier((x, other))[0]


def halves(x):
    high = x.astype(jnp.bfloat16)
    return high, (x - high.astype(jnp.float32)).astype(jnp.bfloat16)


def dot(a, b, contract):
    def part(x, y):
        dims = ((contract[:1], contract[1:]), ((), ()))
        return lax.dot_general(x, y, dims, preferred_element_type=jnp.float32)

    return part(a[0], b[0]) + (part(a[0], b[1]) + part(a[1], b[0]))


def untwist(row, block, me):
    lane = lax.broadcasted_iota(jnp.int32, row.shape, 1)
    step = block
    while step < LANES:
        up, down = pltpu.roll(row, LANES - step, 1), pltpu.roll(row, step, 1)
        flipped = jnp.where((lane // step) % 2 == 0, up, down)
        row = jnp.where((me // (step // block)) % 2 == 1, flipped, row)
        step *= 2
    return row


def far_first(n):
    return [0] + sorted(range(1, n), key=lambda k: -k.bit_count())


def text_ids(shape, n_img, cols, far):
    me_img, me_txt = lax.axis_index("img"), lax.axis_index("txt")
    place = lax.broadcasted_iota(jnp.int32, shape, 0)
    half = n_img // 2 * cols
    core = me_img % 2
    if far:
        core = core ^ (place // half)
        place = place % half
    distance = sum(jnp.where(place // cols == p, k, 0) for p, k in enumerate(far_first(n_img // 2)))
    chip = (me_img // 2) ^ distance
    return (me_txt * n_img + 2 * chip + core) * cols + place % cols


def derivative(texts, images, ids, matched, scale, shift):
    logits = scale * dot(texts, images, (1, 1)) + shift
    match = ids == matched
    v = jnp.where(match, -logits, logits)
    e = jnp.exp(-jnp.abs(v))
    loss = jnp.maximum(v, 0.0) + jnp.log1p(e)
    s = scale * jnp.where(v >= 0, 1.0, e) / (1.0 + e)
    return loss, jnp.where(match, -s, s)


def row_of_numbers(bundle, rows, count):
    matched = untwist(bundle[count:count + 1, :LANES], rows, lax.axis_index("txt"))
    scale = jnp.exp(bundle[count:count + 1, LANES:2 * LANES])
    return matched.astype(jnp.int32), scale, bundle[count:count + 1, 2 * LANES:3 * LANES]


def image_kernel(n_img, n_txt, rows, cols, bundle, near, far, own, loss_ref, d_near, *messages):
    count = n_txt * rows
    matched, scale, shift = row_of_numbers(bundle, rows, count)
    images = halves(bundle[:count])
    texts = halves(jnp.concatenate([near[...], far[...]]))
    ids = text_ids((texts[0].shape[0], count), n_img, cols, True)
    loss, d = derivative(texts, images, ids, matched, scale, shift)
    d_near[...] = d[:near.shape[0]]
    term = dot(halves(d), texts, (0, 0))
    own[...] = term[:rows]
    loss_row = untwist(jnp.sum(loss, axis=0, keepdims=True), rows, lax.axis_index("txt"))
    loss_tile = jnp.broadcast_to(loss_row, (8, LANES))
    loss_ref[...] = loss_tile
    across = term.shape[1] // LANES
    for k, ref in enumerate(messages, 1):
        for r in range(rows // 8):
            for c in range(across):
                ref[r * across + c] = term[
                    k * rows + r * 8:k * rows + r * 8 + 8, c * LANES:(c + 1) * LANES
                ]
        ref[rows // 8 * across] = loss_tile


def text_kernel(n_img, n_txt, rows, cols, *refs):
    bundle, pair, near, d_ref = refs[:4]
    block_refs = refs[4:]
    count = n_txt * rows
    matched, scale, shift = row_of_numbers(pair, rows, count)
    others = halves(pair[:count])
    texts = halves(near[...])
    ids = text_ids((texts[0].shape[0], count), n_img, cols, False)
    _, d = derivative(texts, others, ids, matched, scale, shift)
    term = dot(halves(d_ref[...]), halves(bundle[:count]), (1, 0)) + dot(halves(d), others, (1, 0))
    for k, ref in enumerate(block_refs):
        ref[...] = term[k * cols:(k + 1) * cols]


def sum_kernel(n_txt, n_chips, own_ref, loss_ref, *refs):
    messages, blocks = refs[:n_txt - 1], refs[n_txt - 1:n_txt - 1 + n_chips]
    image_loss, image_grad, text_grad = refs[n_txt - 1 + n_chips:]
    text_grad[...] = sum(b[...] for b in blocks)
    rows, width = own_ref.shape
    across = width // LANES
    for r in range(rows // 8):
        for c in range(across):
            at = (slice(r * 8, r * 8 + 8), slice(c * LANES, (c + 1) * LANES))
            image_grad[at] = own_ref[at] + sum(m[r * across + c] for m in messages)
    image_loss[...] = (loss_ref[...] + sum(m[rows // 8 * across] for m in messages))[:1]


def in_vmem(*arrays):
    return [pltpu.with_memory_space_constraint(x, pltpu.VMEM) for x in arrays]


def vmem(shape):
    return pltpu.VMEM(shape, jnp.float32)


def per_device(sizes, image_emb, text_emb, pairs, log_scale, bias):
    n_img, n_txt = sizes
    chips = n_img // 2
    rows, cols, width = image_emb.shape[0], text_emb.shape[0], image_emb.shape[1]
    count = n_txt * rows
    tiles = rows * width // (8 * LANES)
    whole = pl.BlockSpec(memory_space=pltpu.VMEM)

    text_order = far_first(chips)
    text_blocks = [text_emb] + [exchange(text_emb, "img", n_img, 2 * k) for k in text_order[1:]]
    image_blocks = {k: exchange(image_emb, "txt", n_txt, k) for k in range(2, n_txt)}
    image_blocks[0] = image_emb
    image_blocks[1] = exchange(after(image_emb, text_blocks[min(2, chips - 1)]), "txt", n_txt, 1)
    near = jnp.concatenate(text_blocks)
    far = exchange(near, "img", n_img, 1)
    numbers = jnp.concatenate(
        [pairs.astype(jnp.float32), jnp.broadcast_to(log_scale, LANES), jnp.broadcast_to(bias, LANES)]
    )
    numbers = jnp.pad(numbers[None], ((0, 7), (0, width - numbers.shape[0])))
    bundle = jnp.concatenate([image_blocks[k] for k in range(n_txt)] + [numbers])

    own, loss_tile, d_near, *messages = pl.pallas_call(
        functools.partial(image_kernel, n_img, n_txt, rows, cols),
        out_shape=[vmem((rows, width)), vmem((8, LANES)), vmem((chips * cols, count))]
        + [vmem((tiles + 1, 8, LANES))] * (n_txt - 1),
        in_specs=[whole] * 3,
        out_specs=[whole] * (2 + n_txt),
        name="image_terms",
    )(*in_vmem(bundle, near, far))
    messages = [exchange(messages[k - 1], "txt", n_txt, k) for k in (1, 3, 2)]

    pair = exchange(after(bundle, own), "img", n_img, 1)
    blocks = pl.pallas_call(
        functools.partial(text_kernel, n_img, n_txt, rows, cols),
        out_shape=[vmem((cols, width))] * chips,
        in_specs=[whole] * 4,
        out_specs=[whole] * chips,
        name="text_terms",
    )(*in_vmem(bundle, pair, near, d_near))
    blocks = list(blocks)
    for p, k in enumerate(text_order):
        if k:
            blocks[p] = exchange(blocks[p], "img", n_img, 2 * k)

    image_loss, image_grad, text_grad = pl.pallas_call(
        functools.partial(sum_kernel, n_txt, chips),
        out_shape=[
            jax.ShapeDtypeStruct(shape, jnp.float32)
            for shape in ((1, LANES), image_emb.shape, text_emb.shape)
        ],
        in_specs=[whole] * (1 + n_txt + chips),
        out_specs=[whole] * 3,
        name="sums",
    )(*in_vmem(own, loss_tile, *messages, *blocks))
    return (image_loss.reshape(count), image_grad, text_grad)


def per_device_large(image_emb, text_emb, pairs, log_scale, bias):
    images = lax.all_gather(image_emb, "txt", axis=0, tiled=True)
    texts = lax.all_gather(text_emb, "img", axis=0, tiled=True)
    scale = jnp.exp(log_scale[0])
    shift = bias[0]
    text_count = texts.shape[0]
    dots = lax.dot_general(
        images,
        texts,
        (((1,), (1,)), ((), ())),
        precision=lax.Precision.HIGHEST,
        preferred_element_type=jnp.float32,
    )
    logits = scale * dots + shift
    columns = lax.axis_index("txt") * text_count + jnp.arange(text_count, dtype=jnp.int32)
    sign = jnp.where(pairs[:, None] == columns[None, :], 1.0, -1.0).astype(jnp.float32)
    loss_part = jnp.sum(jax.nn.softplus(-sign * logits), axis=1)
    image_loss = lax.psum(loss_part, "txt")
    dlogits = -sign * jax.nn.sigmoid(-sign * logits)
    image_term = scale * jnp.dot(
        dlogits, texts, precision=lax.Precision.HIGHEST, preferred_element_type=jnp.float32
    )
    image_grad = lax.psum_scatter(image_term, "txt", scatter_dimension=0, tiled=True)
    text_term = scale * lax.dot_general(
        dlogits,
        images,
        (((0,), (0,)), ((), ())),
        precision=lax.Precision.HIGHEST,
        preferred_element_type=jnp.float32,
    )
    text_grad = lax.psum_scatter(text_term, "img", scatter_dimension=0, tiled=True)
    return (image_loss, image_grad, text_grad)


def solution(mesh):
    sizes = (mesh.shape["img"], mesh.shape["txt"])

    def body(image_emb, *others):
        rows = image_emb.shape[0]
        if sizes[0] in (4, 8) and sizes[1] == 4 and rows * 4 == LANES:
            return per_device(sizes, image_emb, *others)
        return per_device_large(image_emb, *others)

    return jax.shard_map(
        body,
        mesh=mesh,
        in_specs=(P(("img", "txt"), None), P(("txt", "img"), None), P("img"), P(), P()),
        out_specs=(P("img"), P(("img", "txt"), None), P(("txt", "img"), None)),
        check_vma=False,
    )
```

```python
import functools

import jax
import jax.numpy as jnp
from jax import lax
from jax.experimental import pallas as pl
from jax.experimental.pallas import tpu as pltpu
from jax.sharding import PartitionSpec as P

LANES = 128

IMAGE_ORDER = (0, 2, 3, 1)


def exchange(x, axis, n, k):
    return lax.ppermute(x, axis, [(i, i ^ k) for i in range(n)])


def after(x, other):
    return lax.optimization_barrier((x, other))[0]


def chip_exchange(x, n_img, distances):
    return lax.ppermute(x, "img", [(i, i ^ (2 * distances[i % 2])) for i in range(n_img)])


def halves(x):
    high = x.astype(jnp.bfloat16)
    return high, (x - high.astype(jnp.float32)).astype(jnp.bfloat16)


def dot(a, b, contract):
    def part(x, y):
        dims = ((contract[:1], contract[1:]), ((), ()))
        return lax.dot_general(x, y, dims, preferred_element_type=jnp.float32)

    return part(a[0], b[0]) + (part(a[0], b[1]) + part(a[1], b[0]))


def untwist(row, block, me):
    lane = lax.broadcasted_iota(jnp.int32, row.shape, 1)
    step = block
    while step < LANES:
        up, down = pltpu.roll(row, LANES - step, 1), pltpu.roll(row, step, 1)
        flipped = jnp.where((lane // step) % 2 == 0, up, down)
        row = jnp.where((me // (step // block)) % 2 == 1, flipped, row)
        step *= 2
    return row


def shuffle(row, block, sources):
    place = lax.broadcasted_iota(jnp.int32, row.shape, 1) // block
    result = row
    for step in range(1, len(sources)):
        moved = pltpu.roll(row, LANES - step * block, 1)
        for p, source in enumerate(sources):
            if (source - p) % len(sources) == step:
                result = jnp.where(place == p, moved, result)
    return result


def text_ids(shape, n_img, cols, far):
    me_img, me_txt = lax.axis_index("img"), lax.axis_index("txt")
    place = lax.broadcasted_iota(jnp.int32, shape, 0)
    half = n_img // 2 * cols
    me_core = me_img % 2
    core = me_core
    if far:
        core = core ^ (place // half)
        place = place % half
    turn = place // cols
    distance = jnp.where(turn == 1, 1 + me_core, jnp.where(turn == 2, 2 - me_core, turn))
    chip = (me_img // 2) ^ distance
    return (me_txt * n_img + 2 * chip + core) * cols + place % cols


def own_core_texts(cols, both, sent, got):
    return [both[:cols], sent[:cols], got[cols:2 * cols], sent[2 * cols:]]


def other_core_texts(cols, both, sent, got):
    return [both[cols:], sent[cols:2 * cols], got[:cols], got[2 * cols:]]


def derivative(texts, images, ids, matched, log_scale, bias):
    scale = jnp.exp(jnp.full((1, LANES), log_scale[0], jnp.float32))
    logits = scale * dot(texts, images, (1, 1)) + bias[0]
    match = ids == matched
    v = jnp.where(match, -logits, logits)
    e = jnp.exp(-jnp.abs(v))
    loss = jnp.maximum(v, 0.0) + jnp.log1p(e)
    s = scale * jnp.where(v >= 0, 1.0, e) / (1.0 + e)
    return loss, jnp.where(match, -s, s)


def matched_texts(bundle, rows, count):
    matched = untwist(bundle[count:count + 1, :LANES], rows, lax.axis_index("txt"))
    return shuffle(matched, rows, IMAGE_ORDER).astype(jnp.int32)


def image_kernel(
    n_img, n_txt, rows, cols, log_scale, bias, bundle, both, sent, got,
    own, loss_ref, d_near, *messages
):
    count = n_txt * rows
    matched = matched_texts(bundle, rows, count)
    images = halves(bundle[:count])
    near = own_core_texts(cols, both, sent, got)
    texts = halves(jnp.concatenate(near + other_core_texts(cols, both, sent, got)))
    ids = text_ids((texts[0].shape[0], count), n_img, cols, True)
    loss, d = derivative(texts, images, ids, matched, log_scale, bias)
    d_near[...] = d[:len(near) * cols]
    term = dot(halves(d), texts, (0, 0))
    own[...] = term[:rows]
    back = [IMAGE_ORDER.index(k) for k in range(n_txt)]
    loss_row = shuffle(jnp.sum(loss, axis=0, keepdims=True), rows, back)
    loss_row = untwist(loss_row, rows, lax.axis_index("txt"))
    loss_tile = jnp.broadcast_to(loss_row, (8, LANES))
    loss_ref[...] = loss_tile
    across = term.shape[1] // LANES
    for p, ref in enumerate(messages, 1):
        for r in range(rows // 8):
            for c in range(across):
                ref[r * across + c] = term[
                    p * rows + r * 8:p * rows + r * 8 + 8, c * LANES:(c + 1) * LANES
                ]
        ref[rows // 8 * across] = loss_tile


def text_kernel(n_img, n_txt, rows, cols, *refs):
    log_scale, bias, bundle, pair, both, sent, got, d_ref = refs[:8]
    block_refs = refs[8:]
    count = n_txt * rows
    matched = matched_texts(pair, rows, count)
    others = halves(pair[:count])
    texts = halves(jnp.concatenate(own_core_texts(cols, both, sent, got)))
    ids = text_ids((texts[0].shape[0], count), n_img, cols, False)
    _, d = derivative(texts, others, ids, matched, log_scale, bias)
    term = dot(halves(d_ref[...]), halves(bundle[:count]), (1, 0)) + dot(halves(d), others, (1, 0))
    for k, ref in enumerate(block_refs):
        ref[...] = term[k * cols:(k + 1) * cols]


def sum_kernel(n_txt, n_chips, own_ref, loss_ref, *refs):
    messages, blocks = refs[:n_txt - 1], refs[n_txt - 1:n_txt - 1 + n_chips]
    image_loss, image_grad, text_grad = refs[n_txt - 1 + n_chips:]
    text_grad[...] = sum(b[...] for b in blocks)
    rows, width = own_ref.shape
    across = width // LANES
    for r in range(rows // 8):
        for c in range(across):
            at = (slice(r * 8, r * 8 + 8), slice(c * LANES, (c + 1) * LANES))
            image_grad[at] = own_ref[at] + sum(m[r * across + c] for m in messages)
    image_loss[...] = (loss_ref[...] + sum(m[rows // 8 * across] for m in messages))[:1]


def in_vmem(*arrays):
    return [pltpu.with_memory_space_constraint(x, pltpu.VMEM) for x in arrays]


def vmem(shape):
    return pltpu.VMEM(shape, jnp.float32)


def per_device(sizes, image_emb, text_emb, pairs, log_scale, bias):
    n_img, n_txt = sizes
    chips = n_img // 2
    rows, cols, width = image_emb.shape[0], text_emb.shape[0], image_emb.shape[1]
    count = n_txt * rows
    tiles = rows * width // (8 * LANES)
    smem, whole = pl.BlockSpec(memory_space=pltpu.SMEM), pl.BlockSpec(memory_space=pltpu.VMEM)

    both = jnp.concatenate([text_emb, exchange(text_emb, "img", n_img, 1)])
    image_blocks = [image_emb] + [None] * (n_txt - 1)
    for k in (2, 3):
        image_blocks[k] = exchange(image_emb, "txt", n_txt, k)
    beside = chip_exchange(both, n_img, (1, 2))
    diagonal = chip_exchange(after(text_emb, both), n_img, (3, 3))
    image_blocks[1] = exchange(after(image_emb, both), "txt", n_txt, 1)
    sent = jnp.concatenate([beside, diagonal])
    got = exchange(sent, "img", n_img, 1)
    numbers = jnp.pad(after(pairs, sent).astype(jnp.float32)[None], ((0, 7), (0, width - count)))
    bundle = jnp.concatenate([image_blocks[k] for k in IMAGE_ORDER] + [numbers])

    own, loss_tile, d_near, *messages = pl.pallas_call(
        functools.partial(image_kernel, n_img, n_txt, rows, cols),
        out_shape=[vmem((rows, width)), vmem((8, LANES)), vmem((chips * cols, count))]
        + [vmem((tiles + 1, 8, LANES))] * (n_txt - 1),
        in_specs=[smem] * 2 + [whole] * 4,
        out_specs=[whole] * (2 + n_txt),
        name="image_terms",
    )(log_scale, bias, *in_vmem(bundle, both, sent, got))
    messages = [exchange(messages[p - 1], "txt", n_txt, IMAGE_ORDER[p]) for p in (3, 2, 1)]

    pair = exchange(after(bundle, own), "img", n_img, 1)
    blocks = pl.pallas_call(
        functools.partial(text_kernel, n_img, n_txt, rows, cols),
        out_shape=[vmem((cols, width))] * chips,
        in_specs=[smem] * 2 + [whole] * 6,
        out_specs=[whole] * chips,
        name="text_terms",
    )(log_scale, bias, *in_vmem(bundle, pair, both, sent, got, d_near))
    blocks = list(blocks)
    for k, distances in ((3, (3, 3)), (1, (1, 2)), (2, (2, 1))):
        blocks[k] = chip_exchange(blocks[k], n_img, distances)

    image_loss, image_grad, text_grad = pl.pallas_call(
        functools.partial(sum_kernel, n_txt, chips),
        out_shape=[
            jax.ShapeDtypeStruct(shape, jnp.float32)
            for shape in ((1, LANES), image_emb.shape, text_emb.shape)
        ],
        in_specs=[whole] * (1 + n_txt + chips),
        out_specs=[whole] * 3,
        name="sums",
    )(*in_vmem(own, loss_tile, *messages, blocks[3], *blocks[:3]))
    return (image_loss.reshape(count), image_grad, text_grad)


def per_device_large(image_emb, text_emb, pairs, log_scale, bias):
    images = lax.all_gather(image_emb, "txt", axis=0, tiled=True)
    texts = lax.all_gather(text_emb, "img", axis=0, tiled=True)
    scale = jnp.exp(log_scale[0])
    shift = bias[0]
    text_count = texts.shape[0]
    dots = lax.dot_general(
        images,
        texts,
        (((1,), (1,)), ((), ())),
        precision=lax.Precision.HIGHEST,
        preferred_element_type=jnp.float32,
    )
    logits = scale * dots + shift
    columns = lax.axis_index("txt") * text_count + jnp.arange(text_count, dtype=jnp.int32)
    sign = jnp.where(pairs[:, None] == columns[None, :], 1.0, -1.0).astype(jnp.float32)
    loss_part = jnp.sum(jax.nn.softplus(-sign * logits), axis=1)
    image_loss = lax.psum(loss_part, "txt")
    dlogits = -sign * jax.nn.sigmoid(-sign * logits)
    image_term = scale * jnp.dot(
        dlogits, texts, precision=lax.Precision.HIGHEST, preferred_element_type=jnp.float32
    )
    image_grad = lax.psum_scatter(image_term, "txt", scatter_dimension=0, tiled=True)
    text_term = scale * lax.dot_general(
        dlogits,
        images,
        (((0,), (0,)), ((), ())),
        precision=lax.Precision.HIGHEST,
        preferred_element_type=jnp.float32,
    )
    text_grad = lax.psum_scatter(text_term, "img", scatter_dimension=0, tiled=True)
    return (image_loss, image_grad, text_grad)


def solution(mesh):
    sizes = (mesh.shape["img"], mesh.shape["txt"])

    def body(image_emb, *others):
        rows = image_emb.shape[0]
        if sizes == (8, 4) and rows * sizes[1] == LANES:
            return per_device(sizes, image_emb, *others)
        return per_device_large(image_emb, *others)

    return jax.shard_map(
        body,
        mesh=mesh,
        in_specs=(P(("img", "txt"), None), P(("txt", "img"), None), P("img"), P(), P()),
        out_specs=(P("img"), P(("img", "txt"), None), P(("txt", "img"), None)),
        check_vma=False,
    )
```

```python
import functools

import jax
import jax.numpy as jnp
from jax import lax
from jax.experimental import pallas as pl
from jax.experimental.pallas import tpu as pltpu
from jax.sharding import PartitionSpec as P

LANES = 128

IMAGE_ORDER = (0, 2, 3, 1)


def exchange(x, axis, n, k):
    return lax.ppermute(x, axis, [(i, i ^ k) for i in range(n)])


def after(x, other):
    return lax.optimization_barrier((x, other))[0]


def chip_exchange(x, n_img, distances):
    return lax.ppermute(x, "img", [(i, i ^ (2 * distances[i % 2])) for i in range(n_img)])


def halves(x):
    high = x.astype(jnp.bfloat16)
    return high, (x - high.astype(jnp.float32)).astype(jnp.bfloat16)


def dot(a, b, contract):
    def part(x, y):
        dims = ((contract[:1], contract[1:]), ((), ()))
        return lax.dot_general(x, y, dims, preferred_element_type=jnp.float32)

    return part(a[0], b[0]) + (part(a[0], b[1]) + part(a[1], b[0]))


def untwist(row, block, me):
    lane = lax.broadcasted_iota(jnp.int32, row.shape, 1)
    step = block
    while step < LANES:
        up, down = pltpu.roll(row, LANES - step, 1), pltpu.roll(row, step, 1)
        flipped = jnp.where((lane // step) % 2 == 0, up, down)
        row = jnp.where((me // (step // block)) % 2 == 1, flipped, row)
        step *= 2
    return row


def shuffle(row, block, sources):
    place = lax.broadcasted_iota(jnp.int32, row.shape, 1) // block
    result = row
    for step in range(1, len(sources)):
        moved = pltpu.roll(row, LANES - step * block, 1)
        for p, source in enumerate(sources):
            if (source - p) % len(sources) == step:
                result = jnp.where(place == p, moved, result)
    return result


def text_ids(shape, n_img, cols, far):
    me_img, me_txt = lax.axis_index("img"), lax.axis_index("txt")
    place = lax.broadcasted_iota(jnp.int32, shape, 0)
    half = n_img // 2 * cols
    me_core = me_img % 2
    core = me_core
    if far:
        core = core ^ (place // half)
        place = place % half
    turn = place // cols
    distance = jnp.where(turn == 1, 1 + me_core, jnp.where(turn == 2, 2 - me_core, turn))
    chip = (me_img // 2) ^ distance
    return (me_txt * n_img + 2 * chip + core) * cols + place % cols


def own_core_texts(cols, both, sent, got):
    return [both[:cols], sent[:cols], got[cols:2 * cols], sent[2 * cols:]]


def other_core_texts(cols, both, sent, got):
    return [both[cols:], sent[cols:2 * cols], got[:cols], got[2 * cols:]]


def derivative(texts, images, ids, matched, log_scale, bias):
    scale = jnp.exp(jnp.full((1, LANES), log_scale[0], jnp.float32))
    logits = scale * dot(texts, images, (1, 1)) + bias[0]
    match = ids == matched
    v = jnp.where(match, -logits, logits)
    e = jnp.exp(-jnp.abs(v))
    loss = jnp.maximum(v, 0.0) + jnp.log1p(e)
    s = scale * jnp.where(v >= 0, 1.0, e) / (1.0 + e)
    return loss, jnp.where(match, -s, s)


def matched_texts(bundle, rows, count):
    matched = untwist(bundle[count:count + 1, :LANES], rows, lax.axis_index("txt"))
    return shuffle(matched, rows, IMAGE_ORDER).astype(jnp.int32)


def image_kernel(
    n_img, n_txt, rows, cols, log_scale, bias, bundle, both, sent, got,
    own, loss_ref, d_near, *messages
):
    count = n_txt * rows
    matched = matched_texts(bundle, rows, count)
    images = halves(bundle[:count])
    near = own_core_texts(cols, both, sent, got)
    texts = halves(jnp.concatenate(near + other_core_texts(cols, both, sent, got)))
    ids = text_ids((texts[0].shape[0], count), n_img, cols, True)
    loss, d = derivative(texts, images, ids, matched, log_scale, bias)
    d_near[...] = d[:len(near) * cols]
    term = dot(halves(d), texts, (0, 0))
    own[...] = term[:rows]
    back = [IMAGE_ORDER.index(k) for k in range(n_txt)]
    loss_row = shuffle(jnp.sum(loss, axis=0, keepdims=True), rows, back)
    loss_row = untwist(loss_row, rows, lax.axis_index("txt"))
    loss_tile = jnp.broadcast_to(loss_row, (8, LANES))
    loss_ref[...] = loss_tile
    across = term.shape[1] // LANES
    for p, ref in enumerate(messages, 1):
        for r in range(rows // 8):
            for c in range(across):
                ref[r * across + c] = term[
                    p * rows + r * 8:p * rows + r * 8 + 8, c * LANES:(c + 1) * LANES
                ]
        ref[rows // 8 * across] = loss_tile


def text_kernel(n_img, n_txt, rows, cols, *refs):
    log_scale, bias, bundle, pair, both, sent, got, d_ref = refs[:8]
    block_refs = refs[8:]
    count = n_txt * rows
    matched = matched_texts(pair, rows, count)
    others = halves(pair[:count])
    texts = halves(jnp.concatenate(own_core_texts(cols, both, sent, got)))
    ids = text_ids((texts[0].shape[0], count), n_img, cols, False)
    _, d = derivative(texts, others, ids, matched, log_scale, bias)
    term = dot(halves(d_ref[...]), halves(bundle[:count]), (1, 0)) + dot(halves(d), others, (1, 0))
    for k, ref in enumerate(block_refs):
        ref[...] = term[k * cols:(k + 1) * cols]


def sum_kernel(n_txt, n_chips, own_ref, loss_ref, *refs):
    messages, blocks = refs[:n_txt - 1], refs[n_txt - 1:n_txt - 1 + n_chips]
    image_loss, image_grad, text_grad = refs[n_txt - 1 + n_chips:]
    text_grad[...] = sum(b[...] for b in blocks)
    rows, width = own_ref.shape
    across = width // LANES
    for r in range(rows // 8):
        for c in range(across):
            at = (slice(r * 8, r * 8 + 8), slice(c * LANES, (c + 1) * LANES))
            image_grad[at] = own_ref[at] + sum(m[r * across + c] for m in messages)
    image_loss[...] = (loss_ref[...] + sum(m[rows // 8 * across] for m in messages))[:1]


def in_vmem(*arrays):
    return [pltpu.with_memory_space_constraint(x, pltpu.VMEM) for x in arrays]


def vmem(shape):
    return pltpu.VMEM(shape, jnp.float32)


def per_device(sizes, image_emb, text_emb, pairs, log_scale, bias):
    n_img, n_txt = sizes
    chips = n_img // 2
    rows, cols, width = image_emb.shape[0], text_emb.shape[0], image_emb.shape[1]
    count = n_txt * rows
    tiles = rows * width // (8 * LANES)
    smem, whole = pl.BlockSpec(memory_space=pltpu.SMEM), pl.BlockSpec(memory_space=pltpu.VMEM)

    both = jnp.concatenate([text_emb, exchange(text_emb, "img", n_img, 1)])
    image_blocks = [image_emb] + [None] * (n_txt - 1)
    for k in (2, 3):
        image_blocks[k] = exchange(image_emb, "txt", n_txt, k)
    beside = chip_exchange(both, n_img, (1, 2))
    diagonal = chip_exchange(text_emb, n_img, (3, 3))
    image_blocks[1] = exchange(after(image_emb, both), "txt", n_txt, 1)
    sent = jnp.concatenate([beside, diagonal])
    got = exchange(sent, "img", n_img, 1)
    numbers = jnp.pad(after(pairs, sent).astype(jnp.float32)[None], ((0, 7), (0, width - count)))
    bundle = jnp.concatenate([image_blocks[k] for k in IMAGE_ORDER] + [numbers])

    own, loss_tile, d_near, *messages = pl.pallas_call(
        functools.partial(image_kernel, n_img, n_txt, rows, cols),
        out_shape=[vmem((rows, width)), vmem((8, LANES)), vmem((chips * cols, count))]
        + [vmem((tiles + 1, 8, LANES))] * (n_txt - 1),
        in_specs=[smem] * 2 + [whole] * 4,
        out_specs=[whole] * (2 + n_txt),
        name="image_terms",
    )(log_scale, bias, *in_vmem(bundle, both, sent, got))
    messages = [exchange(messages[p - 1], "txt", n_txt, IMAGE_ORDER[p]) for p in (3, 2, 1)]

    pair = exchange(bundle, "img", n_img, 1)
    blocks = pl.pallas_call(
        functools.partial(text_kernel, n_img, n_txt, rows, cols),
        out_shape=[vmem((cols, width))] * chips,
        in_specs=[smem] * 2 + [whole] * 6,
        out_specs=[whole] * chips,
        name="text_terms",
    )(log_scale, bias, *in_vmem(bundle, pair, both, sent, got, d_near))
    blocks = list(blocks)
    for k, distances in ((3, (3, 3)), (1, (1, 2)), (2, (2, 1))):
        blocks[k] = chip_exchange(blocks[k], n_img, distances)

    image_loss, image_grad, text_grad = pl.pallas_call(
        functools.partial(sum_kernel, n_txt, chips),
        out_shape=[
            jax.ShapeDtypeStruct(shape, jnp.float32)
            for shape in ((1, LANES), image_emb.shape, text_emb.shape)
        ],
        in_specs=[whole] * (1 + n_txt + chips),
        out_specs=[whole] * 3,
        name="sums",
    )(*in_vmem(own, loss_tile, *messages, blocks[3], *blocks[:3]))
    return (image_loss.reshape(count), image_grad, text_grad)


def per_device_large(image_emb, text_emb, pairs, log_scale, bias):
    images = lax.all_gather(image_emb, "txt", axis=0, tiled=True)
    texts = lax.all_gather(text_emb, "img", axis=0, tiled=True)
    scale = jnp.exp(log_scale[0])
    shift = bias[0]
    text_count = texts.shape[0]
    dots = lax.dot_general(
        images,
        texts,
        (((1,), (1,)), ((), ())),
        precision=lax.Precision.HIGHEST,
        preferred_element_type=jnp.float32,
    )
    logits = scale * dots + shift
    columns = lax.axis_index("txt") * text_count + jnp.arange(text_count, dtype=jnp.int32)
    sign = jnp.where(pairs[:, None] == columns[None, :], 1.0, -1.0).astype(jnp.float32)
    loss_part = jnp.sum(jax.nn.softplus(-sign * logits), axis=1)
    image_loss = lax.psum(loss_part, "txt")
    dlogits = -sign * jax.nn.sigmoid(-sign * logits)
    image_term = scale * jnp.dot(
        dlogits, texts, precision=lax.Precision.HIGHEST, preferred_element_type=jnp.float32
    )
    image_grad = lax.psum_scatter(image_term, "txt", scatter_dimension=0, tiled=True)
    text_term = scale * lax.dot_general(
        dlogits,
        images,
        (((0,), (0,)), ((), ())),
        precision=lax.Precision.HIGHEST,
        preferred_element_type=jnp.float32,
    )
    text_grad = lax.psum_scatter(text_term, "img", scatter_dimension=0, tiled=True)
    return (image_loss, image_grad, text_grad)


def solution(mesh):
    sizes = (mesh.shape["img"], mesh.shape["txt"])

    def body(image_emb, *others):
        rows = image_emb.shape[0]
        if sizes == (8, 4) and rows * sizes[1] == LANES:
            return per_device(sizes, image_emb, *others)
        return per_device_large(image_emb, *others)

    return jax.shard_map(
        body,
        mesh=mesh,
        in_specs=(P(("img", "txt"), None), P(("txt", "img"), None), P("img"), P(), P()),
        out_specs=(P("img"), P(("img", "txt"), None), P(("txt", "img"), None)),
        check_vma=False,
    )
```

```python
import functools

import jax
import jax.numpy as jnp
from jax import lax
from jax.experimental import pallas as pl
from jax.experimental.pallas import tpu as pltpu
from jax.sharding import PartitionSpec as P

LANES = 128

IMAGE_ORDER = (0, 2, 3, 1)


def exchange(x, axis, n, k):
    return lax.ppermute(x, axis, [(i, i ^ k) for i in range(n)])


def after(x, other):
    return lax.optimization_barrier((x, other))[0]


def chip_exchange(x, n_img, distances):
    return lax.ppermute(x, "img", [(i, i ^ (2 * distances[i % 2])) for i in range(n_img)])


def halves(x):
    high = x.astype(jnp.bfloat16)
    return high, (x - high.astype(jnp.float32)).astype(jnp.bfloat16)


def dot(a, b, contract):
    def part(x, y):
        dims = ((contract[:1], contract[1:]), ((), ()))
        return lax.dot_general(x, y, dims, preferred_element_type=jnp.float32)

    return part(a[0], b[0]) + (part(a[0], b[1]) + part(a[1], b[0]))


def untwist(row, block, me):
    lane = lax.broadcasted_iota(jnp.int32, row.shape, 1)
    step = block
    while step < LANES:
        up, down = pltpu.roll(row, LANES - step, 1), pltpu.roll(row, step, 1)
        flipped = jnp.where((lane // step) % 2 == 0, up, down)
        row = jnp.where((me // (step // block)) % 2 == 1, flipped, row)
        step *= 2
    return row


def shuffle(row, block, sources):
    place = lax.broadcasted_iota(jnp.int32, row.shape, 1) // block
    result = row
    for step in range(1, len(sources)):
        moved = pltpu.roll(row, LANES - step * block, 1)
        for p, source in enumerate(sources):
            if (source - p) % len(sources) == step:
                result = jnp.where(place == p, moved, result)
    return result


def text_ids(shape, n_img, cols, far):
    me_img, me_txt = lax.axis_index("img"), lax.axis_index("txt")
    place = lax.broadcasted_iota(jnp.int32, shape, 0)
    half = n_img // 2 * cols
    me_core = me_img % 2
    core = me_core
    if far:
        core = core ^ (place // half)
        place = place % half
    turn = place // cols
    distance = jnp.where(turn == 1, 1 + me_core, jnp.where(turn == 2, 2 - me_core, turn))
    chip = (me_img // 2) ^ distance
    return (me_txt * n_img + 2 * chip + core) * cols + place % cols


def own_core_texts(cols, both, sent, got):
    return [both[:cols], sent[:cols], got[cols:2 * cols], sent[2 * cols:]]


def other_core_texts(cols, both, sent, got):
    return [both[cols:], sent[cols:2 * cols], got[:cols], got[2 * cols:]]


def derivative(texts, images, ids, matched, log_scale, bias):
    scale = jnp.exp(jnp.full((1, LANES), log_scale[0], jnp.float32))
    logits = scale * dot(texts, images, (1, 1)) + bias[0]
    match = ids == matched
    v = jnp.where(match, -logits, logits)
    e = jnp.exp(-jnp.abs(v))
    loss = jnp.maximum(v, 0.0) + jnp.log1p(e)
    s = scale * jnp.where(v >= 0, 1.0, e) / (1.0 + e)
    return loss, jnp.where(match, -s, s)


def matched_texts(bundle, rows, count):
    matched = untwist(bundle[count:count + 1, :LANES], rows, lax.axis_index("txt"))
    return shuffle(matched, rows, IMAGE_ORDER).astype(jnp.int32)


def image_kernel(
    n_img, n_txt, rows, cols, log_scale, bias, bundle, both, sent, got,
    own, loss_ref, d_near, *messages
):
    count = n_txt * rows
    matched = matched_texts(bundle, rows, count)
    images = halves(bundle[:count])
    near = own_core_texts(cols, both, sent, got)
    texts = halves(jnp.concatenate(near + other_core_texts(cols, both, sent, got)))
    ids = text_ids((texts[0].shape[0], count), n_img, cols, True)
    loss, d = derivative(texts, images, ids, matched, log_scale, bias)
    d_near[...] = d[:len(near) * cols]
    term = dot(halves(d), texts, (0, 0))
    own[...] = term[:rows]
    back = [IMAGE_ORDER.index(k) for k in range(n_txt)]
    loss_row = shuffle(jnp.sum(loss, axis=0, keepdims=True), rows, back)
    loss_row = untwist(loss_row, rows, lax.axis_index("txt"))
    loss_tile = jnp.broadcast_to(loss_row, (8, LANES))
    loss_ref[...] = loss_tile
    across = term.shape[1] // LANES
    for p, ref in enumerate(messages, 1):
        for r in range(rows // 8):
            for c in range(across):
                ref[r * across + c] = term[
                    p * rows + r * 8:p * rows + r * 8 + 8, c * LANES:(c + 1) * LANES
                ]
        ref[rows // 8 * across] = loss_tile


def text_kernel(n_img, n_txt, rows, cols, *refs):
    log_scale, bias, bundle, pair, both, sent, got, d_ref = refs[:8]
    block_refs = refs[8:]
    count = n_txt * rows
    matched = matched_texts(pair, rows, count)
    others = halves(pair[:count])
    texts = halves(jnp.concatenate(own_core_texts(cols, both, sent, got)))
    ids = text_ids((texts[0].shape[0], count), n_img, cols, False)
    _, d = derivative(texts, others, ids, matched, log_scale, bias)
    term = dot(halves(d_ref[...]), halves(bundle[:count]), (1, 0)) + dot(halves(d), others, (1, 0))
    for k, ref in enumerate(block_refs):
        ref[...] = term[k * cols:(k + 1) * cols]


def sum_kernel(n_txt, n_chips, own_ref, loss_ref, *refs):
    messages, blocks = refs[:n_txt - 1], refs[n_txt - 1:n_txt - 1 + n_chips]
    image_loss, image_grad, text_grad = refs[n_txt - 1 + n_chips:]
    text_grad[...] = sum(b[...] for b in blocks)
    rows, width = own_ref.shape
    across = width // LANES
    for r in range(rows // 8):
        for c in range(across):
            at = (slice(r * 8, r * 8 + 8), slice(c * LANES, (c + 1) * LANES))
            image_grad[at] = own_ref[at] + sum(m[r * across + c] for m in messages)
    image_loss[...] = (loss_ref[...] + sum(m[rows // 8 * across] for m in messages))[:1]


def in_vmem(*arrays):
    return [pltpu.with_memory_space_constraint(x, pltpu.VMEM) for x in arrays]


def vmem(shape):
    return pltpu.VMEM(shape, jnp.float32)


def per_device(sizes, image_emb, text_emb, pairs, log_scale, bias):
    n_img, n_txt = sizes
    chips = n_img // 2
    rows, cols, width = image_emb.shape[0], text_emb.shape[0], image_emb.shape[1]
    count = n_txt * rows
    tiles = rows * width // (8 * LANES)
    smem, whole = pl.BlockSpec(memory_space=pltpu.SMEM), pl.BlockSpec(memory_space=pltpu.VMEM)

    both = jnp.concatenate([text_emb, exchange(text_emb, "img", n_img, 1)])
    image_blocks = [image_emb] + [None] * (n_txt - 1)
    for k in (2, 3):
        image_blocks[k] = exchange(image_emb, "txt", n_txt, k)
    beside = chip_exchange(both, n_img, (1, 2))
    diagonal = chip_exchange(text_emb, n_img, (3, 3))
    image_blocks[1] = exchange(after(image_emb, both), "txt", n_txt, 1)
    sent = jnp.concatenate([beside, diagonal])
    got = exchange(sent, "img", n_img, 1)
    numbers = jnp.pad(pairs.astype(jnp.float32)[None], ((0, 7), (0, width - count)))
    bundle = jnp.concatenate([image_blocks[k] for k in IMAGE_ORDER] + [numbers])

    own, loss_tile, d_near, *messages = pl.pallas_call(
        functools.partial(image_kernel, n_img, n_txt, rows, cols),
        out_shape=[vmem((rows, width)), vmem((8, LANES)), vmem((chips * cols, count))]
        + [vmem((tiles + 1, 8, LANES))] * (n_txt - 1),
        in_specs=[smem] * 2 + [whole] * 4,
        out_specs=[whole] * (2 + n_txt),
        name="image_terms",
    )(log_scale, bias, *in_vmem(bundle, both, sent, got))
    messages = [exchange(messages[p - 1], "txt", n_txt, IMAGE_ORDER[p]) for p in (3, 2, 1)]

    pair = exchange(after(bundle, own), "img", n_img, 1)
    blocks = pl.pallas_call(
        functools.partial(text_kernel, n_img, n_txt, rows, cols),
        out_shape=[vmem((cols, width))] * chips,
        in_specs=[smem] * 2 + [whole] * 6,
        out_specs=[whole] * chips,
        name="text_terms",
    )(log_scale, bias, *in_vmem(bundle, pair, both, sent, got, d_near))
    blocks = list(blocks)
    for k, distances in ((3, (3, 3)), (1, (1, 2)), (2, (2, 1))):
        blocks[k] = chip_exchange(blocks[k], n_img, distances)

    image_loss, image_grad, text_grad = pl.pallas_call(
        functools.partial(sum_kernel, n_txt, chips),
        out_shape=[
            jax.ShapeDtypeStruct(shape, jnp.float32)
            for shape in ((1, LANES), image_emb.shape, text_emb.shape)
        ],
        in_specs=[whole] * (1 + n_txt + chips),
        out_specs=[whole] * 3,
        name="sums",
    )(*in_vmem(own, loss_tile, *messages, blocks[3], *blocks[:3]))
    return (image_loss.reshape(count), image_grad, text_grad)


def per_device_large(image_emb, text_emb, pairs, log_scale, bias):
    images = lax.all_gather(image_emb, "txt", axis=0, tiled=True)
    texts = lax.all_gather(text_emb, "img", axis=0, tiled=True)
    scale = jnp.exp(log_scale[0])
    shift = bias[0]
    text_count = texts.shape[0]
    dots = lax.dot_general(
        images,
        texts,
        (((1,), (1,)), ((), ())),
        precision=lax.Precision.HIGHEST,
        preferred_element_type=jnp.float32,
    )
    logits = scale * dots + shift
    columns = lax.axis_index("txt") * text_count + jnp.arange(text_count, dtype=jnp.int32)
    sign = jnp.where(pairs[:, None] == columns[None, :], 1.0, -1.0).astype(jnp.float32)
    loss_part = jnp.sum(jax.nn.softplus(-sign * logits), axis=1)
    image_loss = lax.psum(loss_part, "txt")
    dlogits = -sign * jax.nn.sigmoid(-sign * logits)
    image_term = scale * jnp.dot(
        dlogits, texts, precision=lax.Precision.HIGHEST, preferred_element_type=jnp.float32
    )
    image_grad = lax.psum_scatter(image_term, "txt", scatter_dimension=0, tiled=True)
    text_term = scale * lax.dot_general(
        dlogits,
        images,
        (((0,), (0,)), ((), ())),
        precision=lax.Precision.HIGHEST,
        preferred_element_type=jnp.float32,
    )
    text_grad = lax.psum_scatter(text_term, "img", scatter_dimension=0, tiled=True)
    return (image_loss, image_grad, text_grad)


def solution(mesh):
    sizes = (mesh.shape["img"], mesh.shape["txt"])

    def body(image_emb, *others):
        rows = image_emb.shape[0]
        if sizes == (8, 4) and rows * sizes[1] == LANES:
            return per_device(sizes, image_emb, *others)
        return per_device_large(image_emb, *others)

    return jax.shard_map(
        body,
        mesh=mesh,
        in_specs=(P(("img", "txt"), None), P(("txt", "img"), None), P("img"), P(), P()),
        out_specs=(P("img"), P(("img", "txt"), None), P(("txt", "img"), None)),
        check_vma=False,
    )
```

```python
import functools

import jax
import jax.numpy as jnp
from jax import lax
from jax.experimental import pallas as pl
from jax.experimental.pallas import tpu as pltpu
from jax.sharding import PartitionSpec as P

LANES = 128

IMAGE_ORDER = (0, 2, 3, 1)


def exchange(x, axis, n, k):
    return lax.ppermute(x, axis, [(i, i ^ k) for i in range(n)])


def after(x, other):
    return lax.optimization_barrier((x, other))[0]


def chip_exchange(x, n_img, distances):
    return lax.ppermute(x, "img", [(i, i ^ (2 * distances[i % 2])) for i in range(n_img)])


def halves(x):
    high = x.astype(jnp.bfloat16)
    return high, (x - high.astype(jnp.float32)).astype(jnp.bfloat16)


def dot(a, b, contract):
    def part(x, y):
        dims = ((contract[:1], contract[1:]), ((), ()))
        return lax.dot_general(x, y, dims, preferred_element_type=jnp.float32)

    return part(a[0], b[0]) + (part(a[0], b[1]) + part(a[1], b[0]))


def untwist(row, block, me):
    lane = lax.broadcasted_iota(jnp.int32, row.shape, 1)
    step = block
    while step < LANES:
        up, down = pltpu.roll(row, LANES - step, 1), pltpu.roll(row, step, 1)
        flipped = jnp.where((lane // step) % 2 == 0, up, down)
        row = jnp.where((me // (step // block)) % 2 == 1, flipped, row)
        step *= 2
    return row


def shuffle(row, block, sources):
    place = lax.broadcasted_iota(jnp.int32, row.shape, 1) // block
    result = row
    for step in range(1, len(sources)):
        moved = pltpu.roll(row, LANES - step * block, 1)
        for p, source in enumerate(sources):
            if (source - p) % len(sources) == step:
                result = jnp.where(place == p, moved, result)
    return result


def text_ids(shape, n_img, cols, far):
    me_img, me_txt = lax.axis_index("img"), lax.axis_index("txt")
    place = lax.broadcasted_iota(jnp.int32, shape, 0)
    half = n_img // 2 * cols
    me_core = me_img % 2
    core = me_core
    if far:
        core = core ^ (place // half)
        place = place % half
    turn = place // cols
    distance = jnp.where(turn == 1, 1 + me_core, jnp.where(turn == 2, 2 - me_core, turn))
    chip = (me_img // 2) ^ distance
    return (me_txt * n_img + 2 * chip + core) * cols + place % cols


def own_core_texts(cols, both, sent, got):
    return [both[:cols], sent[:cols], got[cols:2 * cols], sent[2 * cols:]]


def other_core_texts(cols, both, sent, got):
    return [both[cols:], sent[cols:2 * cols], got[:cols], got[2 * cols:]]


def derivative(texts, images, ids, matched, log_scale, bias):
    scale = jnp.exp(jnp.full((1, LANES), log_scale[0], jnp.float32))
    logits = scale * dot(texts, images, (1, 1)) + bias[0]
    match = ids == matched
    v = jnp.where(match, -logits, logits)
    e = jnp.exp(-jnp.abs(v))
    loss = jnp.maximum(v, 0.0) + jnp.log1p(e)
    s = scale * jnp.where(v >= 0, 1.0, e) / (1.0 + e)
    return loss, jnp.where(match, -s, s)


def matched_texts(bundle, rows, count):
    matched = untwist(bundle[count:count + 1, :LANES], rows, lax.axis_index("txt"))
    return shuffle(matched, rows, IMAGE_ORDER).astype(jnp.int32)


def image_kernel(
    n_img, n_txt, rows, cols, log_scale, bias, bundle, both, sent, got,
    own, loss_ref, d_near, *messages
):
    count = n_txt * rows
    matched = matched_texts(bundle, rows, count)
    images = halves(bundle[:count])
    near = own_core_texts(cols, both, sent, got)
    texts = halves(jnp.concatenate(near + other_core_texts(cols, both, sent, got)))
    ids = text_ids((texts[0].shape[0], count), n_img, cols, True)
    loss, d = derivative(texts, images, ids, matched, log_scale, bias)
    d_near[...] = d[:len(near) * cols]
    term = dot(halves(d), texts, (0, 0))
    own[...] = term[:rows]
    back = [IMAGE_ORDER.index(k) for k in range(n_txt)]
    loss_row = shuffle(jnp.sum(loss, axis=0, keepdims=True), rows, back)
    loss_row = untwist(loss_row, rows, lax.axis_index("txt"))
    loss_tile = jnp.broadcast_to(loss_row, (8, LANES))
    loss_ref[...] = loss_tile
    across = term.shape[1] // LANES
    for p, ref in enumerate(messages, 1):
        for r in range(rows // 8):
            for c in range(across):
                ref[r * across + c] = term[
                    p * rows + r * 8:p * rows + r * 8 + 8, c * LANES:(c + 1) * LANES
                ]
        ref[rows // 8 * across] = loss_tile


def text_kernel(n_img, n_txt, rows, cols, *refs):
    log_scale, bias, bundle, pair, both, sent, got, d_ref = refs[:8]
    block_refs = refs[8:]
    count = n_txt * rows
    matched = matched_texts(pair, rows, count)
    others = halves(pair[:count])
    texts = halves(jnp.concatenate(own_core_texts(cols, both, sent, got)))
    ids = text_ids((texts[0].shape[0], count), n_img, cols, False)
    _, d = derivative(texts, others, ids, matched, log_scale, bias)
    term = dot(halves(d_ref[...]), halves(bundle[:count]), (1, 0)) + dot(halves(d), others, (1, 0))
    for k, ref in enumerate(block_refs):
        ref[...] = term[k * cols:(k + 1) * cols]


def sum_kernel(n_txt, n_chips, own_ref, loss_ref, *refs):
    messages, blocks = refs[:n_txt - 1], refs[n_txt - 1:n_txt - 1 + n_chips]
    image_loss, image_grad, text_grad = refs[n_txt - 1 + n_chips:]
    text_grad[...] = sum(b[...] for b in blocks)
    rows, width = own_ref.shape
    across = width // LANES
    for r in range(rows // 8):
        for c in range(across):
            at = (slice(r * 8, r * 8 + 8), slice(c * LANES, (c + 1) * LANES))
            image_grad[at] = own_ref[at] + sum(m[r * across + c] for m in messages)
    image_loss[...] = (loss_ref[...] + sum(m[rows // 8 * across] for m in messages))[:1]


def in_vmem(*arrays):
    return [pltpu.with_memory_space_constraint(x, pltpu.VMEM) for x in arrays]


def vmem(shape):
    return pltpu.VMEM(shape, jnp.float32)


def per_device(sizes, image_emb, text_emb, pairs, log_scale, bias):
    n_img, n_txt = sizes
    chips = n_img // 2
    rows, cols, width = image_emb.shape[0], text_emb.shape[0], image_emb.shape[1]
    count = n_txt * rows
    tiles = rows * width // (8 * LANES)
    smem, whole = pl.BlockSpec(memory_space=pltpu.SMEM), pl.BlockSpec(memory_space=pltpu.VMEM)

    both = jnp.concatenate([text_emb, exchange(text_emb, "img", n_img, 1)])
    image_blocks = [image_emb] + [None] * (n_txt - 1)
    for k in (2, 3):
        image_blocks[k] = exchange(image_emb, "txt", n_txt, k)
    beside = chip_exchange(both, n_img, (1, 2))
    diagonal = chip_exchange(text_emb, n_img, (3, 3))
    image_blocks[1] = exchange(after(image_emb, both), "txt", n_txt, 1)
    sent = jnp.concatenate([beside, diagonal])
    got = exchange(sent, "img", n_img, 1)
    numbers = jnp.pad(pairs.astype(jnp.float32)[None], ((0, 7), (0, width - count)))
    bundle = jnp.concatenate([image_blocks[k] for k in IMAGE_ORDER] + [numbers])

    own, loss_tile, d_near, *messages = pl.pallas_call(
        functools.partial(image_kernel, n_img, n_txt, rows, cols),
        out_shape=[vmem((rows, width)), vmem((8, LANES)), vmem((chips * cols, count))]
        + [vmem((tiles + 1, 8, LANES))] * (n_txt - 1),
        in_specs=[smem] * 2 + [whole] * 4,
        out_specs=[whole] * (2 + n_txt),
        name="image_terms",
    )(log_scale, bias, *in_vmem(bundle, both, sent, got))
    messages = [exchange(messages[p - 1], "txt", n_txt, IMAGE_ORDER[p]) for p in (3, 2, 1)]

    pair = exchange(bundle, "img", n_img, 1)
    blocks = pl.pallas_call(
        functools.partial(text_kernel, n_img, n_txt, rows, cols),
        out_shape=[vmem((cols, width))] * chips,
        in_specs=[smem] * 2 + [whole] * 6,
        out_specs=[whole] * chips,
        name="text_terms",
    )(log_scale, bias, *in_vmem(bundle, pair, both, sent, got, d_near))
    blocks = list(blocks)
    for k, distances in ((3, (3, 3)), (1, (1, 2)), (2, (2, 1))):
        blocks[k] = chip_exchange(blocks[k], n_img, distances)

    image_loss, image_grad, text_grad = pl.pallas_call(
        functools.partial(sum_kernel, n_txt, chips),
        out_shape=[
            jax.ShapeDtypeStruct(shape, jnp.float32)
            for shape in ((1, LANES), image_emb.shape, text_emb.shape)
        ],
        in_specs=[whole] * (1 + n_txt + chips),
        out_specs=[whole] * 3,
        name="sums",
    )(*in_vmem(own, loss_tile, *messages, blocks[3], *blocks[:3]))
    return (image_loss.reshape(count), image_grad, text_grad)


def per_device_large(image_emb, text_emb, pairs, log_scale, bias):
    images = lax.all_gather(image_emb, "txt", axis=0, tiled=True)
    texts = lax.all_gather(text_emb, "img", axis=0, tiled=True)
    scale = jnp.exp(log_scale[0])
    shift = bias[0]
    text_count = texts.shape[0]
    dots = lax.dot_general(
        images,
        texts,
        (((1,), (1,)), ((), ())),
        precision=lax.Precision.HIGHEST,
        preferred_element_type=jnp.float32,
    )
    logits = scale * dots + shift
    columns = lax.axis_index("txt") * text_count + jnp.arange(text_count, dtype=jnp.int32)
    sign = jnp.where(pairs[:, None] == columns[None, :], 1.0, -1.0).astype(jnp.float32)
    loss_part = jnp.sum(jax.nn.softplus(-sign * logits), axis=1)
    image_loss = lax.psum(loss_part, "txt")
    dlogits = -sign * jax.nn.sigmoid(-sign * logits)
    image_term = scale * jnp.dot(
        dlogits, texts, precision=lax.Precision.HIGHEST, preferred_element_type=jnp.float32
    )
    image_grad = lax.psum_scatter(image_term, "txt", scatter_dimension=0, tiled=True)
    text_term = scale * lax.dot_general(
        dlogits,
        images,
        (((0,), (0,)), ((), ())),
        precision=lax.Precision.HIGHEST,
        preferred_element_type=jnp.float32,
    )
    text_grad = lax.psum_scatter(text_term, "img", scatter_dimension=0, tiled=True)
    return (image_loss, image_grad, text_grad)


def solution(mesh):
    sizes = (mesh.shape["img"], mesh.shape["txt"])

    def body(image_emb, *others):
        rows = image_emb.shape[0]
        if sizes == (8, 4) and rows * sizes[1] == LANES:
            return per_device(sizes, image_emb, *others)
        return per_device_large(image_emb, *others)

    return jax.shard_map(
        body,
        mesh=mesh,
        in_specs=(P(("img", "txt"), None), P(("txt", "img"), None), P("img"), P(), P()),
        out_specs=(P("img"), P(("img", "txt"), None), P(("txt", "img"), None)),
        check_vma=False,
    )
```

```python
import functools

import jax
import jax.numpy as jnp
from jax import lax
from jax.experimental import pallas as pl
from jax.experimental.pallas import tpu as pltpu
from jax.sharding import PartitionSpec as P

LANES = 128

IMAGE_ORDER = (0, 2, 3, 1)


def exchange(x, axis, n, k):
    return lax.ppermute(x, axis, [(i, i ^ k) for i in range(n)])


def after(x, other):
    return lax.optimization_barrier((x, other))[0]


def chip_exchange(x, n_img, distances):
    return lax.ppermute(x, "img", [(i, i ^ (2 * distances[i % 2])) for i in range(n_img)])


def halves(x):
    high = x.astype(jnp.bfloat16)
    return high, (x - high.astype(jnp.float32)).astype(jnp.bfloat16)


def dot(pairs, contract):
    left = jnp.concatenate([part for a, _ in pairs for part in (a[0], a[0], a[1])], contract[0])
    right = jnp.concatenate([part for _, b in pairs for part in (b[0], b[1], b[0])], contract[1])
    dims = ((contract[:1], contract[1:]), ((), ()))
    return lax.dot_general(left, right, dims, preferred_element_type=jnp.float32)


def untwist(row, block, me):
    lane = lax.broadcasted_iota(jnp.int32, row.shape, 1)
    step = block
    while step < LANES:
        up, down = pltpu.roll(row, LANES - step, 1), pltpu.roll(row, step, 1)
        flipped = jnp.where((lane // step) % 2 == 0, up, down)
        row = jnp.where((me // (step // block)) % 2 == 1, flipped, row)
        step *= 2
    return row


def shuffle(row, block, sources):
    place = lax.broadcasted_iota(jnp.int32, row.shape, 1) // block
    result = row
    for step in range(1, len(sources)):
        moved = pltpu.roll(row, LANES - step * block, 1)
        for p, source in enumerate(sources):
            if (source - p) % len(sources) == step:
                result = jnp.where(place == p, moved, result)
    return result


def text_ids(shape, n_img, cols, far):
    me_img, me_txt = lax.axis_index("img"), lax.axis_index("txt")
    place = lax.broadcasted_iota(jnp.int32, shape, 0)
    half = n_img // 2 * cols
    me_core = me_img % 2
    core = me_core
    if far:
        core = core ^ (place // half)
        place = place % half
    turn = place // cols
    distance = jnp.where(turn == 1, 1 + me_core, jnp.where(turn == 2, 2 - me_core, turn))
    chip = (me_img // 2) ^ distance
    return (me_txt * n_img + 2 * chip + core) * cols + place % cols


def own_core_texts(cols, both, sent, got):
    return [both[:cols], sent[:cols], got[cols:2 * cols], sent[2 * cols:]]


def other_core_texts(cols, both, sent, got):
    return [both[cols:], sent[cols:2 * cols], got[:cols], got[2 * cols:]]


def derivative(texts, images, ids, matched, log_scale, bias):
    scale = jnp.exp(jnp.full((1, LANES), log_scale[0], jnp.float32))
    logits = scale * dot([(texts, images)], (1, 1)) + bias[0]
    match = ids == matched
    v = jnp.where(match, -logits, logits)
    e = jnp.exp(-jnp.abs(v))
    loss = jnp.maximum(v, 0.0) + jnp.log1p(e)
    s = scale * jnp.where(v >= 0, 1.0, e) / (1.0 + e)
    return loss, jnp.where(match, -s, s)


def matched_texts(bundle, rows, count):
    matched = untwist(bundle[count:count + 1, :LANES], rows, lax.axis_index("txt"))
    return shuffle(matched, rows, IMAGE_ORDER).astype(jnp.int32)


def image_kernel(
    n_img, n_txt, rows, cols, log_scale, bias, bundle, both, sent, got,
    own, loss_ref, d_near, *messages
):
    count = n_txt * rows
    matched = matched_texts(bundle, rows, count)
    images = halves(bundle[:count])
    near = own_core_texts(cols, both, sent, got)
    texts = halves(jnp.concatenate(near + other_core_texts(cols, both, sent, got)))
    ids = text_ids((texts[0].shape[0], count), n_img, cols, True)
    loss, d = derivative(texts, images, ids, matched, log_scale, bias)
    d_near[...] = d[:len(near) * cols]
    term = dot([(halves(d), texts)], (0, 0))
    own[...] = term[:rows]
    back = [IMAGE_ORDER.index(k) for k in range(n_txt)]
    loss_row = shuffle(jnp.sum(loss, axis=0, keepdims=True), rows, back)
    loss_row = untwist(loss_row, rows, lax.axis_index("txt"))
    loss_tile = jnp.broadcast_to(loss_row, (8, LANES))
    loss_ref[...] = loss_tile
    across = term.shape[1] // LANES
    for p, ref in enumerate(messages, 1):
        for r in range(rows // 8):
            for c in range(across):
                ref[r * across + c] = term[
                    p * rows + r * 8:p * rows + r * 8 + 8, c * LANES:(c + 1) * LANES
                ]
        ref[rows // 8 * across] = loss_tile


def text_kernel(n_img, n_txt, rows, cols, *refs):
    log_scale, bias, bundle, pair, both, sent, got, d_ref = refs[:8]
    block_refs = refs[8:]
    count = n_txt * rows
    matched = matched_texts(pair, rows, count)
    others = halves(pair[:count])
    texts = halves(jnp.concatenate(own_core_texts(cols, both, sent, got)))
    ids = text_ids((texts[0].shape[0], count), n_img, cols, False)
    _, d = derivative(texts, others, ids, matched, log_scale, bias)
    near = halves(d_ref[...]), halves(bundle[:count])
    term = dot([near, (halves(d), others)], (1, 0))
    for k, ref in enumerate(block_refs):
        ref[...] = term[k * cols:(k + 1) * cols]


def sum_kernel(n_txt, n_chips, own_ref, loss_ref, *refs):
    messages, blocks = refs[:n_txt - 1], refs[n_txt - 1:n_txt - 1 + n_chips]
    image_loss, image_grad, text_grad = refs[n_txt - 1 + n_chips:]
    text_grad[...] = sum(b[...] for b in blocks)
    rows, width = own_ref.shape
    across = width // LANES
    for r in range(rows // 8):
        for c in range(across):
            at = (slice(r * 8, r * 8 + 8), slice(c * LANES, (c + 1) * LANES))
            image_grad[at] = own_ref[at] + sum(m[r * across + c] for m in messages)
    image_loss[...] = (loss_ref[...] + sum(m[rows // 8 * across] for m in messages))[:1]


def in_vmem(*arrays):
    return [pltpu.with_memory_space_constraint(x, pltpu.VMEM) for x in arrays]


def vmem(shape):
    return pltpu.VMEM(shape, jnp.float32)


def per_device(sizes, image_emb, text_emb, pairs, log_scale, bias):
    n_img, n_txt = sizes
    chips = n_img // 2
    rows, cols, width = image_emb.shape[0], text_emb.shape[0], image_emb.shape[1]
    count = n_txt * rows
    tiles = rows * width // (8 * LANES)
    smem, whole = pl.BlockSpec(memory_space=pltpu.SMEM), pl.BlockSpec(memory_space=pltpu.VMEM)

    both = jnp.concatenate([text_emb, exchange(text_emb, "img", n_img, 1)])
    image_blocks = [image_emb] + [None] * (n_txt - 1)
    for k in (2, 3):
        image_blocks[k] = exchange(image_emb, "txt", n_txt, k)
    beside = chip_exchange(both, n_img, (1, 2))
    diagonal = chip_exchange(text_emb, n_img, (3, 3))
    image_blocks[1] = exchange(after(image_emb, both), "txt", n_txt, 1)
    sent = jnp.concatenate([beside, diagonal])
    got = exchange(sent, "img", n_img, 1)
    numbers = jnp.pad(pairs.astype(jnp.float32)[None], ((0, 7), (0, width - count)))
    bundle = jnp.concatenate([image_blocks[k] for k in IMAGE_ORDER] + [numbers])

    own, loss_tile, d_near, *messages = pl.pallas_call(
        functools.partial(image_kernel, n_img, n_txt, rows, cols),
        out_shape=[vmem((rows, width)), vmem((8, LANES)), vmem((chips * cols, count))]
        + [vmem((tiles + 1, 8, LANES))] * (n_txt - 1),
        in_specs=[smem] * 2 + [whole] * 4,
        out_specs=[whole] * (2 + n_txt),
        name="image_terms",
    )(log_scale, bias, *in_vmem(bundle, both, sent, got))
    messages = [exchange(messages[p - 1], "txt", n_txt, IMAGE_ORDER[p]) for p in (3, 2, 1)]

    pair = exchange(bundle, "img", n_img, 1)
    blocks = pl.pallas_call(
        functools.partial(text_kernel, n_img, n_txt, rows, cols),
        out_shape=[vmem((cols, width))] * chips,
        in_specs=[smem] * 2 + [whole] * 6,
        out_specs=[whole] * chips,
        name="text_terms",
    )(log_scale, bias, *in_vmem(bundle, pair, both, sent, got, d_near))
    blocks = list(blocks)
    for k, distances in ((3, (3, 3)), (1, (1, 2)), (2, (2, 1))):
        blocks[k] = chip_exchange(blocks[k], n_img, distances)

    image_loss, image_grad, text_grad = pl.pallas_call(
        functools.partial(sum_kernel, n_txt, chips),
        out_shape=[
            jax.ShapeDtypeStruct(shape, jnp.float32)
            for shape in ((1, LANES), image_emb.shape, text_emb.shape)
        ],
        in_specs=[whole] * (1 + n_txt + chips),
        out_specs=[whole] * 3,
        name="sums",
    )(*in_vmem(own, loss_tile, *messages, blocks[3], *blocks[:3]))
    return (image_loss.reshape(count), image_grad, text_grad)


def per_device_large(image_emb, text_emb, pairs, log_scale, bias):
    images = lax.all_gather(image_emb, "txt", axis=0, tiled=True)
    texts = lax.all_gather(text_emb, "img", axis=0, tiled=True)
    scale = jnp.exp(log_scale[0])
    shift = bias[0]
    text_count = texts.shape[0]
    dots = lax.dot_general(
        images,
        texts,
        (((1,), (1,)), ((), ())),
        precision=lax.Precision.HIGHEST,
        preferred_element_type=jnp.float32,
    )
    logits = scale * dots + shift
    columns = lax.axis_index("txt") * text_count + jnp.arange(text_count, dtype=jnp.int32)
    sign = jnp.where(pairs[:, None] == columns[None, :], 1.0, -1.0).astype(jnp.float32)
    loss_part = jnp.sum(jax.nn.softplus(-sign * logits), axis=1)
    image_loss = lax.psum(loss_part, "txt")
    dlogits = -sign * jax.nn.sigmoid(-sign * logits)
    image_term = scale * jnp.dot(
        dlogits, texts, precision=lax.Precision.HIGHEST, preferred_element_type=jnp.float32
    )
    image_grad = lax.psum_scatter(image_term, "txt", scatter_dimension=0, tiled=True)
    text_term = scale * lax.dot_general(
        dlogits,
        images,
        (((0,), (0,)), ((), ())),
        precision=lax.Precision.HIGHEST,
        preferred_element_type=jnp.float32,
    )
    text_grad = lax.psum_scatter(text_term, "img", scatter_dimension=0, tiled=True)
    return (image_loss, image_grad, text_grad)


def solution(mesh):
    sizes = (mesh.shape["img"], mesh.shape["txt"])

    def body(image_emb, *others):
        rows = image_emb.shape[0]
        if sizes == (8, 4) and rows * sizes[1] == LANES:
            return per_device(sizes, image_emb, *others)
        return per_device_large(image_emb, *others)

    return jax.shard_map(
        body,
        mesh=mesh,
        in_specs=(P(("img", "txt"), None), P(("txt", "img"), None), P("img"), P(), P()),
        out_specs=(P("img"), P(("img", "txt"), None), P(("txt", "img"), None)),
        check_vma=False,
    )
```

```python
import functools

import jax
import jax.numpy as jnp
from jax import lax
from jax.experimental import pallas as pl
from jax.experimental.pallas import tpu as pltpu
from jax.sharding import PartitionSpec as P

LANES = 128

IMAGE_ORDER = (0, 2, 3, 1)


def exchange(x, axis, n, k):
    return lax.ppermute(x, axis, [(i, i ^ k) for i in range(n)])


def after(x, other):
    return lax.optimization_barrier((x, other))[0]


def chip_exchange(x, n_img, distances):
    return lax.ppermute(x, "img", [(i, i ^ (2 * distances[i % 2])) for i in range(n_img)])


def halves(x):
    high = x.astype(jnp.bfloat16)
    return high, (x - high.astype(jnp.float32)).astype(jnp.bfloat16)


def dot(pairs, contract):
    left = jnp.concatenate([part for a, _ in pairs for part in (a[0], a[0], a[1])], contract[0])
    right = jnp.concatenate([part for _, b in pairs for part in (b[0], b[1], b[0])], contract[1])
    dims = ((contract[:1], contract[1:]), ((), ()))
    return lax.dot_general(left, right, dims, preferred_element_type=jnp.float32)


def untwist(row, block, me):
    lane = lax.broadcasted_iota(jnp.int32, row.shape, 1)
    step = block
    while step < LANES:
        up, down = pltpu.roll(row, LANES - step, 1), pltpu.roll(row, step, 1)
        flipped = jnp.where((lane // step) % 2 == 0, up, down)
        row = jnp.where((me // (step // block)) % 2 == 1, flipped, row)
        step *= 2
    return row


def shuffle(row, block, sources):
    place = lax.broadcasted_iota(jnp.int32, row.shape, 1) // block
    result = row
    for step in range(1, len(sources)):
        moved = pltpu.roll(row, LANES - step * block, 1)
        for p, source in enumerate(sources):
            if (source - p) % len(sources) == step:
                result = jnp.where(place == p, moved, result)
    return result


def text_ids(shape, n_img, cols, far):
    me_img, me_txt = lax.axis_index("img"), lax.axis_index("txt")
    place = lax.broadcasted_iota(jnp.int32, shape, 0)
    half = n_img // 2 * cols
    me_core = me_img % 2
    core = me_core
    if far:
        core = core ^ (place // half)
        place = place % half
    turn = place // cols
    distance = jnp.where(turn == 1, 1 + me_core, jnp.where(turn == 2, 2 - me_core, turn))
    chip = (me_img // 2) ^ distance
    return (me_txt * n_img + 2 * chip + core) * cols + place % cols


def own_core_texts(cols, both, sent, got):
    return [both[:cols], sent[:cols], got[cols:2 * cols], sent[2 * cols:]]


def other_core_texts(cols, both, sent, got):
    return [both[cols:], sent[cols:2 * cols], got[:cols], got[2 * cols:]]


def derivative(texts, images, ids, matched, scalars):
    scale = jnp.exp(scalars[0:1])
    logits = scale * dot([(texts, images)], (1, 1)) + scalars[1:2]
    match = ids == matched
    v = jnp.where(match, -logits, logits)
    e = jnp.exp(-jnp.abs(v))
    loss = jnp.maximum(v, 0.0) + jnp.log1p(e)
    s = scale * jnp.where(v >= 0, 1.0, e) / (1.0 + e)
    return loss, jnp.where(match, -s, s)


def matched_texts(bundle, rows, count):
    matched = untwist(bundle[count:count + 1, :LANES], rows, lax.axis_index("txt"))
    return shuffle(matched, rows, IMAGE_ORDER).astype(jnp.int32)


def image_kernel(
    n_img, n_txt, rows, cols, scalars, bundle, both, sent, got,
    own, loss_ref, d_near, *messages
):
    count = n_txt * rows
    matched = matched_texts(bundle, rows, count)
    images = halves(bundle[:count])
    near = own_core_texts(cols, both, sent, got)
    texts = halves(jnp.concatenate(near + other_core_texts(cols, both, sent, got)))
    ids = text_ids((texts[0].shape[0], count), n_img, cols, True)
    loss, d = derivative(texts, images, ids, matched, scalars)
    d_near[...] = d[:len(near) * cols]
    term = dot([(halves(d), texts)], (0, 0))
    own[...] = term[:rows]
    back = [IMAGE_ORDER.index(k) for k in range(n_txt)]
    loss_row = shuffle(jnp.sum(loss, axis=0, keepdims=True), rows, back)
    loss_row = untwist(loss_row, rows, lax.axis_index("txt"))
    loss_tile = jnp.broadcast_to(loss_row, (8, LANES))
    loss_ref[...] = loss_tile
    across = term.shape[1] // LANES
    for p, ref in enumerate(messages, 1):
        for r in range(rows // 8):
            for c in range(across):
                ref[r * across + c] = term[
                    p * rows + r * 8:p * rows + r * 8 + 8, c * LANES:(c + 1) * LANES
                ]
        ref[rows // 8 * across] = loss_tile


def text_kernel(n_img, n_txt, rows, cols, *refs):
    scalars, bundle, pair, both, sent, got, d_ref = refs[:7]
    block_refs = refs[7:]
    count = n_txt * rows
    matched = matched_texts(pair, rows, count)
    others = halves(pair[:count])
    texts = halves(jnp.concatenate(own_core_texts(cols, both, sent, got)))
    ids = text_ids((texts[0].shape[0], count), n_img, cols, False)
    _, d = derivative(texts, others, ids, matched, scalars)
    near = halves(d_ref[...]), halves(bundle[:count])
    term = dot([near, (halves(d), others)], (1, 0))
    for k, ref in enumerate(block_refs):
        ref[...] = term[k * cols:(k + 1) * cols]


def sum_kernel(n_txt, n_chips, own_ref, loss_ref, *refs):
    messages, blocks = refs[:n_txt - 1], refs[n_txt - 1:n_txt - 1 + n_chips]
    image_loss, image_grad, text_grad = refs[n_txt - 1 + n_chips:]
    text_grad[...] = sum(b[...] for b in blocks)
    rows, width = own_ref.shape
    across = width // LANES
    for r in range(rows // 8):
        for c in range(across):
            at = (slice(r * 8, r * 8 + 8), slice(c * LANES, (c + 1) * LANES))
            image_grad[at] = own_ref[at] + sum(m[r * across + c] for m in messages)
    image_loss[...] = (loss_ref[...] + sum(m[rows // 8 * across] for m in messages))[:1]


def in_vmem(*arrays):
    return [pltpu.with_memory_space_constraint(x, pltpu.VMEM) for x in arrays]


def vmem(shape):
    return pltpu.VMEM(shape, jnp.float32)


def per_device(sizes, image_emb, text_emb, pairs, log_scale, bias):
    n_img, n_txt = sizes
    chips = n_img // 2
    rows, cols, width = image_emb.shape[0], text_emb.shape[0], image_emb.shape[1]
    count = n_txt * rows
    tiles = rows * width // (8 * LANES)
    whole = pl.BlockSpec(memory_space=pltpu.VMEM)

    both = jnp.concatenate([text_emb, exchange(text_emb, "img", n_img, 1)])
    image_blocks = [image_emb] + [None] * (n_txt - 1)
    for k in (2, 3):
        image_blocks[k] = exchange(image_emb, "txt", n_txt, k)
    beside = chip_exchange(both, n_img, (1, 2))
    diagonal = chip_exchange(text_emb, n_img, (3, 3))
    image_blocks[1] = exchange(after(image_emb, both), "txt", n_txt, 1)
    sent = jnp.concatenate([beside, diagonal])
    scalars = jnp.stack([jnp.broadcast_to(log_scale, LANES), jnp.broadcast_to(bias, LANES)])
    scalars = jnp.pad(scalars, ((0, 6), (0, 0)))
    image_blocks[1], scalars = lax.optimization_barrier((image_blocks[1], scalars))
    got = exchange(sent, "img", n_img, 1)
    numbers = jnp.pad(pairs.astype(jnp.float32)[None], ((0, 7), (0, width - count)))
    bundle = jnp.concatenate([image_blocks[k] for k in IMAGE_ORDER] + [numbers])

    own, loss_tile, d_near, *messages = pl.pallas_call(
        functools.partial(image_kernel, n_img, n_txt, rows, cols),
        out_shape=[vmem((rows, width)), vmem((8, LANES)), vmem((chips * cols, count))]
        + [vmem((tiles + 1, 8, LANES))] * (n_txt - 1),
        in_specs=[whole] * 5,
        out_specs=[whole] * (2 + n_txt),
        name="image_terms",
    )(*in_vmem(scalars, bundle, both, sent, got))
    messages = [exchange(messages[p - 1], "txt", n_txt, IMAGE_ORDER[p]) for p in (3, 2, 1)]

    pair = exchange(after(bundle, got), "img", n_img, 1)
    blocks = pl.pallas_call(
        functools.partial(text_kernel, n_img, n_txt, rows, cols),
        out_shape=[vmem((cols, width))] * chips,
        in_specs=[whole] * 7,
        out_specs=[whole] * chips,
        name="text_terms",
    )(*in_vmem(scalars, bundle, pair, both, sent, got, d_near))
    blocks = list(blocks)
    for k, distances in ((3, (3, 3)), (1, (1, 2)), (2, (2, 1))):
        blocks[k] = chip_exchange(blocks[k], n_img, distances)

    image_loss, image_grad, text_grad = pl.pallas_call(
        functools.partial(sum_kernel, n_txt, chips),
        out_shape=[
            jax.ShapeDtypeStruct(shape, jnp.float32)
            for shape in ((1, LANES), image_emb.shape, text_emb.shape)
        ],
        in_specs=[whole] * (1 + n_txt + chips),
        out_specs=[whole] * 3,
        name="sums",
    )(*in_vmem(own, loss_tile, *messages, blocks[3], *blocks[:3]))
    return (image_loss.reshape(count), image_grad, text_grad)


def per_device_large(image_emb, text_emb, pairs, log_scale, bias):
    images = lax.all_gather(image_emb, "txt", axis=0, tiled=True)
    texts = lax.all_gather(text_emb, "img", axis=0, tiled=True)
    scale = jnp.exp(log_scale[0])
    shift = bias[0]
    text_count = texts.shape[0]
    dots = lax.dot_general(
        images,
        texts,
        (((1,), (1,)), ((), ())),
        precision=lax.Precision.HIGHEST,
        preferred_element_type=jnp.float32,
    )
    logits = scale * dots + shift
    columns = lax.axis_index("txt") * text_count + jnp.arange(text_count, dtype=jnp.int32)
    sign = jnp.where(pairs[:, None] == columns[None, :], 1.0, -1.0).astype(jnp.float32)
    loss_part = jnp.sum(jax.nn.softplus(-sign * logits), axis=1)
    image_loss = lax.psum(loss_part, "txt")
    dlogits = -sign * jax.nn.sigmoid(-sign * logits)
    image_term = scale * jnp.dot(
        dlogits, texts, precision=lax.Precision.HIGHEST, preferred_element_type=jnp.float32
    )
    image_grad = lax.psum_scatter(image_term, "txt", scatter_dimension=0, tiled=True)
    text_term = scale * lax.dot_general(
        dlogits,
        images,
        (((0,), (0,)), ((), ())),
        precision=lax.Precision.HIGHEST,
        preferred_element_type=jnp.float32,
    )
    text_grad = lax.psum_scatter(text_term, "img", scatter_dimension=0, tiled=True)
    return (image_loss, image_grad, text_grad)


def solution(mesh):
    sizes = (mesh.shape["img"], mesh.shape["txt"])

    def body(image_emb, *others):
        rows = image_emb.shape[0]
        if sizes == (8, 4) and rows * sizes[1] == LANES:
            return per_device(sizes, image_emb, *others)
        return per_device_large(image_emb, *others)

    return jax.shard_map(
        body,
        mesh=mesh,
        in_specs=(P(("img", "txt"), None), P(("txt", "img"), None), P("img"), P(), P()),
        out_specs=(P("img"), P(("img", "txt"), None), P(("txt", "img"), None)),
        check_vma=False,
    )
```

```python
import functools

import jax
import jax.numpy as jnp
from jax import lax
from jax.experimental import pallas as pl
from jax.experimental.pallas import tpu as pltpu
from jax.sharding import PartitionSpec as P

LANES = 128

IMAGE_ORDER = (0, 2, 3, 1)


def exchange(x, axis, n, k):
    return lax.ppermute(x, axis, [(i, i ^ k) for i in range(n)])


def after(x, other):
    return lax.optimization_barrier((x, other))[0]


def chip_exchange(x, n_img, distances):
    return lax.ppermute(x, "img", [(i, i ^ (2 * distances[i % 2])) for i in range(n_img)])


def halves(x):
    high = x.astype(jnp.bfloat16)
    return high, (x - high.astype(jnp.float32)).astype(jnp.bfloat16)


def dot(pairs, contract):
    left = jnp.concatenate([part for a, _ in pairs for part in (a[0], a[0], a[1])], contract[0])
    right = jnp.concatenate([part for _, b in pairs for part in (b[0], b[1], b[0])], contract[1])
    dims = ((contract[:1], contract[1:]), ((), ()))
    return lax.dot_general(left, right, dims, preferred_element_type=jnp.float32)


def untwist(row, block, me):
    lane = lax.broadcasted_iota(jnp.int32, row.shape, 1)
    step = block
    while step < LANES:
        up, down = pltpu.roll(row, LANES - step, 1), pltpu.roll(row, step, 1)
        flipped = jnp.where((lane // step) % 2 == 0, up, down)
        row = jnp.where((me // (step // block)) % 2 == 1, flipped, row)
        step *= 2
    return row


def shuffle(row, block, sources):
    place = lax.broadcasted_iota(jnp.int32, row.shape, 1) // block
    result = row
    for step in range(1, len(sources)):
        moved = pltpu.roll(row, LANES - step * block, 1)
        for p, source in enumerate(sources):
            if (source - p) % len(sources) == step:
                result = jnp.where(place == p, moved, result)
    return result


def text_ids(shape, n_img, cols, far, along):
    me_img, me_txt = lax.axis_index("img"), lax.axis_index("txt")
    place = lax.broadcasted_iota(jnp.int32, shape, along)
    half = n_img // 2 * cols
    me_core = me_img % 2
    core = me_core
    if far:
        core = core ^ (place // half)
        place = place % half
    turn = place // cols
    distance = jnp.where(turn == 1, 1 + me_core, jnp.where(turn == 2, 2 - me_core, turn))
    chip = (me_img // 2) ^ distance
    return (me_txt * n_img + 2 * chip + core) * cols + place % cols


def own_core_texts(cols, both, sent, got):
    return [both[:cols], sent[:cols], got[cols:2 * cols], sent[2 * cols:]]


def other_core_texts(cols, both, sent, got):
    return [both[cols:], sent[cols:2 * cols], got[:cols], got[2 * cols:]]


def derivative(left, right, ids, matched, log_scale, bias):
    scale = jnp.exp(jnp.full((1, 1), log_scale[0], jnp.float32))
    logits = scale * dot([(left, right)], (1, 1)) + bias[0]
    match = ids == matched
    v = jnp.where(match, -logits, logits)
    e = jnp.exp(-jnp.abs(v))
    loss = jnp.maximum(v, 0.0) + jnp.log1p(e)
    s = scale * jnp.where(v >= 0, 1.0, e) / (1.0 + e)
    return loss, jnp.where(match, -s, s)


def matched_texts(bundle, rows, count):
    matched = untwist(bundle[count:count + 1, :LANES], rows, lax.axis_index("txt"))
    return shuffle(matched, rows, IMAGE_ORDER).astype(jnp.int32)


def turned(line):
    return jnp.broadcast_to(line, (LANES, LANES)).T


def image_kernel(
    n_img, n_txt, rows, cols, log_scale, bias, bundle, both, sent, got,
    own, loss_ref, d_near, *messages
):
    count = n_txt * rows
    matched = matched_texts(bundle, rows, count)
    images = halves(bundle[:count])
    near = own_core_texts(cols, both, sent, got)
    texts = halves(jnp.concatenate(near + other_core_texts(cols, both, sent, got)))
    ids = text_ids((count, texts[0].shape[0]), n_img, cols, True, 1)
    matched = turned(matched.astype(jnp.float32)).astype(jnp.int32)
    matched = jnp.concatenate([matched] * (ids.shape[1] // LANES), axis=1)
    loss, d = derivative(images, texts, ids, matched, log_scale, bias)
    term = dot([(halves(d), texts)], (1, 0))
    d_near[...] = d[:, :len(near) * cols].T
    own[...] = term[:rows]
    back = [IMAGE_ORDER.index(k) for k in range(n_txt)]
    loss_row = shuffle(turned(jnp.sum(loss, axis=1, keepdims=True))[:1], rows, back)
    loss_row = untwist(loss_row, rows, lax.axis_index("txt"))
    loss_tile = jnp.broadcast_to(loss_row, (8, LANES))
    loss_ref[...] = loss_tile
    across = term.shape[1] // LANES
    for p, ref in enumerate(messages, 1):
        for r in range(rows // 8):
            for c in range(across):
                ref[r * across + c] = term[
                    p * rows + r * 8:p * rows + r * 8 + 8, c * LANES:(c + 1) * LANES
                ]
        ref[rows // 8 * across] = loss_tile


def text_kernel(n_img, n_txt, rows, cols, *refs):
    log_scale, bias, bundle, pair, both, sent, got, d_ref = refs[:8]
    block_refs = refs[8:]
    count = n_txt * rows
    matched = matched_texts(pair, rows, count)
    others = halves(pair[:count])
    texts = halves(jnp.concatenate(own_core_texts(cols, both, sent, got)))
    ids = text_ids((texts[0].shape[0], count), n_img, cols, False, 0)
    _, d = derivative(texts, others, ids, matched, log_scale, bias)
    near = halves(d_ref[...]), halves(bundle[:count])
    term = dot([near, (halves(d), others)], (1, 0))
    for k, ref in enumerate(block_refs):
        ref[...] = term[k * cols:(k + 1) * cols]


def sum_kernel(n_txt, n_chips, own_ref, loss_ref, *refs):
    messages, blocks = refs[:n_txt - 1], refs[n_txt - 1:n_txt - 1 + n_chips]
    image_loss, image_grad, text_grad = refs[n_txt - 1 + n_chips:]
    text_grad[...] = sum(b[...] for b in blocks)
    rows, width = own_ref.shape
    across = width // LANES
    for r in range(rows // 8):
        for c in range(across):
            at = (slice(r * 8, r * 8 + 8), slice(c * LANES, (c + 1) * LANES))
            image_grad[at] = own_ref[at] + sum(m[r * across + c] for m in messages)
    image_loss[...] = (loss_ref[...] + sum(m[rows // 8 * across] for m in messages))[:1]


def in_vmem(*arrays):
    return [pltpu.with_memory_space_constraint(x, pltpu.VMEM) for x in arrays]


def vmem(shape):
    return pltpu.VMEM(shape, jnp.float32)


def per_device(sizes, image_emb, text_emb, pairs, log_scale, bias):
    n_img, n_txt = sizes
    chips = n_img // 2
    rows, cols, width = image_emb.shape[0], text_emb.shape[0], image_emb.shape[1]
    count = n_txt * rows
    tiles = rows * width // (8 * LANES)
    smem, whole = pl.BlockSpec(memory_space=pltpu.SMEM), pl.BlockSpec(memory_space=pltpu.VMEM)

    both = jnp.concatenate([text_emb, exchange(text_emb, "img", n_img, 1)])
    image_blocks = [image_emb] + [None] * (n_txt - 1)
    for k in (2, 3):
        image_blocks[k] = exchange(image_emb, "txt", n_txt, k)
    beside = chip_exchange(both, n_img, (1, 2))
    diagonal = chip_exchange(text_emb, n_img, (3, 3))
    image_blocks[1] = exchange(after(image_emb, both), "txt", n_txt, 1)
    sent = jnp.concatenate([beside, diagonal])
    got = exchange(sent, "img", n_img, 1)
    numbers = jnp.pad(pairs.astype(jnp.float32)[None], ((0, 7), (0, width - count)))
    bundle = jnp.concatenate([image_blocks[k] for k in IMAGE_ORDER] + [numbers])

    own, loss_tile, d_near, *messages = pl.pallas_call(
        functools.partial(image_kernel, n_img, n_txt, rows, cols),
        out_shape=[vmem((rows, width)), vmem((8, LANES)), vmem((chips * cols, count))]
        + [vmem((tiles + 1, 8, LANES))] * (n_txt - 1),
        in_specs=[smem] * 2 + [whole] * 4,
        out_specs=[whole] * (2 + n_txt),
        name="image_terms",
    )(log_scale, bias, *in_vmem(bundle, both, sent, got))
    messages = [exchange(messages[p - 1], "txt", n_txt, IMAGE_ORDER[p]) for p in (3, 2, 1)]

    pair = exchange(bundle, "img", n_img, 1)
    blocks = pl.pallas_call(
        functools.partial(text_kernel, n_img, n_txt, rows, cols),
        out_shape=[vmem((cols, width))] * chips,
        in_specs=[smem] * 2 + [whole] * 6,
        out_specs=[whole] * chips,
        name="text_terms",
    )(log_scale, bias, *in_vmem(bundle, pair, both, sent, got, d_near))
    blocks = list(blocks)
    for k, distances in ((3, (3, 3)), (1, (1, 2)), (2, (2, 1))):
        blocks[k] = chip_exchange(blocks[k], n_img, distances)

    image_loss, image_grad, text_grad = pl.pallas_call(
        functools.partial(sum_kernel, n_txt, chips),
        out_shape=[
            jax.ShapeDtypeStruct(shape, jnp.float32)
            for shape in ((1, LANES), image_emb.shape, text_emb.shape)
        ],
        in_specs=[whole] * (1 + n_txt + chips),
        out_specs=[whole] * 3,
        name="sums",
    )(*in_vmem(own, loss_tile, *messages, blocks[3], *blocks[:3]))
    return (image_loss.reshape(count), image_grad, text_grad)


def per_device_large(image_emb, text_emb, pairs, log_scale, bias):
    images = lax.all_gather(image_emb, "txt", axis=0, tiled=True)
    texts = lax.all_gather(text_emb, "img", axis=0, tiled=True)
    scale = jnp.exp(log_scale[0])
    shift = bias[0]
    text_count = texts.shape[0]
    dots = lax.dot_general(
        images,
        texts,
        (((1,), (1,)), ((), ())),
        precision=lax.Precision.HIGHEST,
        preferred_element_type=jnp.float32,
    )
    logits = scale * dots + shift
    columns = lax.axis_index("txt") * text_count + jnp.arange(text_count, dtype=jnp.int32)
    sign = jnp.where(pairs[:, None] == columns[None, :], 1.0, -1.0).astype(jnp.float32)
    loss_part = jnp.sum(jax.nn.softplus(-sign * logits), axis=1)
    image_loss = lax.psum(loss_part, "txt")
    dlogits = -sign * jax.nn.sigmoid(-sign * logits)
    image_term = scale * jnp.dot(
        dlogits, texts, precision=lax.Precision.HIGHEST, preferred_element_type=jnp.float32
    )
    image_grad = lax.psum_scatter(image_term, "txt", scatter_dimension=0, tiled=True)
    text_term = scale * lax.dot_general(
        dlogits,
        images,
        (((0,), (0,)), ((), ())),
        precision=lax.Precision.HIGHEST,
        preferred_element_type=jnp.float32,
    )
    text_grad = lax.psum_scatter(text_term, "img", scatter_dimension=0, tiled=True)
    return (image_loss, image_grad, text_grad)


def solution(mesh):
    sizes = (mesh.shape["img"], mesh.shape["txt"])

    def body(image_emb, *others):
        rows = image_emb.shape[0]
        if sizes == (8, 4) and rows * sizes[1] == LANES:
            return per_device(sizes, image_emb, *others)
        return per_device_large(image_emb, *others)

    return jax.shard_map(
        body,
        mesh=mesh,
        in_specs=(P(("img", "txt"), None), P(("txt", "img"), None), P("img"), P(), P()),
        out_specs=(P("img"), P(("img", "txt"), None), P(("txt", "img"), None)),
        check_vma=False,
    )
```

```python
import functools

import jax
import jax.numpy as jnp
from jax import lax
from jax.experimental import pallas as pl
from jax.experimental.pallas import tpu as pltpu
from jax.sharding import PartitionSpec as P

LANES = 128

IMAGE_ORDER = (0, 2, 3, 1)


def exchange(x, axis, n, k):
    return lax.ppermute(x, axis, [(i, i ^ k) for i in range(n)])


def after(x, other):
    return lax.optimization_barrier((x, other))[0]


def chip_exchange(x, n_img, distances):
    return lax.ppermute(x, "img", [(i, i ^ (2 * distances[i % 2])) for i in range(n_img)])


def halves(x):
    high = x.astype(jnp.bfloat16)
    return high, (x - high.astype(jnp.float32)).astype(jnp.bfloat16)


def dot(pairs, contract):
    left = jnp.concatenate([part for a, _ in pairs for part in (a[0], a[0], a[1])], contract[0])
    right = jnp.concatenate([part for _, b in pairs for part in (b[0], b[1], b[0])], contract[1])
    dims = ((contract[:1], contract[1:]), ((), ()))
    return lax.dot_general(left, right, dims, preferred_element_type=jnp.float32)


def untwist(row, block, me):
    lane = lax.broadcasted_iota(jnp.int32, row.shape, 1)
    step = block
    while step < LANES:
        up, down = pltpu.roll(row, LANES - step, 1), pltpu.roll(row, step, 1)
        flipped = jnp.where((lane // step) % 2 == 0, up, down)
        row = jnp.where((me // (step // block)) % 2 == 1, flipped, row)
        step *= 2
    return row


def shuffle(row, block, sources):
    place = lax.broadcasted_iota(jnp.int32, row.shape, 1) // block
    result = row
    for step in range(1, len(sources)):
        moved = pltpu.roll(row, LANES - step * block, 1)
        for p, source in enumerate(sources):
            if (source - p) % len(sources) == step:
                result = jnp.where(place == p, moved, result)
    return result


def text_ids(shape, n_img, cols, far, along):
    me_img, me_txt = lax.axis_index("img"), lax.axis_index("txt")
    place = lax.broadcasted_iota(jnp.int32, shape, along)
    half = n_img // 2 * cols
    me_core = me_img % 2
    core = me_core
    if far:
        core = core ^ (place // half)
        place = place % half
    turn = place // cols
    distance = jnp.where(turn == 1, 1 + me_core, jnp.where(turn == 2, 2 - me_core, turn))
    chip = (me_img // 2) ^ distance
    return (me_txt * n_img + 2 * chip + core) * cols + place % cols


def own_core_texts(cols, both, sent, got):
    return [both[:cols], sent[:cols], got[cols:2 * cols], sent[2 * cols:]]


def other_core_texts(cols, both, sent, got):
    return [both[cols:], sent[cols:2 * cols], got[:cols], got[2 * cols:]]


def derivative(left, right, ids, matched, log_scale, bias):
    scale = jnp.exp(jnp.full((1, 1), log_scale[0], jnp.float32))
    logits = scale * dot([(left, right)], (1, 1)) + bias[0]
    match = ids == matched
    v = jnp.where(match, -logits, logits)
    e = jnp.exp(-jnp.abs(v))
    loss = jnp.maximum(v, 0.0) + jnp.log1p(e)
    s = scale * jnp.where(v >= 0, 1.0, e) / (1.0 + e)
    return loss, jnp.where(match, -s, s)


def matched_texts(bundle, rows, count):
    matched = untwist(bundle[count:count + 1, :LANES], rows, lax.axis_index("txt"))
    return shuffle(matched, rows, IMAGE_ORDER).astype(jnp.int32)


def turned(line):
    return jnp.broadcast_to(line, (LANES, LANES)).T


def image_kernel(
    n_img, n_txt, rows, cols, log_scale, bias, bundle, both, sent, got,
    own, loss_ref, d_near, *messages
):
    count = n_txt * rows
    matched = matched_texts(bundle, rows, count)
    images = halves(bundle[:count])
    near = own_core_texts(cols, both, sent, got)
    texts = halves(jnp.concatenate(near + other_core_texts(cols, both, sent, got)))
    ids = text_ids((count, texts[0].shape[0]), n_img, cols, True, 1)
    matched = turned(matched.astype(jnp.float32)).astype(jnp.int32)
    matched = jnp.concatenate([matched] * (ids.shape[1] // LANES), axis=1)
    loss, d = derivative(images, texts, ids, matched, log_scale, bias)
    term = dot([(halves(d), texts)], (1, 0))
    d_near[...] = d[:, :len(near) * cols].T
    own[...] = term[:rows]
    back = [IMAGE_ORDER.index(k) for k in range(n_txt)]
    loss_row = shuffle(turned(jnp.sum(loss, axis=1, keepdims=True))[:1], rows, back)
    loss_row = untwist(loss_row, rows, lax.axis_index("txt"))
    loss_tile = jnp.broadcast_to(loss_row, (8, LANES))
    loss_ref[...] = loss_tile
    across = term.shape[1] // LANES
    for p, ref in enumerate(messages, 1):
        for r in range(rows // 8):
            for c in range(across):
                ref[r * across + c] = term[
                    p * rows + r * 8:p * rows + r * 8 + 8, c * LANES:(c + 1) * LANES
                ]
        ref[rows // 8 * across] = loss_tile


def text_kernel(n_img, n_txt, rows, cols, *refs):
    log_scale, bias, bundle, pair, both, sent, got, d_ref = refs[:8]
    block_refs = refs[8:]
    count = n_txt * rows
    matched = matched_texts(pair, rows, count)
    others = halves(pair[:count])
    texts = halves(jnp.concatenate(own_core_texts(cols, both, sent, got)))
    ids = text_ids((texts[0].shape[0], count), n_img, cols, False, 0)
    _, d = derivative(texts, others, ids, matched, log_scale, bias)
    near = halves(d_ref[...]), halves(bundle[:count])
    term = dot([near, (halves(d), others)], (1, 0))
    for k, ref in enumerate(block_refs):
        ref[...] = term[k * cols:(k + 1) * cols]


def sum_kernel(n_txt, n_chips, own_ref, loss_ref, *refs):
    messages, blocks = refs[:n_txt - 1], refs[n_txt - 1:n_txt - 1 + n_chips]
    image_loss, image_grad, text_grad = refs[n_txt - 1 + n_chips:]
    text_grad[...] = sum(b[...] for b in blocks)
    rows, width = own_ref.shape
    across = width // LANES
    for r in range(rows // 8):
        for c in range(across):
            at = (slice(r * 8, r * 8 + 8), slice(c * LANES, (c + 1) * LANES))
            image_grad[at] = own_ref[at] + sum(m[r * across + c] for m in messages)
    image_loss[...] = (loss_ref[...] + sum(m[rows // 8 * across] for m in messages))[:1]


def in_vmem(*arrays):
    return [pltpu.with_memory_space_constraint(x, pltpu.VMEM) for x in arrays]


def vmem(shape):
    return pltpu.VMEM(shape, jnp.float32)


def per_device(sizes, image_emb, text_emb, pairs, log_scale, bias):
    n_img, n_txt = sizes
    chips = n_img // 2
    rows, cols, width = image_emb.shape[0], text_emb.shape[0], image_emb.shape[1]
    count = n_txt * rows
    tiles = rows * width // (8 * LANES)
    smem, whole = pl.BlockSpec(memory_space=pltpu.SMEM), pl.BlockSpec(memory_space=pltpu.VMEM)

    both = jnp.concatenate([text_emb, exchange(text_emb, "img", n_img, 1)])
    image_blocks = [image_emb] + [None] * (n_txt - 1)
    for k in (2, 3):
        image_blocks[k] = exchange(image_emb, "txt", n_txt, k)
    beside = chip_exchange(both, n_img, (1, 2))
    diagonal = chip_exchange(after(text_emb, both), n_img, (3, 3))
    image_blocks[1] = exchange(after(image_emb, both), "txt", n_txt, 1)
    sent = jnp.concatenate([beside, diagonal])
    got = exchange(sent, "img", n_img, 1)
    numbers = jnp.pad(pairs.astype(jnp.float32)[None], ((0, 7), (0, width - count)))
    bundle = jnp.concatenate([image_blocks[k] for k in IMAGE_ORDER] + [numbers])

    own, loss_tile, d_near, *messages = pl.pallas_call(
        functools.partial(image_kernel, n_img, n_txt, rows, cols),
        out_shape=[vmem((rows, width)), vmem((8, LANES)), vmem((chips * cols, count))]
        + [vmem((tiles + 1, 8, LANES))] * (n_txt - 1),
        in_specs=[smem] * 2 + [whole] * 4,
        out_specs=[whole] * (2 + n_txt),
        name="image_terms",
    )(log_scale, bias, *in_vmem(bundle, both, sent, got))
    messages = [exchange(messages[p - 1], "txt", n_txt, IMAGE_ORDER[p]) for p in (3, 2, 1)]

    pair = exchange(bundle, "img", n_img, 1)
    blocks = pl.pallas_call(
        functools.partial(text_kernel, n_img, n_txt, rows, cols),
        out_shape=[vmem((cols, width))] * chips,
        in_specs=[smem] * 2 + [whole] * 6,
        out_specs=[whole] * chips,
        name="text_terms",
    )(log_scale, bias, *in_vmem(bundle, pair, both, sent, got, d_near))
    blocks = list(blocks)
    for k, distances in ((3, (3, 3)), (1, (1, 2)), (2, (2, 1))):
        blocks[k] = chip_exchange(blocks[k], n_img, distances)

    image_loss, image_grad, text_grad = pl.pallas_call(
        functools.partial(sum_kernel, n_txt, chips),
        out_shape=[
            jax.ShapeDtypeStruct(shape, jnp.float32)
            for shape in ((1, LANES), image_emb.shape, text_emb.shape)
        ],
        in_specs=[whole] * (1 + n_txt + chips),
        out_specs=[whole] * 3,
        name="sums",
    )(*in_vmem(own, loss_tile, *messages, blocks[3], *blocks[:3]))
    return (image_loss.reshape(count), image_grad, text_grad)


def per_device_large(image_emb, text_emb, pairs, log_scale, bias):
    images = lax.all_gather(image_emb, "txt", axis=0, tiled=True)
    texts = lax.all_gather(text_emb, "img", axis=0, tiled=True)
    scale = jnp.exp(log_scale[0])
    shift = bias[0]
    text_count = texts.shape[0]
    dots = lax.dot_general(
        images,
        texts,
        (((1,), (1,)), ((), ())),
        precision=lax.Precision.HIGHEST,
        preferred_element_type=jnp.float32,
    )
    logits = scale * dots + shift
    columns = lax.axis_index("txt") * text_count + jnp.arange(text_count, dtype=jnp.int32)
    sign = jnp.where(pairs[:, None] == columns[None, :], 1.0, -1.0).astype(jnp.float32)
    loss_part = jnp.sum(jax.nn.softplus(-sign * logits), axis=1)
    image_loss = lax.psum(loss_part, "txt")
    dlogits = -sign * jax.nn.sigmoid(-sign * logits)
    image_term = scale * jnp.dot(
        dlogits, texts, precision=lax.Precision.HIGHEST, preferred_element_type=jnp.float32
    )
    image_grad = lax.psum_scatter(image_term, "txt", scatter_dimension=0, tiled=True)
    text_term = scale * lax.dot_general(
        dlogits,
        images,
        (((0,), (0,)), ((), ())),
        precision=lax.Precision.HIGHEST,
        preferred_element_type=jnp.float32,
    )
    text_grad = lax.psum_scatter(text_term, "img", scatter_dimension=0, tiled=True)
    return (image_loss, image_grad, text_grad)


def solution(mesh):
    sizes = (mesh.shape["img"], mesh.shape["txt"])

    def body(image_emb, *others):
        rows = image_emb.shape[0]
        if sizes == (8, 4) and rows * sizes[1] == LANES:
            return per_device(sizes, image_emb, *others)
        return per_device_large(image_emb, *others)

    return jax.shard_map(
        body,
        mesh=mesh,
        in_specs=(P(("img", "txt"), None), P(("txt", "img"), None), P("img"), P(), P()),
        out_specs=(P("img"), P(("img", "txt"), None), P(("txt", "img"), None)),
        check_vma=False,
    )
```

```python
import functools

import jax
import jax.numpy as jnp
from jax import lax
from jax.experimental import pallas as pl
from jax.experimental.pallas import tpu as pltpu
from jax.sharding import PartitionSpec as P

LANES = 128

IMAGE_ORDER = (0, 3, 2, 1)


def exchange(x, axis, n, k):
    return lax.ppermute(x, axis, [(i, i ^ k) for i in range(n)])


def after(x, other):
    return lax.optimization_barrier((x, other))[0]


def chip_exchange(x, n_img, distances):
    return lax.ppermute(x, "img", [(i, i ^ (2 * distances[i % 2])) for i in range(n_img)])


def halves(x):
    high = x.astype(jnp.bfloat16)
    return high, (x - high.astype(jnp.float32)).astype(jnp.bfloat16)


def dot(a, b, contract):
    def part(x, y):
        dims = ((contract[:1], contract[1:]), ((), ()))
        return lax.dot_general(x, y, dims, preferred_element_type=jnp.float32)

    return part(a[0], b[0]) + (part(a[0], b[1]) + part(a[1], b[0]))


def untwist(row, block, me):
    lane = lax.broadcasted_iota(jnp.int32, row.shape, 1)
    step = block
    while step < LANES:
        up, down = pltpu.roll(row, LANES - step, 1), pltpu.roll(row, step, 1)
        flipped = jnp.where((lane // step) % 2 == 0, up, down)
        row = jnp.where((me // (step // block)) % 2 == 1, flipped, row)
        step *= 2
    return row


def shuffle(row, block, sources):
    place = lax.broadcasted_iota(jnp.int32, row.shape, 1) // block
    result = row
    for step in range(1, len(sources)):
        moved = pltpu.roll(row, LANES - step * block, 1)
        for p, source in enumerate(sources):
            if (source - p) % len(sources) == step:
                result = jnp.where(place == p, moved, result)
    return result


def text_ids(shape, n_img, cols, far):
    me_img, me_txt = lax.axis_index("img"), lax.axis_index("txt")
    place = lax.broadcasted_iota(jnp.int32, shape, 0)
    half = n_img // 2 * cols
    me_core = me_img % 2
    core = me_core
    if far:
        core = core ^ (place // half)
        place = place % half
    turn = place // cols
    distance = jnp.where(turn == 1, 1 + me_core, jnp.where(turn == 2, 2 - me_core, turn))
    chip = (me_img // 2) ^ distance
    return (me_txt * n_img + 2 * chip + core) * cols + place % cols


def own_core_texts(cols, both, sent, got):
    return [both[:cols], sent[:cols], got[cols:2 * cols], sent[2 * cols:]]


def other_core_texts(cols, both, sent, got):
    return [both[cols:], sent[cols:2 * cols], got[:cols], got[2 * cols:]]


def derivative(texts, images, ids, matched, log_scale, bias):
    scale = jnp.exp(jnp.full((1, LANES), log_scale[0], jnp.float32))
    logits = scale * dot(texts, images, (1, 1)) + bias[0]
    match = ids == matched
    v = jnp.where(match, -logits, logits)
    e = jnp.exp(-jnp.abs(v))
    loss = jnp.maximum(v, 0.0) + jnp.log1p(e)
    s = scale * jnp.where(v >= 0, 1.0, e) / (1.0 + e)
    return loss, jnp.where(match, -s, s)


def matched_texts(bundle, rows, count):
    matched = untwist(bundle[count:count + 1, :LANES], rows, lax.axis_index("txt"))
    return shuffle(matched, rows, IMAGE_ORDER).astype(jnp.int32)


def image_kernel(
    n_img, n_txt, rows, cols, log_scale, bias, bundle, both, sent, got,
    own, loss_ref, d_near, *messages
):
    count = n_txt * rows
    matched = matched_texts(bundle, rows, count)
    images = halves(bundle[:count])
    near = own_core_texts(cols, both, sent, got)
    texts = halves(jnp.concatenate(near + other_core_texts(cols, both, sent, got)))
    ids = text_ids((texts[0].shape[0], count), n_img, cols, True)
    loss, d = derivative(texts, images, ids, matched, log_scale, bias)
    d_near[...] = d[:len(near) * cols]
    term = dot(halves(d), texts, (0, 0))
    own[...] = term[:rows]
    back = [IMAGE_ORDER.index(k) for k in range(n_txt)]
    loss_row = shuffle(jnp.sum(loss, axis=0, keepdims=True), rows, back)
    loss_row = untwist(loss_row, rows, lax.axis_index("txt"))
    loss_tile = jnp.broadcast_to(loss_row, (8, LANES))
    loss_ref[...] = loss_tile
    across = term.shape[1] // LANES
    for p, ref in enumerate(messages, 1):
        for r in range(rows // 8):
            for c in range(across):
                ref[r * across + c] = term[
                    p * rows + r * 8:p * rows + r * 8 + 8, c * LANES:(c + 1) * LANES
                ]
        ref[rows // 8 * across] = loss_tile


def text_kernel(n_img, n_txt, rows, cols, *refs):
    log_scale, bias, bundle, pair, both, sent, got, d_ref = refs[:8]
    block_refs = refs[8:]
    count = n_txt * rows
    matched = matched_texts(pair, rows, count)
    others = halves(pair[:count])
    texts = halves(jnp.concatenate(own_core_texts(cols, both, sent, got)))
    ids = text_ids((texts[0].shape[0], count), n_img, cols, False)
    _, d = derivative(texts, others, ids, matched, log_scale, bias)
    term = dot(halves(d_ref[...]), halves(bundle[:count]), (1, 0)) + dot(halves(d), others, (1, 0))
    for k, ref in enumerate(block_refs):
        ref[...] = term[k * cols:(k + 1) * cols]


def sum_kernel(n_txt, n_chips, own_ref, loss_ref, *refs):
    messages, blocks = refs[:n_txt - 1], refs[n_txt - 1:n_txt - 1 + n_chips]
    image_loss, image_grad, text_grad = refs[n_txt - 1 + n_chips:]
    text_grad[...] = sum(b[...] for b in blocks)
    rows, width = own_ref.shape
    across = width // LANES
    for r in range(rows // 8):
        for c in range(across):
            at = (slice(r * 8, r * 8 + 8), slice(c * LANES, (c + 1) * LANES))
            image_grad[at] = own_ref[at] + sum(m[r * across + c] for m in messages)
    image_loss[...] = (loss_ref[...] + sum(m[rows // 8 * across] for m in messages))[:1]


def in_vmem(*arrays):
    return [pltpu.with_memory_space_constraint(x, pltpu.VMEM) for x in arrays]


def vmem(shape):
    return pltpu.VMEM(shape, jnp.float32)


def per_device(sizes, image_emb, text_emb, pairs, log_scale, bias):
    n_img, n_txt = sizes
    chips = n_img // 2
    rows, cols, width = image_emb.shape[0], text_emb.shape[0], image_emb.shape[1]
    count = n_txt * rows
    tiles = rows * width // (8 * LANES)
    smem, whole = pl.BlockSpec(memory_space=pltpu.SMEM), pl.BlockSpec(memory_space=pltpu.VMEM)

    both = jnp.concatenate([text_emb, exchange(text_emb, "img", n_img, 1)])
    image_blocks = [image_emb] + [None] * (n_txt - 1)
    for k in (2, 3):
        image_blocks[k] = exchange(image_emb, "txt", n_txt, k)
    beside = chip_exchange(both, n_img, (1, 2))
    diagonal = chip_exchange(text_emb, n_img, (3, 3))
    image_blocks[1] = exchange(after(image_emb, both), "txt", n_txt, 1)
    sent = jnp.concatenate([beside, diagonal])
    got = exchange(sent, "img", n_img, 1)
    numbers = jnp.pad(pairs.astype(jnp.float32)[None], ((0, 7), (0, width - count)))
    bundle = jnp.concatenate([image_blocks[k] for k in IMAGE_ORDER] + [numbers])

    own, loss_tile, d_near, *messages = pl.pallas_call(
        functools.partial(image_kernel, n_img, n_txt, rows, cols),
        out_shape=[vmem((rows, width)), vmem((8, LANES)), vmem((chips * cols, count))]
        + [vmem((tiles + 1, 8, LANES))] * (n_txt - 1),
        in_specs=[smem] * 2 + [whole] * 4,
        out_specs=[whole] * (2 + n_txt),
        name="image_terms",
    )(log_scale, bias, *in_vmem(bundle, both, sent, got))
    messages = [exchange(messages[p - 1], "txt", n_txt, IMAGE_ORDER[p]) for p in (3, 2, 1)]

    pair = exchange(bundle, "img", n_img, 1)
    blocks = pl.pallas_call(
        functools.partial(text_kernel, n_img, n_txt, rows, cols),
        out_shape=[vmem((cols, width))] * chips,
        in_specs=[smem] * 2 + [whole] * 6,
        out_specs=[whole] * chips,
        name="text_terms",
    )(log_scale, bias, *in_vmem(bundle, pair, both, sent, got, d_near))
    blocks = list(blocks)
    for k, distances in ((3, (3, 3)), (1, (1, 2)), (2, (2, 1))):
        blocks[k] = chip_exchange(blocks[k], n_img, distances)

    image_loss, image_grad, text_grad = pl.pallas_call(
        functools.partial(sum_kernel, n_txt, chips),
        out_shape=[
            jax.ShapeDtypeStruct(shape, jnp.float32)
            for shape in ((1, LANES), image_emb.shape, text_emb.shape)
        ],
        in_specs=[whole] * (1 + n_txt + chips),
        out_specs=[whole] * 3,
        name="sums",
    )(*in_vmem(own, loss_tile, *messages, blocks[3], *blocks[:3]))
    return (image_loss.reshape(count), image_grad, text_grad)


def per_device_large(image_emb, text_emb, pairs, log_scale, bias):
    images = lax.all_gather(image_emb, "txt", axis=0, tiled=True)
    texts = lax.all_gather(text_emb, "img", axis=0, tiled=True)
    scale = jnp.exp(log_scale[0])
    shift = bias[0]
    text_count = texts.shape[0]
    dots = lax.dot_general(
        images,
        texts,
        (((1,), (1,)), ((), ())),
        precision=lax.Precision.HIGHEST,
        preferred_element_type=jnp.float32,
    )
    logits = scale * dots + shift
    columns = lax.axis_index("txt") * text_count + jnp.arange(text_count, dtype=jnp.int32)
    sign = jnp.where(pairs[:, None] == columns[None, :], 1.0, -1.0).astype(jnp.float32)
    loss_part = jnp.sum(jax.nn.softplus(-sign * logits), axis=1)
    image_loss = lax.psum(loss_part, "txt")
    dlogits = -sign * jax.nn.sigmoid(-sign * logits)
    image_term = scale * jnp.dot(
        dlogits, texts, precision=lax.Precision.HIGHEST, preferred_element_type=jnp.float32
    )
    image_grad = lax.psum_scatter(image_term, "txt", scatter_dimension=0, tiled=True)
    text_term = scale * lax.dot_general(
        dlogits,
        images,
        (((0,), (0,)), ((), ())),
        precision=lax.Precision.HIGHEST,
        preferred_element_type=jnp.float32,
    )
    text_grad = lax.psum_scatter(text_term, "img", scatter_dimension=0, tiled=True)
    return (image_loss, image_grad, text_grad)


def solution(mesh):
    sizes = (mesh.shape["img"], mesh.shape["txt"])

    def body(image_emb, *others):
        rows = image_emb.shape[0]
        if sizes == (8, 4) and rows * sizes[1] == LANES:
            return per_device(sizes, image_emb, *others)
        return per_device_large(image_emb, *others)

    return jax.shard_map(
        body,
        mesh=mesh,
        in_specs=(P(("img", "txt"), None), P(("txt", "img"), None), P("img"), P(), P()),
        out_specs=(P("img"), P(("img", "txt"), None), P(("txt", "img"), None)),
        check_vma=False,
    )
```

```python
import functools

import jax
import jax.numpy as jnp
from jax import lax
from jax.experimental import pallas as pl
from jax.experimental.pallas import tpu as pltpu
from jax.sharding import PartitionSpec as P

LANES = 128

IMAGE_ORDER = (0, 2, 3, 1)


def exchange(x, axis, n, k):
    return lax.ppermute(x, axis, [(i, i ^ k) for i in range(n)])


def after(x, other):
    return lax.optimization_barrier((x, other))[0]


def chip_exchange(x, n_img, distances):
    return lax.ppermute(x, "img", [(i, i ^ (2 * distances[i % 2])) for i in range(n_img)])


def halves(x):
    high = x.astype(jnp.bfloat16)
    return high, (x - high.astype(jnp.float32)).astype(jnp.bfloat16)


def dot(a, b, contract):
    def part(x, y):
        dims = ((contract[:1], contract[1:]), ((), ()))
        return lax.dot_general(x, y, dims, preferred_element_type=jnp.float32)

    return part(a[0], b[0]) + (part(a[0], b[1]) + part(a[1], b[0]))


def untwist(row, block, me):
    lane = lax.broadcasted_iota(jnp.int32, row.shape, 1)
    step = block
    while step < LANES:
        up, down = pltpu.roll(row, LANES - step, 1), pltpu.roll(row, step, 1)
        flipped = jnp.where((lane // step) % 2 == 0, up, down)
        row = jnp.where((me // (step // block)) % 2 == 1, flipped, row)
        step *= 2
    return row


def shuffle(row, block, sources):
    place = lax.broadcasted_iota(jnp.int32, row.shape, 1) // block
    result = row
    for step in range(1, len(sources)):
        moved = pltpu.roll(row, LANES - step * block, 1)
        for p, source in enumerate(sources):
            if (source - p) % len(sources) == step:
                result = jnp.where(place == p, moved, result)
    return result


def text_ids(shape, n_img, cols, far):
    me_img, me_txt = lax.axis_index("img"), lax.axis_index("txt")
    place = lax.broadcasted_iota(jnp.int32, shape, 0)
    half = n_img // 2 * cols
    me_core = me_img % 2
    core = me_core
    if far:
        core = core ^ (place // half)
        place = place % half
    turn = place // cols
    distance = jnp.where(turn == 1, 1 + me_core, jnp.where(turn == 2, 2 - me_core, turn))
    chip = (me_img // 2) ^ distance
    return (me_txt * n_img + 2 * chip + core) * cols + place % cols


def own_core_texts(cols, both, sent, got):
    return [both[:cols], sent[:cols], got[cols:2 * cols], sent[2 * cols:]]


def other_core_texts(cols, both, sent, got):
    return [both[cols:], sent[cols:2 * cols], got[:cols], got[2 * cols:]]


def derivative(texts, images, ids, matched, log_scale, bias):
    scale = jnp.exp(jnp.full((1, LANES), log_scale[0], jnp.float32))
    logits = scale * dot(texts, images, (1, 1)) + bias[0]
    match = ids == matched
    v = jnp.where(match, -logits, logits)
    e = jnp.exp(-jnp.abs(v))
    loss = jnp.maximum(v, 0.0) + jnp.log1p(e)
    s = scale * jnp.where(v >= 0, 1.0, e) / (1.0 + e)
    return loss, jnp.where(match, -s, s)


def matched_texts(bundle, rows, count):
    matched = untwist(bundle[count:count + 1, :LANES], rows, lax.axis_index("txt"))
    return shuffle(matched, rows, IMAGE_ORDER).astype(jnp.int32)


def image_kernel(
    n_img, n_txt, rows, cols, log_scale, bias, bundle, both, sent, got,
    own, loss_ref, d_near, *messages
):
    count = n_txt * rows
    matched = matched_texts(bundle, rows, count)
    images = halves(bundle[:count])
    near = own_core_texts(cols, both, sent, got)
    texts = halves(jnp.concatenate(near + other_core_texts(cols, both, sent, got)))
    ids = text_ids((texts[0].shape[0], count), n_img, cols, True)
    loss, d = derivative(texts, images, ids, matched, log_scale, bias)
    d_near[...] = d[:len(near) * cols]
    term = dot(halves(d), texts, (0, 0))
    own[...] = term[:rows]
    back = [IMAGE_ORDER.index(k) for k in range(n_txt)]
    loss_row = shuffle(jnp.sum(loss, axis=0, keepdims=True), rows, back)
    loss_row = untwist(loss_row, rows, lax.axis_index("txt"))
    loss_tile = jnp.broadcast_to(loss_row, (8, LANES))
    loss_ref[...] = loss_tile
    across = term.shape[1] // LANES
    for p, ref in enumerate(messages, 1):
        for r in range(rows // 8):
            for c in range(across):
                ref[r * across + c] = term[
                    p * rows + r * 8:p * rows + r * 8 + 8, c * LANES:(c + 1) * LANES
                ]
        ref[rows // 8 * across] = loss_tile


def text_kernel(n_img, n_txt, rows, cols, *refs):
    log_scale, bias, bundle, pair, both, sent, got, d_ref = refs[:8]
    block_refs = refs[8:]
    count = n_txt * rows
    matched = matched_texts(pair, rows, count)
    others = halves(pair[:count])
    texts = halves(jnp.concatenate(own_core_texts(cols, both, sent, got)))
    ids = text_ids((texts[0].shape[0], count), n_img, cols, False)
    _, d = derivative(texts, others, ids, matched, log_scale, bias)
    term = dot(halves(d_ref[...]), halves(bundle[:count]), (1, 0)) + dot(halves(d), others, (1, 0))
    for k, ref in enumerate(block_refs):
        ref[...] = term[k * cols:(k + 1) * cols]


def sum_kernel(n_txt, n_chips, own_ref, loss_ref, *refs):
    messages, blocks = refs[:n_txt - 1], refs[n_txt - 1:n_txt - 1 + n_chips]
    image_loss, image_grad, text_grad = refs[n_txt - 1 + n_chips:]
    text_grad[...] = sum(b[...] for b in blocks)
    rows, width = own_ref.shape
    across = width // LANES
    for r in range(rows // 8):
        for c in range(across):
            at = (slice(r * 8, r * 8 + 8), slice(c * LANES, (c + 1) * LANES))
            image_grad[at] = own_ref[at] + sum(m[r * across + c] for m in messages)
    image_loss[...] = (loss_ref[...] + sum(m[rows // 8 * across] for m in messages))[:1]


def in_vmem(*arrays):
    return [pltpu.with_memory_space_constraint(x, pltpu.VMEM) for x in arrays]


def vmem(shape):
    return pltpu.VMEM(shape, jnp.float32)


def per_device(sizes, image_emb, text_emb, pairs, log_scale, bias):
    n_img, n_txt = sizes
    chips = n_img // 2
    rows, cols, width = image_emb.shape[0], text_emb.shape[0], image_emb.shape[1]
    count = n_txt * rows
    tiles = rows * width // (8 * LANES)
    smem, whole = pl.BlockSpec(memory_space=pltpu.SMEM), pl.BlockSpec(memory_space=pltpu.VMEM)

    both = jnp.concatenate([text_emb, exchange(text_emb, "img", n_img, 1)])
    image_blocks = [image_emb] + [None] * (n_txt - 1)
    for k in (2, 3):
        image_blocks[k] = exchange(image_emb, "txt", n_txt, k)
    beside = chip_exchange(both, n_img, (1, 2))
    diagonal = chip_exchange(text_emb, n_img, (3, 3))
    image_blocks[1] = exchange(after(image_emb, both), "txt", n_txt, 1)
    sent = jnp.concatenate([beside, diagonal])
    got = exchange(sent, "img", n_img, 1)
    numbers = jnp.pad(pairs.astype(jnp.float32)[None], ((0, 7), (0, width - count)))
    bundle = jnp.concatenate([image_blocks[k] for k in IMAGE_ORDER] + [numbers])

    own, loss_tile, d_near, *messages = pl.pallas_call(
        functools.partial(image_kernel, n_img, n_txt, rows, cols),
        out_shape=[vmem((rows, width)), vmem((8, LANES)), vmem((chips * cols, count))]
        + [vmem((tiles + 1, 8, LANES))] * (n_txt - 1),
        in_specs=[smem] * 2 + [whole] * 4,
        out_specs=[whole] * (2 + n_txt),
        name="image_terms",
    )(log_scale, bias, *in_vmem(bundle, both, sent, got))
    messages = [exchange(messages[p - 1], "txt", n_txt, IMAGE_ORDER[p]) for p in (3, 1, 2)]

    pair = exchange(bundle, "img", n_img, 1)
    blocks = pl.pallas_call(
        functools.partial(text_kernel, n_img, n_txt, rows, cols),
        out_shape=[vmem((cols, width))] * chips,
        in_specs=[smem] * 2 + [whole] * 6,
        out_specs=[whole] * chips,
        name="text_terms",
    )(log_scale, bias, *in_vmem(bundle, pair, both, sent, got, d_near))
    blocks = list(blocks)
    for k, distances in ((3, (3, 3)), (1, (1, 2)), (2, (2, 1))):
        blocks[k] = chip_exchange(blocks[k], n_img, distances)

    image_loss, image_grad, text_grad = pl.pallas_call(
        functools.partial(sum_kernel, n_txt, chips),
        out_shape=[
            jax.ShapeDtypeStruct(shape, jnp.float32)
            for shape in ((1, LANES), image_emb.shape, text_emb.shape)
        ],
        in_specs=[whole] * (1 + n_txt + chips),
        out_specs=[whole] * 3,
        name="sums",
    )(*in_vmem(own, loss_tile, *messages, blocks[3], *blocks[:3]))
    return (image_loss.reshape(count), image_grad, text_grad)


def per_device_large(image_emb, text_emb, pairs, log_scale, bias):
    images = lax.all_gather(image_emb, "txt", axis=0, tiled=True)
    texts = lax.all_gather(text_emb, "img", axis=0, tiled=True)
    scale = jnp.exp(log_scale[0])
    shift = bias[0]
    text_count = texts.shape[0]
    dots = lax.dot_general(
        images,
        texts,
        (((1,), (1,)), ((), ())),
        precision=lax.Precision.HIGHEST,
        preferred_element_type=jnp.float32,
    )
    logits = scale * dots + shift
    columns = lax.axis_index("txt") * text_count + jnp.arange(text_count, dtype=jnp.int32)
    sign = jnp.where(pairs[:, None] == columns[None, :], 1.0, -1.0).astype(jnp.float32)
    loss_part = jnp.sum(jax.nn.softplus(-sign * logits), axis=1)
    image_loss = lax.psum(loss_part, "txt")
    dlogits = -sign * jax.nn.sigmoid(-sign * logits)
    image_term = scale * jnp.dot(
        dlogits, texts, precision=lax.Precision.HIGHEST, preferred_element_type=jnp.float32
    )
    image_grad = lax.psum_scatter(image_term, "txt", scatter_dimension=0, tiled=True)
    text_term = scale * lax.dot_general(
        dlogits,
        images,
        (((0,), (0,)), ((), ())),
        precision=lax.Precision.HIGHEST,
        preferred_element_type=jnp.float32,
    )
    text_grad = lax.psum_scatter(text_term, "img", scatter_dimension=0, tiled=True)
    return (image_loss, image_grad, text_grad)


def solution(mesh):
    sizes = (mesh.shape["img"], mesh.shape["txt"])

    def body(image_emb, *others):
        rows = image_emb.shape[0]
        if sizes == (8, 4) and rows * sizes[1] == LANES:
            return per_device(sizes, image_emb, *others)
        return per_device_large(image_emb, *others)

    return jax.shard_map(
        body,
        mesh=mesh,
        in_specs=(P(("img", "txt"), None), P(("txt", "img"), None), P("img"), P(), P()),
        out_specs=(P("img"), P(("img", "txt"), None), P(("txt", "img"), None)),
        check_vma=False,
    )
```

```python
import functools

import jax
import jax.numpy as jnp
from jax import lax
from jax.experimental import pallas as pl
from jax.experimental.pallas import tpu as pltpu
from jax.sharding import PartitionSpec as P

LANES = 128

IMAGE_ORDER = (0, 2, 3, 1)


def exchange(x, axis, n, k):
    return lax.ppermute(x, axis, [(i, i ^ k) for i in range(n)])


def after(x, other):
    return lax.optimization_barrier((x, other))[0]


def chip_exchange(x, n_img, distances):
    return lax.ppermute(x, "img", [(i, i ^ (2 * distances[i % 2])) for i in range(n_img)])


def halves(x):
    high = x.astype(jnp.bfloat16)
    return high, (x - high.astype(jnp.float32)).astype(jnp.bfloat16)


def dot(a, b, contract):
    def part(x, y):
        dims = ((contract[:1], contract[1:]), ((), ()))
        return lax.dot_general(x, y, dims, preferred_element_type=jnp.float32)

    return part(a[0], b[0]) + (part(a[0], b[1]) + part(a[1], b[0]))


def untwist(row, block, me):
    lane = lax.broadcasted_iota(jnp.int32, row.shape, 1)
    step = block
    while step < LANES:
        up, down = pltpu.roll(row, LANES - step, 1), pltpu.roll(row, step, 1)
        flipped = jnp.where((lane // step) % 2 == 0, up, down)
        row = jnp.where((me // (step // block)) % 2 == 1, flipped, row)
        step *= 2
    return row


def shuffle(row, block, sources):
    place = lax.broadcasted_iota(jnp.int32, row.shape, 1) // block
    result = row
    for step in range(1, len(sources)):
        moved = pltpu.roll(row, LANES - step * block, 1)
        for p, source in enumerate(sources):
            if (source - p) % len(sources) == step:
                result = jnp.where(place == p, moved, result)
    return result


def text_ids(shape, n_img, cols, far):
    me_img, me_txt = lax.axis_index("img"), lax.axis_index("txt")
    place = lax.broadcasted_iota(jnp.int32, shape, 0)
    half = n_img // 2 * cols
    me_core = me_img % 2
    core = me_core
    if far:
        core = core ^ (place // half)
        place = place % half
    turn = place // cols
    distance = jnp.where(turn == 1, 1 + me_core, jnp.where(turn == 2, 2 - me_core, turn))
    chip = (me_img // 2) ^ distance
    return (me_txt * n_img + 2 * chip + core) * cols + place % cols


def own_core_texts(cols, both, sent, got):
    return [both[:cols], sent[:cols], got[cols:2 * cols], sent[2 * cols:]]


def other_core_texts(cols, both, sent, got):
    return [both[cols:], sent[cols:2 * cols], got[:cols], got[2 * cols:]]


def derivative(texts, images, ids, matched, log_scale, bias):
    scale = jnp.exp(jnp.full((1, LANES), log_scale[0], jnp.float32))
    logits = scale * dot(texts, images, (1, 1)) + bias[0]
    match = ids == matched
    v = jnp.where(match, -logits, logits)
    e = jnp.exp(-jnp.abs(v))
    loss = jnp.maximum(v, 0.0) + jnp.log1p(e)
    s = scale * jnp.where(v >= 0, 1.0, e) / (1.0 + e)
    return loss, jnp.where(match, -s, s)


def matched_texts(bundle, rows, count):
    matched = untwist(bundle[count:count + 1, :LANES], rows, lax.axis_index("txt"))
    return shuffle(matched, rows, IMAGE_ORDER).astype(jnp.int32)


def image_kernel(
    n_img, n_txt, rows, cols, log_scale, bias, bundle, both, sent, got,
    own, loss_ref, d_near, *messages
):
    count = n_txt * rows
    matched = matched_texts(bundle, rows, count)
    images = halves(bundle[:count])
    near = own_core_texts(cols, both, sent, got)
    texts = halves(jnp.concatenate(near + other_core_texts(cols, both, sent, got)))
    ids = text_ids((texts[0].shape[0], count), n_img, cols, True)
    loss, d = derivative(texts, images, ids, matched, log_scale, bias)
    d_near[...] = d[:len(near) * cols]
    term = dot(halves(d), texts, (0, 0))
    own[...] = term[:rows]
    back = [IMAGE_ORDER.index(k) for k in range(n_txt)]
    loss_row = shuffle(jnp.sum(loss, axis=0, keepdims=True), rows, back)
    loss_row = untwist(loss_row, rows, lax.axis_index("txt"))
    loss_tile = jnp.broadcast_to(loss_row, (8, LANES))
    loss_ref[...] = loss_tile
    across = term.shape[1] // LANES
    for p, ref in enumerate(messages, 1):
        for r in range(rows // 8):
            for c in range(across):
                ref[r * across + c] = term[
                    p * rows + r * 8:p * rows + r * 8 + 8, c * LANES:(c + 1) * LANES
                ]
        ref[rows // 8 * across] = loss_tile


def text_kernel(n_img, n_txt, rows, cols, *refs):
    log_scale, bias, bundle, pair, both, sent, got, d_ref = refs[:8]
    block_refs = refs[8:]
    count = n_txt * rows
    matched = matched_texts(pair, rows, count)
    others = halves(pair[:count])
    texts = halves(jnp.concatenate(own_core_texts(cols, both, sent, got)))
    ids = text_ids((texts[0].shape[0], count), n_img, cols, False)
    _, d = derivative(texts, others, ids, matched, log_scale, bias)
    term = dot(halves(d_ref[...]), halves(bundle[:count]), (1, 0)) + dot(halves(d), others, (1, 0))
    for k, ref in enumerate(block_refs):
        ref[...] = term[k * cols:(k + 1) * cols]


def sum_kernel(n_txt, n_chips, own_ref, loss_ref, *refs):
    messages, blocks = refs[:n_txt - 1], refs[n_txt - 1:n_txt - 1 + n_chips]
    image_loss, image_grad, text_grad = refs[n_txt - 1 + n_chips:]
    text_grad[...] = sum(b[...] for b in blocks)
    rows, width = own_ref.shape
    across = width // LANES
    for r in range(rows // 8):
        for c in range(across):
            at = (slice(r * 8, r * 8 + 8), slice(c * LANES, (c + 1) * LANES))
            image_grad[at] = own_ref[at] + sum(m[r * across + c] for m in messages)
    image_loss[...] = (loss_ref[...] + sum(m[rows // 8 * across] for m in messages))[:1]


def in_vmem(*arrays):
    return [pltpu.with_memory_space_constraint(x, pltpu.VMEM) for x in arrays]


def vmem(shape):
    return pltpu.VMEM(shape, jnp.float32)


def per_device(sizes, image_emb, text_emb, pairs, log_scale, bias):
    n_img, n_txt = sizes
    chips = n_img // 2
    rows, cols, width = image_emb.shape[0], text_emb.shape[0], image_emb.shape[1]
    count = n_txt * rows
    tiles = rows * width // (8 * LANES)
    smem, whole = pl.BlockSpec(memory_space=pltpu.SMEM), pl.BlockSpec(memory_space=pltpu.VMEM)

    both = jnp.concatenate([text_emb, exchange(text_emb, "img", n_img, 1)])
    image_blocks = [image_emb] + [None] * (n_txt - 1)
    for k in (2, 3):
        image_blocks[k] = exchange(image_emb, "txt", n_txt, k)
    beside = chip_exchange(both, n_img, (1, 2))
    diagonal = chip_exchange(text_emb, n_img, (3, 3))
    image_blocks[1] = exchange(after(image_emb, both), "txt", n_txt, 1)
    sent = jnp.concatenate([beside, diagonal])
    got = exchange(sent, "img", n_img, 1)
    numbers = jnp.pad(pairs.astype(jnp.float32)[None], ((0, 7), (0, width - count)))
    bundle = jnp.concatenate([image_blocks[k] for k in IMAGE_ORDER] + [numbers])

    own, loss_tile, d_near, *messages = pl.pallas_call(
        functools.partial(image_kernel, n_img, n_txt, rows, cols),
        out_shape=[vmem((rows, width)), vmem((8, LANES)), vmem((chips * cols, count))]
        + [vmem((tiles + 1, 8, LANES))] * (n_txt - 1),
        in_specs=[smem] * 2 + [whole] * 4,
        out_specs=[whole] * (2 + n_txt),
        name="image_terms",
    )(log_scale, bias, *in_vmem(bundle, both, sent, got))
    messages = [exchange(messages[p - 1], "txt", n_txt, IMAGE_ORDER[p]) for p in (3, 2, 1)]

    pair = exchange(after(bundle, got), "img", n_img, 1)
    blocks = pl.pallas_call(
        functools.partial(text_kernel, n_img, n_txt, rows, cols),
        out_shape=[vmem((cols, width))] * chips,
        in_specs=[smem] * 2 + [whole] * 6,
        out_specs=[whole] * chips,
        name="text_terms",
    )(log_scale, bias, *in_vmem(bundle, pair, both, sent, got, d_near))
    blocks = list(blocks)
    for k, distances in ((3, (3, 3)), (1, (1, 2)), (2, (2, 1))):
        blocks[k] = chip_exchange(blocks[k], n_img, distances)

    image_loss, image_grad, text_grad = pl.pallas_call(
        functools.partial(sum_kernel, n_txt, chips),
        out_shape=[
            jax.ShapeDtypeStruct(shape, jnp.float32)
            for shape in ((1, LANES), image_emb.shape, text_emb.shape)
        ],
        in_specs=[whole] * (1 + n_txt + chips),
        out_specs=[whole] * 3,
        name="sums",
    )(*in_vmem(own, loss_tile, *messages, blocks[3], *blocks[:3]))
    return (image_loss.reshape(count), image_grad, text_grad)


def per_device_large(image_emb, text_emb, pairs, log_scale, bias):
    images = lax.all_gather(image_emb, "txt", axis=0, tiled=True)
    texts = lax.all_gather(text_emb, "img", axis=0, tiled=True)
    scale = jnp.exp(log_scale[0])
    shift = bias[0]
    text_count = texts.shape[0]
    dots = lax.dot_general(
        images,
        texts,
        (((1,), (1,)), ((), ())),
        precision=lax.Precision.HIGHEST,
        preferred_element_type=jnp.float32,
    )
    logits = scale * dots + shift
    columns = lax.axis_index("txt") * text_count + jnp.arange(text_count, dtype=jnp.int32)
    sign = jnp.where(pairs[:, None] == columns[None, :], 1.0, -1.0).astype(jnp.float32)
    loss_part = jnp.sum(jax.nn.softplus(-sign * logits), axis=1)
    image_loss = lax.psum(loss_part, "txt")
    dlogits = -sign * jax.nn.sigmoid(-sign * logits)
    image_term = scale * jnp.dot(
        dlogits, texts, precision=lax.Precision.HIGHEST, preferred_element_type=jnp.float32
    )
    image_grad = lax.psum_scatter(image_term, "txt", scatter_dimension=0, tiled=True)
    text_term = scale * lax.dot_general(
        dlogits,
        images,
        (((0,), (0,)), ((), ())),
        precision=lax.Precision.HIGHEST,
        preferred_element_type=jnp.float32,
    )
    text_grad = lax.psum_scatter(text_term, "img", scatter_dimension=0, tiled=True)
    return (image_loss, image_grad, text_grad)


def solution(mesh):
    sizes = (mesh.shape["img"], mesh.shape["txt"])

    def body(image_emb, *others):
        rows = image_emb.shape[0]
        if sizes == (8, 4) and rows * sizes[1] == LANES:
            return per_device(sizes, image_emb, *others)
        return per_device_large(image_emb, *others)

    return jax.shard_map(
        body,
        mesh=mesh,
        in_specs=(P(("img", "txt"), None), P(("txt", "img"), None), P("img"), P(), P()),
        out_specs=(P("img"), P(("img", "txt"), None), P(("txt", "img"), None)),
        check_vma=False,
    )
```

```python
import functools

import jax
import jax.numpy as jnp
from jax import lax
from jax.experimental import pallas as pl
from jax.experimental.pallas import tpu as pltpu
from jax.sharding import PartitionSpec as P

LANES = 128

IMAGE_ORDER = (0, 2, 3, 1)


def exchange(x, axis, n, k):
    return lax.ppermute(x, axis, [(i, i ^ k) for i in range(n)])


def after(x, other):
    return lax.optimization_barrier((x, other))[0]


def chip_exchange(x, n_img, distances):
    return lax.ppermute(x, "img", [(i, i ^ (2 * distances[i % 2])) for i in range(n_img)])


def halves(x):
    high = x.astype(jnp.bfloat16)
    return high, (x - high.astype(jnp.float32)).astype(jnp.bfloat16)


def dot(a, b, contract):
    def part(x, y):
        dims = ((contract[:1], contract[1:]), ((), ()))
        return lax.dot_general(x, y, dims, preferred_element_type=jnp.float32)

    return part(a[0], b[0]) + (part(a[0], b[1]) + part(a[1], b[0]))


def untwist(row, block, me):
    lane = lax.broadcasted_iota(jnp.int32, row.shape, 1)
    step = block
    while step < LANES:
        up, down = pltpu.roll(row, LANES - step, 1), pltpu.roll(row, step, 1)
        flipped = jnp.where((lane // step) % 2 == 0, up, down)
        row = jnp.where((me // (step // block)) % 2 == 1, flipped, row)
        step *= 2
    return row


def shuffle(row, block, sources):
    place = lax.broadcasted_iota(jnp.int32, row.shape, 1) // block
    result = row
    for step in range(1, len(sources)):
        moved = pltpu.roll(row, LANES - step * block, 1)
        for p, source in enumerate(sources):
            if (source - p) % len(sources) == step:
                result = jnp.where(place == p, moved, result)
    return result


def text_ids(shape, n_img, cols, far):
    me_img, me_txt = lax.axis_index("img"), lax.axis_index("txt")
    place = lax.broadcasted_iota(jnp.int32, shape, 0)
    half = n_img // 2 * cols
    me_core = me_img % 2
    core = me_core
    if far:
        core = core ^ (place // half)
        place = place % half
    turn = place // cols
    distance = jnp.where(turn == 1, 1 + me_core, jnp.where(turn == 2, 2 - me_core, turn))
    chip = (me_img // 2) ^ distance
    return (me_txt * n_img + 2 * chip + core) * cols + place % cols


def own_core_texts(cols, both, sent, got):
    return [both[:cols], sent[:cols], got[cols:2 * cols], sent[2 * cols:]]


def other_core_texts(cols, both, sent, got):
    return [both[cols:], sent[cols:2 * cols], got[:cols], got[2 * cols:]]


def derivative(texts, images, ids, matched, log_scale, bias):
    scale = jnp.exp(jnp.full((1, LANES), log_scale[0], jnp.float32))
    logits = scale * dot(texts, images, (1, 1)) + bias[0]
    match = ids == matched
    v = jnp.where(match, -logits, logits)
    e = jnp.exp(-jnp.abs(v))
    loss = jnp.maximum(v, 0.0) + jnp.log1p(e)
    s = scale * jnp.where(v >= 0, 1.0, e) / (1.0 + e)
    return loss, jnp.where(match, -s, s)


def matched_texts(bundle, rows, count):
    matched = untwist(bundle[count:count + 1, :LANES], rows, lax.axis_index("txt"))
    return shuffle(matched, rows, IMAGE_ORDER).astype(jnp.int32)


def image_kernel(
    n_img, n_txt, rows, cols, log_scale, bias, bundle, both, sent, got,
    own, loss_ref, d_near, *messages
):
    count = n_txt * rows
    matched = matched_texts(bundle, rows, count)
    images = halves(bundle[:count])
    near = own_core_texts(cols, both, sent, got)
    texts = halves(jnp.concatenate(near + other_core_texts(cols, both, sent, got)))
    ids = text_ids((texts[0].shape[0], count), n_img, cols, True)
    loss, d = derivative(texts, images, ids, matched, log_scale, bias)
    d_near[...] = d[:len(near) * cols]
    term = dot(halves(d), texts, (0, 0))
    own[...] = term[:rows]
    back = [IMAGE_ORDER.index(k) for k in range(n_txt)]
    loss_row = shuffle(jnp.sum(loss, axis=0, keepdims=True), rows, back)
    loss_row = untwist(loss_row, rows, lax.axis_index("txt"))
    loss_tile = jnp.broadcast_to(loss_row, (8, LANES))
    loss_ref[...] = loss_tile
    across = term.shape[1] // LANES
    for p, ref in enumerate(messages, 1):
        for r in range(rows // 8):
            for c in range(across):
                ref[r * across + c] = term[
                    p * rows + r * 8:p * rows + r * 8 + 8, c * LANES:(c + 1) * LANES
                ]
        ref[rows // 8 * across] = loss_tile


def text_kernel(n_img, n_txt, rows, cols, *refs):
    log_scale, bias, bundle, pair, both, sent, got, d_ref = refs[:8]
    block_refs = refs[8:]
    count = n_txt * rows
    matched = matched_texts(pair, rows, count)
    others = halves(pair[:count])
    texts = halves(jnp.concatenate(own_core_texts(cols, both, sent, got)))
    ids = text_ids((texts[0].shape[0], count), n_img, cols, False)
    _, d = derivative(texts, others, ids, matched, log_scale, bias)
    weights = jnp.concatenate([d_ref[...], d], axis=1)
    images = [jnp.concatenate(parts) for parts in zip(halves(bundle[:count]), others)]
    term = dot(halves(weights), images, (1, 0))
    for k, ref in enumerate(block_refs):
        ref[...] = term[k * cols:(k + 1) * cols]


def sum_kernel(n_txt, n_chips, own_ref, loss_ref, *refs):
    messages, blocks = refs[:n_txt - 1], refs[n_txt - 1:n_txt - 1 + n_chips]
    image_loss, image_grad, text_grad = refs[n_txt - 1 + n_chips:]
    text_grad[...] = sum(b[...] for b in blocks)
    rows, width = own_ref.shape
    across = width // LANES
    for r in range(rows // 8):
        for c in range(across):
            at = (slice(r * 8, r * 8 + 8), slice(c * LANES, (c + 1) * LANES))
            image_grad[at] = own_ref[at] + sum(m[r * across + c] for m in messages)
    image_loss[...] = (loss_ref[...] + sum(m[rows // 8 * across] for m in messages))[:1]


def in_vmem(*arrays):
    return [pltpu.with_memory_space_constraint(x, pltpu.VMEM) for x in arrays]


def vmem(shape):
    return pltpu.VMEM(shape, jnp.float32)


def per_device(sizes, image_emb, text_emb, pairs, log_scale, bias):
    n_img, n_txt = sizes
    chips = n_img // 2
    rows, cols, width = image_emb.shape[0], text_emb.shape[0], image_emb.shape[1]
    count = n_txt * rows
    tiles = rows * width // (8 * LANES)
    smem, whole = pl.BlockSpec(memory_space=pltpu.SMEM), pl.BlockSpec(memory_space=pltpu.VMEM)

    both = jnp.concatenate([text_emb, exchange(text_emb, "img", n_img, 1)])
    image_blocks = [image_emb] + [None] * (n_txt - 1)
    for k in (2, 3):
        image_blocks[k] = exchange(image_emb, "txt", n_txt, k)
    beside = chip_exchange(both, n_img, (1, 2))
    diagonal = chip_exchange(text_emb, n_img, (3, 3))
    image_blocks[1] = exchange(after(image_emb, both), "txt", n_txt, 1)
    sent = jnp.concatenate([beside, diagonal])
    got = exchange(sent, "img", n_img, 1)
    numbers = jnp.pad(pairs.astype(jnp.float32)[None], ((0, 7), (0, width - count)))
    bundle = jnp.concatenate([image_blocks[k] for k in IMAGE_ORDER] + [numbers])

    own, loss_tile, d_near, *messages = pl.pallas_call(
        functools.partial(image_kernel, n_img, n_txt, rows, cols),
        out_shape=[vmem((rows, width)), vmem((8, LANES)), vmem((chips * cols, count))]
        + [vmem((tiles + 1, 8, LANES))] * (n_txt - 1),
        in_specs=[smem] * 2 + [whole] * 4,
        out_specs=[whole] * (2 + n_txt),
        name="image_terms",
    )(log_scale, bias, *in_vmem(bundle, both, sent, got))
    messages = [exchange(messages[p - 1], "txt", n_txt, IMAGE_ORDER[p]) for p in (3, 2, 1)]

    pair = exchange(bundle, "img", n_img, 1)
    blocks = pl.pallas_call(
        functools.partial(text_kernel, n_img, n_txt, rows, cols),
        out_shape=[vmem((cols, width))] * chips,
        in_specs=[smem] * 2 + [whole] * 6,
        out_specs=[whole] * chips,
        name="text_terms",
    )(log_scale, bias, *in_vmem(bundle, pair, both, sent, got, d_near))
    blocks = list(blocks)
    for k, distances in ((3, (3, 3)), (1, (1, 2)), (2, (2, 1))):
        blocks[k] = chip_exchange(blocks[k], n_img, distances)

    image_loss, image_grad, text_grad = pl.pallas_call(
        functools.partial(sum_kernel, n_txt, chips),
        out_shape=[
            jax.ShapeDtypeStruct(shape, jnp.float32)
            for shape in ((1, LANES), image_emb.shape, text_emb.shape)
        ],
        in_specs=[whole] * (1 + n_txt + chips),
        out_specs=[whole] * 3,
        name="sums",
    )(*in_vmem(own, loss_tile, *messages, blocks[3], *blocks[:3]))
    return (image_loss.reshape(count), image_grad, text_grad)


def per_device_large(image_emb, text_emb, pairs, log_scale, bias):
    images = lax.all_gather(image_emb, "txt", axis=0, tiled=True)
    texts = lax.all_gather(text_emb, "img", axis=0, tiled=True)
    scale = jnp.exp(log_scale[0])
    shift = bias[0]
    text_count = texts.shape[0]
    dots = lax.dot_general(
        images,
        texts,
        (((1,), (1,)), ((), ())),
        precision=lax.Precision.HIGHEST,
        preferred_element_type=jnp.float32,
    )
    logits = scale * dots + shift
    columns = lax.axis_index("txt") * text_count + jnp.arange(text_count, dtype=jnp.int32)
    sign = jnp.where(pairs[:, None] == columns[None, :], 1.0, -1.0).astype(jnp.float32)
    loss_part = jnp.sum(jax.nn.softplus(-sign * logits), axis=1)
    image_loss = lax.psum(loss_part, "txt")
    dlogits = -sign * jax.nn.sigmoid(-sign * logits)
    image_term = scale * jnp.dot(
        dlogits, texts, precision=lax.Precision.HIGHEST, preferred_element_type=jnp.float32
    )
    image_grad = lax.psum_scatter(image_term, "txt", scatter_dimension=0, tiled=True)
    text_term = scale * lax.dot_general(
        dlogits,
        images,
        (((0,), (0,)), ((), ())),
        precision=lax.Precision.HIGHEST,
        preferred_element_type=jnp.float32,
    )
    text_grad = lax.psum_scatter(text_term, "img", scatter_dimension=0, tiled=True)
    return (image_loss, image_grad, text_grad)


def solution(mesh):
    sizes = (mesh.shape["img"], mesh.shape["txt"])

    def body(image_emb, *others):
        rows = image_emb.shape[0]
        if sizes == (8, 4) and rows * sizes[1] == LANES:
            return per_device(sizes, image_emb, *others)
        return per_device_large(image_emb, *others)

    return jax.shard_map(
        body,
        mesh=mesh,
        in_specs=(P(("img", "txt"), None), P(("txt", "img"), None), P("img"), P(), P()),
        out_specs=(P("img"), P(("img", "txt"), None), P(("txt", "img"), None)),
        check_vma=False,
    )
```
